256 devices in a mesh: gx: 64 (over z_lo, x, y), gy: 4 (over z_hi, core).
Axes of the slice: x: 4, y: 4, z: 8 (z_hi: 2, z_lo: 4; z = z_hi * 4 + z_lo), core: 2. Of those that a mesh axis runs over, the one named last changes fastest.
Arguments:
- positions: float32 [3, 16384], P(None, ('gx', 'gy')), may hold values from 0 to 22.4, as said below
- features: bfloat16 [64, 16384], P(None, ('gx', 'gy')), may hold values from -6 to 6
- send_list: int32 [8192], P(('gx', 'gy')), may hold values from 0 to 63, as said below
- edge_src: int32 [262144], P(('gx', 'gy')), may hold values from 0 to 319, as said below
- edge_dst: int32 [262144], P(('gx', 'gy')), may hold values from 0 to 63, as said below
- edge_count: int32 [256], P(('gx', 'gy')), may hold values from 128 to 1024, as said below
- w_embed: float32 [136, 64], replicated, may hold values from -0.5 to 0.5
- w_env: float32 [2, 64, 192], replicated, may hold values from -0.75 to 0.75
- w_update: float32 [2, 256, 64], replicated, may hold values from -0.375 to 0.375
- w_out: float32 [64], replicated, may hold values from -0.75 to 0.75
Outputs:
- forces: float32 [3, 16384], P(None, ('gx', 'gy'))
- energy: float32 [], replicated
The draws below stay inside these ranges and needn't reach their ends.
Inputs may be any that keep to these rules, and one draw needn't show every extreme that they name: `positions`: x and y lie within the device's cell of width 6; z lies within the slab. `send_list`: each device's 32 entries are distinct owned slots in increasing order. `edge_src`: indices into the device's table of 64 own atoms and 8 ghost blocks. `edge_dst`: owned slots of the device. `edge_count`: each device's count is a multiple of 128; some device has all 1024 slots live in every draw.
All inputs are finite; a program needn't handle non-finite values.
Results may differ from the reference program's by a relative error of at most 0.00035.
Values sent between devices are 32-bit elements; how exact they have to be, the bound alone decides.
A program may use at most 64 MiB of HBM per device.

```python
import math
import jax
import jax.numpy as jnp
from jax import lax

C = 64
NB = 8
LAYERS = 2
NEIGH = 16
ATOM_DEV = 64
GHOST = 32
EDGE_DEV = 1024
ATOMS = 16384
EDGES = 262144
N_GX = 64
N_GY = 4


def edge_pairs(key):
    first, second, third, fourth = jax.random.split(key, 4)
    dst = jax.random.randint(first, (EDGES,), 0, ATOM_DEV)
    kind = jax.random.randint(second, (EDGES,), 0, 9)
    own = jnp.clip(dst + jax.random.randint(third, (EDGES,), -12, 13), 0, ATOM_DEV - 1)
    place = jnp.clip(dst // 2 + jax.random.randint(fourth, (EDGES,), -6, 7), 0, GHOST - 1)
    remote = ATOM_DEV + (kind - 1) * GHOST + place
    src = jnp.where(kind == 0, own, remote)
    slot = jnp.arange(EDGES) % EDGE_DEV
    src = jnp.where(slot == 0, ATOM_DEV + 8 * GHOST - 1, src)
    dst = jnp.where(slot == 0, ATOM_DEV - 1, dst)
    src = jnp.where(slot == 1, 0, src)
    dst = jnp.where(slot == 1, 0, dst)
    return (src.astype(jnp.int32), dst.astype(jnp.int32))


def draw_edge_src(key, part):
    pairs = edge_pairs(key)
    return pairs[0]


def draw_edge_dst(key, part):
    pairs = edge_pairs(key)
    return pairs[1]


def draw_send_list(key, part):
    key = jax.random.fold_in(key, 5)
    devices = EDGES // EDGE_DEV
    total = GHOST * devices
    place = jnp.arange(total) % GHOST
    slots = 2 * place + jax.random.randint(key, (total,), 0, 2)
    slots = jnp.where(place == 0, 0, slots)
    slots = jnp.where(place == GHOST - 1, ATOM_DEV - 1, slots)
    return slots.astype(jnp.int32)


def draw_positions(key, part):
    key = jax.random.fold_in(key, 3)
    first, second = jax.random.split(key)
    devices = EDGES // EDGE_DEV
    total = ATOM_DEV * devices
    plane = jax.random.uniform(first, (2, total), jnp.float32) * 6.0
    slot = (jnp.arange(total) % ATOM_DEV).astype(jnp.float32)
    height = (slot + jax.random.uniform(second, (total,), jnp.float32)) * 0.35
    return jnp.concatenate([plane, height[None, :]], axis=0).astype(jnp.float32)


def draw_edge_count(key, part):
    key = jax.random.fold_in(key, 7)
    first, second = jax.random.split(key)
    devices = EDGES // EDGE_DEV
    blocks = EDGE_DEV // 128
    counts = jax.random.randint(first, (devices,), 1, blocks + 1) * 128
    chosen = jax.random.randint(second, (), 0, devices)
    return jnp.where(jnp.arange(devices) == chosen, EDGE_DEV, counts).astype(jnp.int32)


def level_of(own_key, extent, cuts, low, largest):
    gain, own = 1.0, jax.random.fold_in(own_key, 6)
    for position, blocks in cuts:
        heights = jnp.exp(jax.random.uniform(jax.random.fold_in(own, position), (blocks,), jnp.float32, low / len(cuts), largest / len(cuts)))
        gain = gain * jnp.repeat(heights, extent[position] // blocks).reshape([-1 if axis == position else 1 for axis in range(len(extent))])
    return gain


def normal_values(key, dims, spread, reach, pieces=(), kind=jnp.bfloat16):
    result = spread * jax.random.normal(key, dims, jnp.float32)
    if pieces:
        result = result * level_of(key, dims, pieces, -0.22, 0.18)
    return jnp.clip(result, -reach, reach).astype(kind)


def setup_inputs(seed: int = 0) -> dict:
    streams_of = jax.random.split(jax.random.key(seed), 11)
    return {
        "positions": draw_positions(jax.random.fold_in(streams_of[10], 71), 0),
        "features": normal_values(streams_of[1], (C, ATOMS), 1.0, 6.0, ((1, 256),)),
        "send_list": draw_send_list(jax.random.fold_in(streams_of[10], 71), 0),
        "edge_src": draw_edge_src(jax.random.fold_in(streams_of[10], 71), 0),
        "edge_dst": draw_edge_dst(jax.random.fold_in(streams_of[10], 71), 0),
        "edge_count": draw_edge_count(jax.random.fold_in(streams_of[10], 71), 0),
        "w_embed": normal_values(streams_of[6], (2 * C + NB, C), (2 * C + NB) ** -0.5, 0.5, (), jnp.float32),
        "w_env": normal_values(streams_of[7], (LAYERS, C, 3 * C), C ** -0.5, 0.75, (), jnp.float32),
        "w_update": normal_values(streams_of[8], (LAYERS, 4 * C, C), (4 * C) ** -0.5, 0.375, (), jnp.float32),
        "w_out": normal_values(streams_of[9], (C,), C ** -0.5, 0.75, (), jnp.float32),
    }


neighbour_offsets = ((-1, -1), (-1, 0), (-1, 1), (0, -1), (0, 1), (1, -1), (1, 0), (1, 1))
cell_width = 6.0
cutoff = 5.0
degree_of = (0, 1, 1, 1, 2, 2, 2, 2, 2)

def edge_energy(table_pos, table_feat, src, dst, live, w_embed, w_env, w_update, w_out):
    highest = lax.Precision.HIGHEST
    diff = table_pos[:, src] - table_pos[:, dst]
    dist = jnp.sqrt(lax.optimization_barrier(jnp.sum(diff * diff, axis=0)) + 1.0)
    unit = diff / dist
    ux, uy, uz = (unit[0], unit[1], unit[2])
    root = math.sqrt(3.0)
    harm = jnp.stack([jnp.ones_like(ux), ux, uy, uz, root * ux * uy, root * uy * uz, 0.5 * (3.0 * uz * uz - 1.0), root * ux * uz, 0.5 * root * (ux * ux - uy * uy)])
    ratio = dist / cutoff
    envelope = jnp.maximum(1.0 - ratio * ratio, 0.0) ** 2
    cut = live * envelope
    orders = jnp.arange(1, NB + 1, dtype=jnp.float32)[:, None]
    radial = jnp.sin(orders * (math.pi / cutoff) * dist[None, :]) * (envelope / dist)[None, :]
    stacked = jnp.concatenate([table_feat[:, src], table_feat[:, dst], radial], axis=0)
    feat = jax.nn.silu(jnp.dot(w_embed.T, stacked, precision=highest)) * cut
    edges = feat.shape[1]
    pick = jnp.array(degree_of, dtype=jnp.int32)
    for layer in range(LAYERS):
        weights = jnp.dot(w_env[layer].T, feat, precision=highest).reshape(3, C, edges)
        terms = weights[pick] * harm[:, None, :]
        atom_env = jax.ops.segment_sum(terms.reshape(9 * C, edges).T, dst, num_segments=ATOM_DEV)
        back = atom_env[dst].T.reshape(9, C, edges) * harm[:, None, :]
        invariants = jnp.concatenate([back[0], lax.optimization_barrier(jnp.sum(back[1:4], axis=0)), lax.optimization_barrier(jnp.sum(back[4:9], axis=0))], axis=0)
        invariants = invariants * NEIGH ** (-0.5)
        joined = jnp.concatenate([feat, invariants], axis=0)
        feat = feat + jax.nn.silu(jnp.dot(w_update[layer].T, joined, precision=highest)) * cut
    return jnp.sum(jnp.dot(w_out, feat, precision=highest) * live)

def device_energy(index, positions, features, send_list, edge_src, edge_dst, edge_count, w_embed, w_env, w_update, w_out):
    column = index // N_GY
    row = index % N_GY
    start = (index * ATOM_DEV).astype(jnp.int32)
    pieces_pos = [lax.dynamic_slice_in_dim(positions, start, ATOM_DEV, 1)]
    pieces_feat = [lax.dynamic_slice_in_dim(features, start, ATOM_DEV, 1).astype(jnp.float32)]
    flags = [jnp.ones((ATOM_DEV,), jnp.float32)]
    for step_x, step_y in neighbour_offsets:
        src_col = (column + step_x) % N_GX
        src_row = row + step_y
        valid = ((src_row >= 0) & (src_row < N_GY)).astype(jnp.float32)
        peer = (src_col * N_GY + jnp.clip(src_row, 0, N_GY - 1)).astype(jnp.int32)
        rows = lax.dynamic_slice_in_dim(send_list, (peer * GHOST).astype(jnp.int32), GHOST)
        global_rows = (peer * ATOM_DEV + rows).astype(jnp.int32)
        offset = jnp.array([step_x * cell_width, step_y * cell_width, 0.0], jnp.float32)[:, None]
        pieces_pos.append((positions[:, global_rows] + offset) * valid)
        pieces_feat.append(features[:, global_rows].astype(jnp.float32) * valid)
        flags.append(jnp.zeros((GHOST,), jnp.float32) + valid)
    table_pos = jnp.concatenate(pieces_pos, axis=1)
    table_feat = jnp.concatenate(pieces_feat, axis=1)
    flag_table = jnp.concatenate(flags)
    edge_start = (index * EDGE_DEV).astype(jnp.int32)
    src = lax.dynamic_slice_in_dim(edge_src, edge_start, EDGE_DEV)
    dst = lax.dynamic_slice_in_dim(edge_dst, edge_start, EDGE_DEV)
    count = lax.dynamic_slice_in_dim(edge_count, index.astype(jnp.int32), 1)[0]
    live = (jnp.arange(EDGE_DEV, dtype=jnp.int32) < count).astype(jnp.float32) * flag_table[src]
    return edge_energy(table_pos, table_feat, src, dst, live, w_embed, w_env, w_update, w_out)

def reference(positions, features, send_list, edge_src, edge_dst, edge_count, w_embed, w_env, w_update, w_out):

    def total(coords):
        single = jax.checkpoint(lambda index: device_energy(index, coords, features, send_list, edge_src, edge_dst, edge_count, w_embed, w_env, w_update, w_out))
        parts = lax.map(single, jnp.arange(N_GX * N_GY, dtype=jnp.int32))
        return jnp.sum(parts)
    energy, gradient = jax.value_and_grad(total)(positions)
    return (-gradient, energy)
```

```python
import math

import jax
import jax.numpy as jnp
from jax import lax
from jax.experimental import pallas as pl
from jax.experimental.pallas import tpu as pltpu
from jax.sharding import PartitionSpec as P

C = 64
NB = 8
LAYERS = 2
ATOMS = 64
GHOST = 32
EDGES = 1024
SCALE = 16 ** (-0.5)
OFFSETS = ((-1, -1), (-1, 0), (-1, 1), (0, -1), (0, 1), (1, -1), (1, 0), (1, 1))
WIDTH = 6.0
CUTOFF = 5.0
SPAN = ((0, 64), (64, 256), (256, 576))
F32 = jnp.float32
BF16 = jnp.bfloat16
MESH = pl.DeviceIdType.MESH


def split(x):
    hi = x.astype(BF16)
    return hi, (x - hi.astype(F32)).astype(BF16)


def split3(x):
    hi = x.astype(BF16)
    rest = x - hi.astype(F32)
    mid = rest.astype(BF16)
    return hi, mid, (rest - mid.astype(F32)).astype(BF16)


def dot(x, y):
    return lax.dot_general(x, y, (((1,), (0,)), ((), ())), preferred_element_type=F32)


def dot_t(x, y):
    return lax.dot_general(x, y, (((1,), (1,)), ((), ())), preferred_element_type=F32)


def mul3(x, y, product=dot):
    return product(x[0], y[0]) + product(x[1], y[0]) + product(x[0], y[1])


def row_of(v):
    return jnp.concatenate([v[j : j + 1, :] for j in range(8)], axis=1)


def pick_lane(tables, index):
    lane = index & 127
    which = index >> 7
    result = None
    for t, table in enumerate(tables):
        wide = jnp.broadcast_to(table, (8, 128))
        got = jnp.take_along_axis(wide, lane, axis=1, mode="promise_in_bounds")
        result = got if result is None else jnp.where(which == t, got, result)
    return result


def silu_pair(q):
    s = 1.0 / (1.0 + jnp.exp(-q))
    value = q * s
    return value, s + value * (1.0 - s)


def phases_of(columns, rows):
    phases = []
    stride = 1
    while stride < columns:
        size = 4 if (columns // stride) % 4 == 0 else columns // stride
        phases.append(("gx", stride, size))
        stride *= size
    phases.append(("gy", 1, rows))
    return phases


def kernel(
    columns, rows, phases,
    pos_ref, feat_ref, send_ref, src_ref, dst_ref, count_ref, we_ref, wv_ref, wu_ref, wo_ref,
    forces_ref, energy_ref,
    pay, table, ah, al, oh, vh, vl, gsrc, gbuf, ebuf,
    send_sem, recv_sem, gsend_sem, grecv_sem, esend_sem, erecv_sem,
):
    a = lax.axis_index("gx")
    b = lax.axis_index("gy")

    def peer(k):
        dx, dy = OFFSETS[k]
        return (lax.rem(a + dx + columns, columns), b + dy)

    def when_valid(k, act, otherwise=None):
        dy = OFFSETS[k][1]
        if dy == 0:
            act()
            return
        good = (b > 0) if dy < 0 else (b < rows - 1)
        pl.when(good)(act)
        if otherwise is not None:
            pl.when(jnp.logical_not(good))(otherwise)

    def member(ph):
        axis, stride, size = phases[ph]
        index = a if axis == "gx" else b
        return lax.rem(index // stride, size)

    def energy_peer(ph, t):
        axis, stride, size = phases[ph]
        me = member(ph)
        step = (lax.rem(me + t, size) - me) * stride
        return (a + step, b) if axis == "gx" else (a, b + step)

    barrier = pltpu.get_barrier_semaphore()
    for k in range(8):
        when_valid(k, lambda k=k: pl.semaphore_signal(barrier, inc=1, device_id=peer(k), device_id_type=MESH))
    greeted = 0
    for ph in range(len(phases)):
        for t in range(1, phases[ph][2]):
            pl.semaphore_signal(barrier, inc=1, device_id=energy_peer(ph, t), device_id_type=MESH)
            greeted += 1

    we_hi, we_lo = split(we_ref[0 : 2 * C, :].T)
    we_both = jnp.concatenate(
        [jnp.concatenate([we_hi[:, 0:C], we_lo[:, 0:C]], axis=1),
         jnp.concatenate([we_hi[:, C : 2 * C], we_lo[:, C : 2 * C]], axis=1)], axis=0)
    feat = feat_ref[...]
    own = dot(we_both, jnp.concatenate([feat, feat], axis=0))
    own_src, own_dst = own[0:C], own[C : 2 * C]
    pos = pos_ref[...]
    send4 = jnp.concatenate([send_ref[...]] * 4, axis=1)
    st4 = (lax.broadcasted_iota(jnp.int32, (ATOMS, 128), 0) == send4).astype(F32).astype(BF16)
    exported = jnp.concatenate([own_src, pos, jnp.zeros((61, ATOMS), F32)], axis=0)
    e3 = split3(jnp.concatenate([exported, jnp.zeros((128, 128 - ATOMS), F32)], axis=1))
    st4_tall = jnp.concatenate([st4, jnp.zeros((128 - ATOMS, 128), BF16)], axis=0)
    payload = (dot(e3[2], st4_tall) + dot(e3[1], st4_tall)) + dot(e3[0], st4_tall)
    pay[...] = payload.T[0:GHOST, :]

    inner = jnp.logical_and(b > 0, b < rows - 1)
    pl.semaphore_wait(barrier, greeted + jnp.where(inner, 8, 5))

    def ghost_copy(k):
        return pltpu.make_async_remote_copy(
            src_ref=pay, dst_ref=table.at[7 - k], send_sem=send_sem.at[k], recv_sem=recv_sem.at[7 - k],
            device_id=peer(k), device_id_type=MESH,
        )

    for k in range(8):
        when_valid(k, lambda k=k: ghost_copy(k).start())

    src = src_ref[...]
    dst = dst_ref[...]
    block = (src - ATOMS) >> 5
    ghost = src >= ATOMS
    ox = jnp.zeros((8, 128), F32)
    oy = jnp.zeros((8, 128), F32)
    for k, (dx, dy) in enumerate(OFFSETS):
        here = jnp.logical_and(ghost, block == k)
        if dx:
            ox = jnp.where(here, WIDTH * dx, ox)
        if dy:
            oy = jnp.where(here, WIDTH * dy, oy)
    step_y = (oy * (1.0 / WIDTH)).astype(jnp.int32)
    reach = jnp.logical_and(b + step_y >= 0, b + step_y < rows)
    place = lax.broadcasted_iota(jnp.int32, (8, 128), 0) * 128 + lax.broadcasted_iota(jnp.int32, (8, 128), 1)
    live = jnp.where(jnp.logical_and(place < count_ref[...], reach), 1.0, 0.0)
    slot = jnp.where(ghost, src - ATOMS, src + 8 * GHOST)
    slot_row = row_of(slot)
    dst_row = row_of(dst)
    oh[0:320, :] = (lax.broadcasted_iota(jnp.int32, (320, EDGES), 0) == slot_row).astype(F32).astype(BF16)
    mask = lax.broadcasted_iota(jnp.int32, (ATOMS, EDGES), 0) == dst_row
    hot = mask.astype(F32).astype(BF16)
    oh[320:384, :] = hot
    ah[0:64, :] = hot
    al[0:64, :] = jnp.zeros((64, EDGES), BF16)
    pre_own = dot(jnp.concatenate(split(jnp.concatenate([own_src, own_dst], axis=1)), axis=0), oh[256:384, :])
    pre_own = pre_own[0:C] + pre_own[C : 2 * C]

    back_lhs, back_rhs, fore_lhs, fore_rhs, w0, w0t = [], [], [], [], [], []
    zero = jnp.zeros((C, C), F32)
    for layer in range(LAYERS):
        rows_fl, rows_fr, rows_bl, rows_br = [], [], [], []
        for d in range(3):
            env_hi, env_lo = split(wv_ref[layer, :, d * C : (d + 1) * C])
            upd_hi, upd_lo = split(wu_ref[layer, (d + 1) * C : (d + 2) * C, :])
            mt = dot(jnp.concatenate([env_hi, env_hi, env_lo, env_lo], axis=1),
                     jnp.concatenate([upd_hi, upd_lo, upd_hi, upd_lo], axis=0)) * SCALE
            m = mt.T
            mh, ml = split(jnp.concatenate([m, m], axis=1))
            rows_fl.append((jnp.concatenate([mh, ml], axis=0), mh))
            th, tl = split(jnp.concatenate([mt, mt], axis=1))
            rows_bl.append((jnp.concatenate([th, tl], axis=0), th))
            wide = jnp.concatenate([mt, zero], axis=1)
            rows_fr.append(split(jnp.concatenate([wide, wide], axis=0)))
            wide = jnp.concatenate([zero, m], axis=1)
            rows_br.append(split(jnp.concatenate([wide, wide], axis=0)))
        fore_lhs.append(rows_fl)
        fore_rhs.append(rows_fr)
        back_lhs.append(rows_bl)
        back_rhs.append(rows_br)
        own_w = wu_ref[layer, 0:C, :]
        w0.append(own_w)
        w0t.append(own_w.T)
    wr = we_ref[2 * C : 2 * C + NB, :]
    wr_low = wr - wr.astype(BF16).astype(F32)
    wr4 = jnp.concatenate([wr, wr, wr_low, jnp.zeros((104, C), F32)], axis=0).T.astype(BF16)
    wr2 = jnp.concatenate([wr, wr_low], axis=0)
    wr2 = jnp.concatenate([wr2, wr2], axis=1).astype(BF16)
    diagonal = lax.broadcasted_iota(jnp.int32, (C, C), 0) == lax.broadcasted_iota(jnp.int32, (C, C), 1)
    wo = jnp.sum(jnp.where(diagonal, wo_ref[...], 0.0), axis=1, keepdims=True)

    def blank(k):
        table[k] = jnp.zeros((GHOST, 128), F32)
        gbuf[k] = jnp.zeros((8, 128), F32)

    for k in range(8):
        when_valid(k, lambda k=k: ghost_copy(7 - k).wait_recv(), lambda k=k: blank(k))

    ghosts = jnp.concatenate([table[0:4].reshape(128, 128).T, table[4:8].reshape(128, 128).T], axis=1)
    own_pos = jnp.concatenate([pos, jnp.zeros((3, 64), F32)], axis=1)
    diff = []
    for i in range(3):
        at_ghost = ghosts[C + i : C + i + 1, :]
        mine = own_pos[i : i + 1, :]
        at_src = pick_lane([at_ghost[:, 0:128], at_ghost[:, 128:256], mine], slot)
        if i < 2:
            at_src = at_src + (ox, oy)[i]
        diff.append(at_src - pick_lane([mine], dst))
    dist = jnp.sqrt(diff[0] * diff[0] + diff[1] * diff[1] + diff[2] * diff[2] + 1.0)
    inv = 1.0 / dist
    ux, uy, uz = (v * inv for v in diff)
    root = math.sqrt(3.0)
    harm = [ux, uy, uz, root * ux * uy, root * uy * uz, 0.5 * (3.0 * uz * uz - 1.0), root * ux * uz,
            0.5 * root * (ux * ux - uy * uy)]
    short = jnp.maximum(1.0 - (dist * dist) * (1.0 / CUTOFF**2), 0.0)
    envelope = short * short
    cut = row_of(live * envelope)
    gain = envelope * inv
    slope = (-4.0 / CUTOFF**2) * dist * short
    gain_slope = (slope - gain) * inv
    for m in range(8):
        row = row_of(harm[m])
        high = row.astype(BF16).astype(F32)
        low = row - high
        ah[64 * (m + 1) : 64 * (m + 2), :] = jnp.where(mask, high, 0.0).astype(BF16)
        al[64 * (m + 1) : 64 * (m + 2), :] = jnp.where(mask, low, 0.0).astype(BF16)

    order = (lax.broadcasted_iota(jnp.int32, (NB, EDGES), 0) + 1).astype(F32)
    turns = order * row_of(jnp.minimum(dist, CUTOFF) * (1.0 / CUTOFF))
    whole = jnp.floor(turns + 0.5)
    angle = (turns - whole) * math.pi
    odd = whole - 2.0 * jnp.floor(whole * 0.5)
    sign = 1.0 - 2.0 * odd
    sq = angle * angle
    sine = 1.0 / 39916800.0
    for c in (-1.0 / 362880.0, 1.0 / 5040.0, -1.0 / 120.0, 1.0 / 6.0, -1.0):
        sine = c + sq * sine
    sine = -(angle * sine) * sign
    cosine = 1.0 / 479001600.0
    for c in (-1.0 / 3628800.0, 1.0 / 40320.0, -1.0 / 720.0, 1.0 / 24.0, -0.5, 1.0):
        cosine = c + sq * cosine
    cosine = cosine * sign
    gain_row = row_of(gain)
    radial = sine * gain_row
    radial_low = radial - radial.astype(BF16).astype(F32)
    radial4 = jnp.concatenate([radial, radial_low, radial, jnp.zeros((104, EDGES), F32)], axis=0).astype(BF16)

    from_ghost = dot(jnp.concatenate(split(ghosts[0:C, :]), axis=0), oh[0:256, :])
    pre = pre_own + from_ghost[0:C] + from_ghost[C : 2 * C] + dot(wr4, radial4)
    value0, grad0 = silu_pair(pre)
    feats = [value0 * cut]
    values, grads, maps = [], [], []

    def environment(two):
        first = dot_t(ah[0:576, :], two)
        return first[0:64], first[64:576] + dot_t(al[64:576, :], two)

    def mixed(parts, lhs, rhs, own_w):
        flat, tall = [], []
        for d in range(3):
            lo, hi = SPAN[d]
            x = split(parts[0] if d == 0 else parts[1][lo - 64 : hi - 64])
            both = dot_t(lhs[d][0], x[0])
            flat.append(both[0:C] + both[C : 2 * C] + dot_t(lhs[d][1], x[1]))
            if d:
                tall.append(mul3(x, rhs[d]))
        return jnp.concatenate(flat + [own_w], axis=1), jnp.concatenate(tall, axis=0)

    def spread(flat):
        hi, lo = split(flat)
        both = dot(jnp.concatenate([hi, lo], axis=0), ah[...])
        return both[0:C] + both[C : 2 * C] + dot(hi, al[...])

    def keep(row, x):
        hi, lo = split(x)
        vh[row : row + C, :] = hi
        vl[row : row + C, :] = lo
        ah[576:640, :] = hi
        al[576:640, :] = lo
        return jnp.concatenate([hi, lo], axis=0)

    for layer in range(LAYERS):
        f = feats[-1]
        parts = environment(keep(192 - 128 * layer, f))
        flat, tall = mixed(parts, fore_lhs[layer], fore_rhs[layer], w0t[layer])
        maps.append(tall)
        q = spread(flat)
        value, grad = silu_pair(q)
        values.append(value)
        grads.append(grad)
        feats.append(f + value * cut)

    def energy_copy(ph, t):
        size = phases[ph][2]
        me = member(ph)
        return pltpu.make_async_remote_copy(
            src_ref=ebuf.at[ph, me], dst_ref=ebuf.at[ph, me], send_sem=esend_sem.at[ph, t],
            recv_sem=erecv_sem.at[ph, t], device_id=energy_peer(ph, t), device_id_type=MESH,
        )

    def energy_out(ph, x):
        ebuf[ph, member(ph)] = x
        for t in range(1, phases[ph][2]):
            energy_copy(ph, t).start()

    def energy_in(ph):
        size = phases[ph][2]
        for t in range(1, size):
            came = lax.rem(member(ph) + size - t, size)
            pltpu.make_async_remote_copy(
                src_ref=ebuf.at[ph, came], dst_ref=ebuf.at[ph, came], send_sem=esend_sem.at[ph, t],
                recv_sem=erecv_sem.at[ph, t], device_id=energy_peer(ph, t), device_id_type=MESH,
            ).wait_recv()
        total = ebuf[ph, 0]
        for t in range(1, size):
            total = total + ebuf[ph, t]
        return total

    live_row = row_of(live)
    df = wo * live_row
    per_edge = feats[LAYERS] * df
    folded = per_edge[0:8]
    for s in range(1, 8):
        folded = folded + per_edge[8 * s : 8 * s + 8]
    piece = folded[:, 0:128]
    for j in range(1, 8):
        piece = piece + folded[:, 128 * j : 128 * j + 128]
    energy_out(0, piece)
    last = len(phases) - 1
    done = 0

    dcut = jnp.zeros((1, EDGES), F32)
    uts = [None] * LAYERS
    for layer in reversed(range(LAYERS)):
        dcut = dcut + jnp.sum(df * values[layer], axis=0, keepdims=True)
        dq = df * cut * grads[layer]
        parts = environment(keep(128 - 128 * layer, dq))
        flat, tall = mixed(parts, back_lhs[layer], back_rhs[layer], w0[layer])
        uts[layer] = maps[layer] + tall
        df = df + spread(flat)
        if done < last:
            energy_out(done + 1, energy_in(done))
            done += 1
    dcut = dcut + jnp.sum(df * value0, axis=0, keepdims=True)
    dpre = df * cut * grad0
    both = dot(wr2, jnp.concatenate(split(dpre), axis=0))
    dradial = both[0:8] + both[8:16]
    steps = order * (math.pi / CUTOFF)
    dr = jnp.sum(dradial * (steps * cosine * gain_row + sine * row_of(gain_slope)), axis=0, keepdims=True)
    dr = dr + dcut * row_of(live * slope)
    ut = jnp.concatenate([uts[1], uts[0]], axis=1)
    uh, ul = split(ut)
    tiles = []
    for n in range(4):
        lanes = slice(256 * n, 256 * (n + 1))
        right = vh[:, lanes]
        part = dot(uh, right) + dot(ul, right) + dot(uh, vl[:, lanes])
        keep_here = mask[:, lanes]
        tiles.append([
            jnp.sum(jnp.where(keep_here, part[64 * m : 64 * (m + 1)], 0.0), axis=0, keepdims=True) for m in range(8)
        ])
    g = [jnp.concatenate([tiles[n][m] for n in range(4)], axis=1) for m in range(8)]
    while done < last:
        energy_out(done + 1, energy_in(done))
        done += 1
    xr, yr, zr, ir = row_of(ux), row_of(uy), row_of(uz), row_of(inv)
    dux = g[0] + root * (g[3] * yr + g[6] * zr + g[7] * xr)
    duy = g[1] + root * (g[3] * xr + g[4] * zr - g[7] * yr)
    duz = g[2] + root * (g[4] * yr + g[6] * xr) + 3.0 * g[5] * zr
    radial_part = dr - (dux * xr + duy * yr + duz * zr) * ir
    dd = jnp.concatenate(
        [dux * ir + radial_part * xr, duy * ir + radial_part * yr, duz * ir + radial_part * zr,
         jnp.zeros((5, EDGES), F32)], axis=0)
    dd_low = dd - dd.astype(BF16).astype(F32)
    scattered = dot_t(jnp.concatenate([dd, dd_low], axis=0).astype(BF16), oh[...])
    scattered = scattered[0:8] + scattered[8:16]
    gsrc[0] = scattered[:, 0:128]
    gsrc[1] = scattered[:, 128:256]

    def force_copy(k):
        return pltpu.make_async_remote_copy(
            src_ref=gsrc.at[k // 4], dst_ref=gbuf.at[7 - k], send_sem=gsend_sem.at[k], recv_sem=grecv_sem.at[7 - k],
            device_id=peer(k), device_id_type=MESH,
        )

    for k in range(8):
        when_valid(k, lambda k=k: force_copy(k).start())
    at_own = scattered[:, 256:320] - scattered[:, 320:384]
    for k in range(8):
        when_valid(k, lambda k=k: force_copy(7 - k).wait_recv())
    group = lax.broadcasted_iota(jnp.int32, (8, 128), 1) >> 5
    acc = jnp.zeros((8, 128), F32)
    for k in range(8):
        acc = acc + jnp.where(group == (7 - k) % 4, gbuf[k], 0.0)
    acc_low = acc - acc.astype(BF16).astype(F32)
    returned = dot_t(jnp.concatenate([acc, acc_low], axis=0).astype(BF16), st4)
    returned = returned[0:8] + returned[8:16]
    forces_ref[...] = -(at_own + returned)[0:3, :]

    total = energy_in(last)
    energy_ref[...] = jnp.sum(jnp.sum(total, axis=0, keepdims=True), axis=1, keepdims=True)

    for k in range(8):
        when_valid(k, lambda k=k: (ghost_copy(k).wait_send(), force_copy(k).wait_send())[0])
    for ph in range(len(phases)):
        for t in range(1, phases[ph][2]):
            energy_copy(ph, t).wait_send()


def solution(mesh):
    columns, rows = mesh.shape["gx"], mesh.shape["gy"]
    phases = phases_of(columns, rows)
    most = max(size for _, _, size in phases)

    def per_device(positions, features, send_list, edge_src, edge_dst, edge_count, w_embed, w_env, w_update, w_out):
        def body(*refs):
            kernel(columns, rows, phases, *refs)

        vmem = pl.BlockSpec(memory_space=pltpu.VMEM)
        forces, energy = pl.pallas_call(
            body,
            out_shape=(jax.ShapeDtypeStruct((3, ATOMS), F32), jax.ShapeDtypeStruct((1, 1), F32)),
            in_specs=[vmem] * 10,
            out_specs=(vmem, vmem),
            scratch_shapes=[
                pltpu.VMEM((GHOST, 128), F32),
                pltpu.VMEM((8, GHOST, 128), F32),
                pltpu.VMEM((640, EDGES), BF16),
                pltpu.VMEM((640, EDGES), BF16),
                pltpu.VMEM((384, EDGES), BF16),
                pltpu.VMEM((256, EDGES), BF16),
                pltpu.VMEM((256, EDGES), BF16),
                pltpu.VMEM((2, 8, 128), F32),
                pltpu.VMEM((8, 8, 128), F32),
                pltpu.VMEM((len(phases), most, 8, 128), F32),
                pltpu.SemaphoreType.DMA((8,)),
                pltpu.SemaphoreType.DMA((8,)),
                pltpu.SemaphoreType.DMA((8,)),
                pltpu.SemaphoreType.DMA((8,)),
                pltpu.SemaphoreType.DMA((len(phases), most)),
                pltpu.SemaphoreType.DMA((len(phases), most)),
            ],
            compiler_params=pltpu.CompilerParams(
                collective_id=0, has_side_effects=True, vmem_limit_bytes=40 * 1024 * 1024
            ),
        )(
            positions, features, send_list.reshape(1, GHOST), edge_src.reshape(8, 128), edge_dst.reshape(8, 128),
            edge_count.reshape(1, 1), w_embed, w_env, w_update, w_out.reshape(1, C),
        )
        return forces, energy.reshape(())

    placed = (
        P(None, ("gx", "gy")), P(None, ("gx", "gy")), P(("gx", "gy")), P(("gx", "gy")), P(("gx", "gy")),
        P(("gx", "gy")), P(), P(), P(), P(),
    )
    return jax.shard_map(
        per_device, mesh=mesh, in_specs=placed, out_specs=(P(None, ("gx", "gy")), P()), check_vma=False
    )
```

```python
import math

import jax
import jax.numpy as jnp
from jax import lax
from jax.experimental import pallas as pl
from jax.experimental.pallas import tpu as pltpu
from jax.sharding import PartitionSpec as P

C = 64
NB = 8
LAYERS = 2
ATOMS = 64
GHOST = 32
EDGES = 1024
SCALE = 16 ** (-0.5)
OFFSETS = ((-1, -1), (-1, 0), (-1, 1), (0, -1), (0, 1), (1, -1), (1, 0), (1, 1))
WIDTH = 6.0
CUTOFF = 5.0
SPAN = ((0, 64), (64, 256), (256, 576))
F32 = jnp.float32
BF16 = jnp.bfloat16
MESH = pl.DeviceIdType.MESH
TILE = 256
CUT, LIVE, UX, UY, UZ, INV, DIST, GAIN, BEND, SLOPE, DCUT = 0, 1, 2, 3, 4, 5, 6, 7, 8, 9, 10


def split(x):
    hi = x.astype(BF16)
    return hi, (x - hi.astype(F32)).astype(BF16)


def split3(x):
    hi = x.astype(BF16)
    rest = x - hi.astype(F32)
    mid = rest.astype(BF16)
    return hi, mid, (rest - mid.astype(F32)).astype(BF16)


def dot(x, y):
    return lax.dot_general(x, y, (((1,), (0,)), ((), ())), preferred_element_type=F32)


def dot_t(x, y):
    return lax.dot_general(x, y, (((1,), (1,)), ((), ())), preferred_element_type=F32)


def mul3(x, y, product=dot):
    return product(x[0], y[0]) + product(x[1], y[0]) + product(x[0], y[1])


def pick_lane(tables, index):
    lane = index & 127
    which = index >> 7
    result = None
    for t, table in enumerate(tables):
        wide = jnp.broadcast_to(table, (8, 128))
        got = jnp.take_along_axis(wide, lane, axis=1, mode="promise_in_bounds")
        result = got if result is None else jnp.where(which == t, got, result)
    return result


def phases_of(columns, rows):
    phases = []
    stride = 1
    while stride < columns:
        size = 4 if (columns // stride) % 4 == 0 else columns // stride
        phases.append(("gx", stride, size))
        stride *= size
    phases.append(("gy", 1, rows))
    return phases


def kernel(
    columns, rows, phases,
    pos_in, feat_in, send_in, src_in, dst_in, count_in, we_in, wv_in, wu_in, wo_in,
    forces_ref, energy_ref,
    pos_ref, feat_ref, send_ref, src_ref, dst_ref, count_ref, we_ref, wv_ref, wu_ref, wo_ref,
    pay, table, ah, al, oh, vh, vl, two, row, value, gain_cut, df, dradial_map, ddb, gsrc, gbuf, ebuf,
    in_sem, send_sem, recv_sem, gsend_sem, grecv_sem, esend_sem, erecv_sem,
):
    a = lax.axis_index("gx")
    b = lax.axis_index("gy")

    def peer(k):
        dx, dy = OFFSETS[k]
        return (lax.rem(a + dx + columns, columns), b + dy)

    def when_valid(k, act, otherwise=None):
        dy = OFFSETS[k][1]
        if dy == 0:
            act()
            return
        good = (b > 0) if dy < 0 else (b < rows - 1)
        pl.when(good)(act)
        if otherwise is not None:
            pl.when(jnp.logical_not(good))(otherwise)

    def member(ph):
        axis, stride, size = phases[ph]
        index = a if axis == "gx" else b
        return lax.rem(index // stride, size)

    def energy_peer(ph, t):
        axis, stride, size = phases[ph]
        me = member(ph)
        step = (lax.rem(me + t, size) - me) * stride
        return (a + step, b) if axis == "gx" else (a, b + step)

    barrier = pltpu.get_barrier_semaphore()
    for k in range(8):
        when_valid(k, lambda k=k: pl.semaphore_signal(barrier, inc=1, device_id=peer(k), device_id_type=MESH))
    greeted = 0
    for ph in range(len(phases)):
        for t in range(1, phases[ph][2]):
            pl.semaphore_signal(barrier, inc=1, device_id=energy_peer(ph, t), device_id_type=MESH)
            greeted += 1

    fetched = [
        pltpu.make_async_copy(given, held, in_sem.at[i])
        for i, (given, held) in enumerate([
            (pos_in, pos_ref), (feat_in, feat_ref), (send_in, send_ref), (we_in, we_ref), (src_in, src_ref),
            (dst_in, dst_ref), (count_in, count_ref), (wv_in, wv_ref), (wu_in, wu_ref), (wo_in, wo_ref)])
    ]
    for copy in fetched:
        copy.start()
    for copy in fetched[0:4]:
        copy.wait()

    we_hi, we_lo = split(we_ref[:, 0 : 2 * C])
    we_both = jnp.concatenate(
        [jnp.concatenate([we_hi[:, 0:C], we_lo[:, 0:C]], axis=1),
         jnp.concatenate([we_hi[:, C : 2 * C], we_lo[:, C : 2 * C]], axis=1)], axis=0)
    feat = feat_ref[...]
    own = dot(we_both, jnp.concatenate([feat, feat], axis=0))
    own_src, own_dst = own[0:C], own[C : 2 * C]
    pos = pos_ref[...]
    send4 = jnp.concatenate([send_ref[...]] * 4, axis=1)
    st4 = (lax.broadcasted_iota(jnp.int32, (ATOMS, 128), 0) == send4).astype(F32).astype(BF16)
    exported = jnp.concatenate([own_src, pos, jnp.zeros((61, ATOMS), F32)], axis=0)
    e3 = split3(jnp.concatenate([exported, jnp.zeros((128, 128 - ATOMS), F32)], axis=1))
    st4_tall = jnp.concatenate([st4, jnp.zeros((128 - ATOMS, 128), BF16)], axis=0)
    payload = (dot(e3[2], st4_tall) + dot(e3[1], st4_tall)) + dot(e3[0], st4_tall)
    pay[...] = payload.T[0:GHOST, :]

    inner = jnp.logical_and(b > 0, b < rows - 1)
    pl.semaphore_wait(barrier, greeted + jnp.where(inner, 8, 5))

    def ghost_copy(k):
        return pltpu.make_async_remote_copy(
            src_ref=pay, dst_ref=table.at[7 - k], send_sem=send_sem.at[k], recv_sem=recv_sem.at[7 - k],
            device_id=peer(k), device_id_type=MESH,
        )

    for k in range(8):
        when_valid(k, lambda k=k: ghost_copy(k).start())
    for copy in fetched[4:]:
        copy.wait()

    def put_row(i, v):
        for j in range(8):
            row[i : i + 1, 128 * j : 128 * (j + 1)] = v[j : j + 1, :]

    def lanes_of(n):
        return slice(TILE * n, TILE * (n + 1))

    def tiles(act):
        for n in range(EDGES // TILE):
            act(lanes_of(n))

    src = src_ref[...]
    dst = dst_ref[...]
    block = (src - ATOMS) >> 5
    ghost = src >= ATOMS
    ox = jnp.zeros((8, 128), F32)
    oy = jnp.zeros((8, 128), F32)
    for k, (dx, dy) in enumerate(OFFSETS):
        here = jnp.logical_and(ghost, block == k)
        if dx:
            ox = jnp.where(here, WIDTH * dx, ox)
        if dy:
            oy = jnp.where(here, WIDTH * dy, oy)
    step_y = (oy * (1.0 / WIDTH)).astype(jnp.int32)
    reach = jnp.logical_and(b + step_y >= 0, b + step_y < rows)
    place = lax.broadcasted_iota(jnp.int32, (8, 128), 0) * 128 + lax.broadcasted_iota(jnp.int32, (8, 128), 1)
    live = jnp.where(jnp.logical_and(place < count_ref[...], reach), 1.0, 0.0)
    put_row(LIVE, live)
    slot = jnp.where(ghost, src - ATOMS, src + 8 * GHOST)
    for j in range(8):
        lanes = slice(128 * j, 128 * (j + 1))
        oh[0:320, lanes] = (
            lax.broadcasted_iota(jnp.int32, (320, 128), 0) == slot[j : j + 1, :]).astype(F32).astype(BF16)
        hot = (lax.broadcasted_iota(jnp.int32, (ATOMS, 128), 0) == dst[j : j + 1, :]).astype(F32).astype(BF16)
        oh[320:384, lanes] = hot
        ah[0:64, lanes] = hot
        al[0:64, lanes] = jnp.zeros((64, 128), BF16)

    back_lhs, back_rhs, fore_lhs, fore_rhs, w0, w0t = [], [], [], [], [], []
    zero = jnp.zeros((C, C), F32)
    for layer in range(LAYERS):
        rows_fl, rows_fr, rows_bl, rows_br = [], [], [], []
        for d in range(3):
            env_hi, env_lo = split(wv_ref[layer, :, d * C : (d + 1) * C])
            upd_hi, upd_lo = split(wu_ref[layer, :, (d + 1) * C : (d + 2) * C])
            m = dot_t(jnp.concatenate([upd_hi, upd_hi, upd_lo, upd_lo], axis=1),
                      jnp.concatenate([env_hi, env_lo, env_hi, env_lo], axis=1)) * SCALE
            mt = m.T
            mh, ml = split(jnp.concatenate([m, m], axis=1))
            rows_fl.append((jnp.concatenate([mh, ml], axis=0), mh))
            th, tl = split(jnp.concatenate([mt, mt], axis=1))
            rows_bl.append((jnp.concatenate([th, tl], axis=0), th))
            wide = jnp.concatenate([mt, zero], axis=1)
            rows_fr.append(split(jnp.concatenate([wide, wide], axis=0)))
            wide = jnp.concatenate([zero, m], axis=1)
            rows_br.append(split(jnp.concatenate([wide, wide], axis=0)))
        fore_lhs.append(rows_fl)
        fore_rhs.append(rows_fr)
        back_lhs.append(rows_bl)
        back_rhs.append(rows_br)
        own_w = wu_ref[layer, :, 0:C]
        w0.append(own_w.T)
        w0t.append(own_w)
    wrt = we_ref[:, 2 * C : 2 * C + NB]
    wr = jnp.concatenate([wrt, jnp.zeros((C, 128 - NB), F32)], axis=1).T[0:NB, :]
    wr_low = wr - wr.astype(BF16).astype(F32)
    wr4 = jnp.concatenate([wr, wr, wr_low, jnp.zeros((104, C), F32)], axis=0).T.astype(BF16)
    wr2 = jnp.concatenate([wr, wr_low], axis=0)
    wr2 = jnp.concatenate([wr2, wr2], axis=1).astype(BF16)
    diagonal = lax.broadcasted_iota(jnp.int32, (C, C), 0) == lax.broadcasted_iota(jnp.int32, (C, C), 1)
    wo = jnp.sum(jnp.where(diagonal, wo_ref[...], 0.0), axis=1, keepdims=True)

    def blank(k):
        table[k] = jnp.zeros((GHOST, 128), F32)
        gbuf[k] = jnp.zeros((8, 128), F32)

    for k in range(8):
        when_valid(k, lambda k=k: ghost_copy(7 - k).wait_recv(), lambda k=k: blank(k))

    ghosts = jnp.concatenate([table[0:4].reshape(128, 128).T, table[4:8].reshape(128, 128).T], axis=1)
    own_pos = jnp.concatenate([pos, jnp.zeros((3, 64), F32)], axis=1)
    diff = []
    for i in range(3):
        at_ghost = ghosts[C + i : C + i + 1, :]
        mine = own_pos[i : i + 1, :]
        at_src = pick_lane([at_ghost[:, 0:128], at_ghost[:, 128:256], mine], slot)
        if i < 2:
            at_src = at_src + (ox, oy)[i]
        diff.append(at_src - pick_lane([mine], dst))
    dist = jnp.sqrt(diff[0] * diff[0] + diff[1] * diff[1] + diff[2] * diff[2] + 1.0)
    inv = 1.0 / dist
    ux, uy, uz = (v * inv for v in diff)
    root = math.sqrt(3.0)
    harm = [ux, uy, uz, root * ux * uy, root * uy * uz, 0.5 * (3.0 * uz * uz - 1.0), root * ux * uz,
            0.5 * root * (ux * ux - uy * uy)]
    short = jnp.maximum(1.0 - (dist * dist) * (1.0 / CUTOFF**2), 0.0)
    envelope = short * short
    gain = envelope * inv
    slope = (-4.0 / CUTOFF**2) * dist * short
    put_row(DIST, jnp.minimum(dist, CUTOFF) * (1.0 / CUTOFF))
    put_row(GAIN, gain)
    put_row(BEND, (slope - gain) * inv)
    put_row(CUT, live * envelope)
    put_row(SLOPE, live * slope)
    for i, v in ((UX, ux), (UY, uy), (UZ, uz), (INV, inv)):
        put_row(i, v)
    for m in range(8):
        for j in range(8):
            lanes = slice(128 * j, 128 * (j + 1))
            wide = jnp.broadcast_to(harm[m][j : j + 1, :], (16, 128))
            high, low = split(wide)
            hot = ah[0:64, lanes]
            ah[64 * (m + 1) : 64 * (m + 2), lanes] = hot * jnp.concatenate([high] * 4, axis=0)
            al[64 * (m + 1) : 64 * (m + 2), lanes] = hot * jnp.concatenate([low] * 4, axis=0)

    emb_hi, emb_lo = split(jnp.concatenate([ghosts[0:C, :], own_src, own_dst], axis=1))
    emb = jnp.concatenate(
        [jnp.concatenate([emb_hi, wr4], axis=1), jnp.concatenate([emb_lo, jnp.zeros((C, 128), BF16)], axis=1)], axis=0)
    order = (lax.broadcasted_iota(jnp.int32, (NB, TILE), 0) + 1).astype(F32)

    def keep(lanes, place, x):
        hi, lo = split(x)
        vh[place : place + C, lanes] = hi
        vl[place : place + C, lanes] = lo
        ah[576:640, lanes] = hi
        al[576:640, lanes] = lo
        two[0:C, lanes] = hi
        two[C : 2 * C, lanes] = lo

    def activate(lanes, stage, q):
        s = 1.0 / (1.0 + jnp.exp(-q))
        v = q * s
        cut = row[CUT : CUT + 1, lanes]
        value[stage, :, lanes] = v
        gain_cut[stage, :, lanes] = (s + v * (1.0 - s)) * cut
        return v * cut

    def embed(lanes):
        turns = order * row[DIST : DIST + 1, lanes]
        whole = jnp.floor(turns + 0.5)
        angle = (turns - whole) * math.pi
        sign = 1.0 - 2.0 * (whole - 2.0 * jnp.floor(whole * 0.5))
        sq = angle * angle
        sine = 1.0 / 39916800.0
        for c in (-1.0 / 362880.0, 1.0 / 5040.0, -1.0 / 120.0, 1.0 / 6.0, -1.0):
            sine = c + sq * sine
        sine = -(angle * sine) * sign
        cosine = 1.0 / 479001600.0
        for c in (-1.0 / 3628800.0, 1.0 / 40320.0, -1.0 / 720.0, 1.0 / 24.0, -0.5, 1.0):
            cosine = c + sq * cosine
        cosine = cosine * sign
        near = row[GAIN : GAIN + 1, lanes]
        radial = sine * near
        dradial_map[:, lanes] = order * (math.pi / CUTOFF) * cosine * near + sine * row[BEND : BEND + 1, lanes]
        low = radial - radial.astype(BF16).astype(F32)
        oh[384:512, lanes] = jnp.concatenate([radial, low, radial, jnp.zeros((104, TILE), F32)], axis=0).astype(BF16)
        both = dot(emb, oh[:, lanes])
        f = activate(lanes, 0, both[0:C] + both[C : 2 * C])
        df[:, lanes] = f
        keep(lanes, 192, f)

    def environment():
        first = dot_t(ah[0:576, :], two[...])
        return first[0:64], first[64:576] + dot_t(al[64:576, :], two[...])

    def mixed(parts, lhs, rhs, own_w):
        flat, tall = [], []
        for d in range(3):
            lo, hi = SPAN[d]
            x = split(parts[0] if d == 0 else parts[1][lo - 64 : hi - 64])
            both = dot_t(lhs[d][0], x[0])
            flat.append(both[0:C] + both[C : 2 * C] + dot_t(lhs[d][1], x[1]))
            if d:
                tall.append(mul3(x, rhs[d]))
        hi, lo = split(jnp.concatenate(flat + [own_w], axis=1))
        return (jnp.concatenate([hi, lo], axis=0), hi), jnp.concatenate(tall, axis=0)

    def spread(lanes, flat):
        both = dot(flat[0], ah[:, lanes])
        return both[0:C] + both[C : 2 * C] + dot(flat[1], al[:, lanes])

    def energy_copy(ph, t):
        me = member(ph)
        return pltpu.make_async_remote_copy(
            src_ref=ebuf.at[ph, me], dst_ref=ebuf.at[ph, me], send_sem=esend_sem.at[ph, t],
            recv_sem=erecv_sem.at[ph, t], device_id=energy_peer(ph, t), device_id_type=MESH,
        )

    def energy_out(ph, x):
        ebuf[ph, member(ph)] = x
        for t in range(1, phases[ph][2]):
            energy_copy(ph, t).start()

    def energy_in(ph):
        size = phases[ph][2]
        for t in range(1, size):
            came = lax.rem(member(ph) + size - t, size)
            pltpu.make_async_remote_copy(
                src_ref=ebuf.at[ph, came], dst_ref=ebuf.at[ph, came], send_sem=esend_sem.at[ph, t],
                recv_sem=erecv_sem.at[ph, t], device_id=energy_peer(ph, t), device_id_type=MESH,
            ).wait_recv()
        total = ebuf[ph, 0]
        for t in range(1, size):
            total = total + ebuf[ph, t]
        return total

    last = len(phases) - 1

    tiles(embed)
    flat, map0 = mixed(environment(), fore_lhs[0], fore_rhs[0], w0t[0])

    def first_layer(lanes):
        f = df[:, lanes] + activate(lanes, 1, spread(lanes, flat))
        df[:, lanes] = f
        keep(lanes, 64, f)

    tiles(first_layer)
    flat, map1 = mixed(environment(), fore_lhs[1], fore_rhs[1], w0t[1])
    pieces = []

    def turn(lanes):
        q = spread(lanes, flat)
        s = 1.0 / (1.0 + jnp.exp(-q))
        v = q * s
        cut = row[CUT : CUT + 1, lanes]
        f = df[:, lanes] + v * cut
        g = wo * row[LIVE : LIVE + 1, lanes]
        per_edge = f * g
        piece = per_edge[0:8]
        for i in range(1, 8):
            piece = piece + per_edge[8 * i : 8 * i + 8]
        pieces.append(piece[:, 0:128] + piece[:, 128:256])
        df[:, lanes] = g
        row[DCUT : DCUT + 1, lanes] = jnp.sum(g * v, axis=0, keepdims=True)
        keep(lanes, 0, g * ((s + v * (1.0 - s)) * cut))

    tiles(turn)
    energy_out(0, (pieces[0] + pieces[1]) + (pieces[2] + pieces[3]))

    flat, tall = mixed(environment(), back_lhs[1], back_rhs[1], w0[1])
    ut1 = map1 + tall

    def back_first(lanes):
        g = df[:, lanes] + spread(lanes, flat)
        df[:, lanes] = g
        row[DCUT : DCUT + 1, lanes] += jnp.sum(g * value[1, :, lanes], axis=0, keepdims=True)
        keep(lanes, 128, g * gain_cut[1, :, lanes])

    tiles(back_first)
    for ph in range(0, min(1, last)):
        energy_out(ph + 1, energy_in(ph))
    flat, tall = mixed(environment(), back_lhs[0], back_rhs[0], w0[0])
    for ph in range(1, min(2, last)):
        energy_out(ph + 1, energy_in(ph))
    uh, ul = split(jnp.concatenate([ut1, map0 + tall], axis=1))

    def back_embed(lanes):
        g = df[:, lanes] + spread(lanes, flat)
        dcut = row[DCUT : DCUT + 1, lanes] + jnp.sum(g * value[0, :, lanes], axis=0, keepdims=True)
        both = dot(wr2, jnp.concatenate(split(g * gain_cut[0, :, lanes]), axis=0))
        dr = jnp.sum((both[0:8] + both[8:16]) * dradial_map[:, lanes], axis=0, keepdims=True)
        dr = dr + dcut * row[SLOPE : SLOPE + 1, lanes]
        right = vh[:, lanes]
        part = dot(uh, right) + dot(ul, right) + dot(uh, vl[:, lanes])
        hot = ah[0:64, lanes].astype(F32)
        g = [jnp.sum(hot * part[64 * m : 64 * (m + 1)], axis=0, keepdims=True) for m in range(8)]
        xr, yr, zr, ir = (row[i : i + 1, lanes] for i in (UX, UY, UZ, INV))
        dux = g[0] + root * (g[3] * yr + g[6] * zr + g[7] * xr)
        duy = g[1] + root * (g[3] * xr + g[4] * zr - g[7] * yr)
        duz = g[2] + root * (g[4] * yr + g[6] * xr) + 3.0 * g[5] * zr
        along = dr - (dux * xr + duy * yr + duz * zr) * ir
        dd = jnp.concatenate(
            [dux * ir + along * xr, duy * ir + along * yr, duz * ir + along * zr, jnp.zeros((5, TILE), F32)], axis=0)
        ddb[:, lanes] = jnp.concatenate([dd, dd - dd.astype(BF16).astype(F32)], axis=0).astype(BF16)

    tiles(back_embed)
    for ph in range(2, last):
        energy_out(ph + 1, energy_in(ph))
    scattered = dot_t(ddb[...], oh[0:384, :])
    scattered = scattered[0:8] + scattered[8:16]
    gsrc[0] = scattered[:, 0:128]
    gsrc[1] = scattered[:, 128:256]
    def force_copy(k):
        return pltpu.make_async_remote_copy(
            src_ref=gsrc.at[k // 4], dst_ref=gbuf.at[7 - k], send_sem=gsend_sem.at[k], recv_sem=grecv_sem.at[7 - k],
            device_id=peer(k), device_id_type=MESH,
        )

    for k in range(8):
        when_valid(k, lambda k=k: force_copy(k).start())
    at_own = scattered[:, 256:320] - scattered[:, 320:384]
    for k in range(8):
        when_valid(k, lambda k=k: force_copy(7 - k).wait_recv())
    group = lax.broadcasted_iota(jnp.int32, (8, 128), 1) >> 5
    acc = jnp.zeros((8, 128), F32)
    for k in range(8):
        acc = acc + jnp.where(group == (7 - k) % 4, gbuf[k], 0.0)
    acc_low = acc - acc.astype(BF16).astype(F32)
    returned = dot_t(jnp.concatenate([acc, acc_low], axis=0).astype(BF16), st4)
    returned = returned[0:8] + returned[8:16]
    forces_ref[...] = -(at_own + returned)[0:3, :]

    total = energy_in(last)
    energy_ref[...] = jnp.sum(jnp.sum(total, axis=0, keepdims=True), axis=1, keepdims=True)

    for k in range(8):
        when_valid(k, lambda k=k: (ghost_copy(k).wait_send(), force_copy(k).wait_send())[0])
    for ph in range(len(phases)):
        for t in range(1, phases[ph][2]):
            energy_copy(ph, t).wait_send()


def solution(mesh):
    columns, rows = mesh.shape["gx"], mesh.shape["gy"]
    phases = phases_of(columns, rows)
    most = max(size for _, _, size in phases)

    def per_device(positions, features, send_list, edge_src, edge_dst, edge_count, w_embed, w_env, w_update, w_out):
        def body(*refs):
            kernel(columns, rows, phases, *refs)

        vmem = pl.BlockSpec(memory_space=pltpu.VMEM)
        anywhere = pl.BlockSpec(memory_space=pl.ANY)
        forces, energy = pl.pallas_call(
            body,
            out_shape=(jax.ShapeDtypeStruct((3, ATOMS), F32), jax.ShapeDtypeStruct((1, 1), F32)),
            in_specs=[anywhere] * 10,
            out_specs=(vmem, vmem),
            scratch_shapes=[
                pltpu.VMEM((3, ATOMS), F32),
                pltpu.VMEM((C, ATOMS), BF16),
                pltpu.VMEM((1, GHOST), jnp.int32),
                pltpu.VMEM((8, 128), jnp.int32),
                pltpu.VMEM((8, 128), jnp.int32),
                pltpu.VMEM((1, 1), jnp.int32),
                pltpu.VMEM((C, 2 * C + NB), F32),
                pltpu.VMEM((LAYERS, C, 3 * C), F32),
                pltpu.VMEM((LAYERS, C, 4 * C), F32),
                pltpu.VMEM((1, C), F32),
                pltpu.VMEM((GHOST, 128), F32),
                pltpu.VMEM((8, GHOST, 128), F32),
                pltpu.VMEM((640, EDGES), BF16),
                pltpu.VMEM((640, EDGES), BF16),
                pltpu.VMEM((512, EDGES), BF16),
                pltpu.VMEM((256, EDGES), BF16),
                pltpu.VMEM((256, EDGES), BF16),
                pltpu.VMEM((128, EDGES), BF16),
                pltpu.VMEM((16, EDGES), F32),
                pltpu.VMEM((2, C, EDGES), F32),
                pltpu.VMEM((2, C, EDGES), F32),
                pltpu.VMEM((C, EDGES), F32),
                pltpu.VMEM((NB, EDGES), F32),
                pltpu.VMEM((16, EDGES), BF16),
                pltpu.VMEM((2, 8, 128), F32),
                pltpu.VMEM((8, 8, 128), F32),
                pltpu.VMEM((len(phases), most, 8, 128), F32),
                pltpu.SemaphoreType.DMA((10,)),
                pltpu.SemaphoreType.DMA((8,)),
                pltpu.SemaphoreType.DMA((8,)),
                pltpu.SemaphoreType.DMA((8,)),
                pltpu.SemaphoreType.DMA((8,)),
                pltpu.SemaphoreType.DMA((len(phases), most)),
                pltpu.SemaphoreType.DMA((len(phases), most)),
            ],
            compiler_params=pltpu.CompilerParams(
                collective_id=0, has_side_effects=True, vmem_limit_bytes=60 * 1024 * 1024
            ),
        )(
            positions, features, send_list.reshape(1, GHOST), edge_src.reshape(8, 128), edge_dst.reshape(8, 128),
            edge_count.reshape(1, 1), w_embed.T, w_env, jnp.swapaxes(w_update, 1, 2), w_out.reshape(1, C),
        )
        return forces, energy.reshape(())

    placed = (
        P(None, ("gx", "gy")), P(None, ("gx", "gy")), P(("gx", "gy")), P(("gx", "gy")), P(("gx", "gy")),
        P(("gx", "gy")), P(), P(), P(), P(),
    )
    return jax.shard_map(
        per_device, mesh=mesh, in_specs=placed, out_specs=(P(None, ("gx", "gy")), P()), check_vma=False
    )
```

```python
import math

import jax
import jax.numpy as jnp
from jax import lax
from jax.experimental import pallas as pl
from jax.experimental.pallas import tpu as pltpu
from jax.sharding import PartitionSpec as P

C = 64
NB = 8
LAYERS = 2
ATOMS = 64
GHOST = 32
EDGES = 1024
SCALE = 16 ** (-0.5)
OFFSETS = ((-1, -1), (-1, 0), (-1, 1), (0, -1), (0, 1), (1, -1), (1, 0), (1, 1))
WIDTH = 6.0
CUTOFF = 5.0
F32 = jnp.float32
BF16 = jnp.bfloat16
MESH = pl.DeviceIdType.MESH
TILE = 256
CUT, LIVE, UX, UY, UZ, INV, DIST, GAIN, BEND, SLOPE, DCUT = 0, 1, 2, 3, 4, 5, 6, 7, 8, 9, 10


def split(x):
    hi = x.astype(BF16)
    return hi, (x - hi.astype(F32)).astype(BF16)


def split3(x):
    hi = x.astype(BF16)
    rest = x - hi.astype(F32)
    mid = rest.astype(BF16)
    return hi, mid, (rest - mid.astype(F32)).astype(BF16)


def dot(x, y):
    return lax.dot_general(x, y, (((1,), (0,)), ((), ())), preferred_element_type=F32)


def dot_t(x, y):
    return lax.dot_general(x, y, (((1,), (1,)), ((), ())), preferred_element_type=F32)


def pick_lane(tables, index):
    lane = index & 127
    which = index >> 7
    result = None
    for t, table in enumerate(tables):
        wide = jnp.broadcast_to(table, (8, 128))
        got = jnp.take_along_axis(wide, lane, axis=1, mode="promise_in_bounds")
        result = got if result is None else jnp.where(which == t, got, result)
    return result


def phases_of(columns, rows):
    phases = []
    stride = 1
    while stride < columns:
        size = 4 if (columns // stride) % 4 == 0 else columns // stride
        phases.append(("gx", stride, size))
        stride *= size
    phases.append(("gy", 1, rows))
    return phases


def kernel(
    columns, rows, phases,
    pos_in, feat_in, send_in, src_in, dst_in, count_in, we_in, wv_in, wu_in, wo_in,
    forces_ref, energy_ref,
    pos_ref, feat_ref, send_ref, src_ref, dst_ref, count_ref, we_ref, wv_ref, wu_ref, wo_ref,
    pay, table, ah, al, oh, vh, vl, row, value, gain_cut, df, dradial_map, ddb, lhs, own_weights, flat, kept, folded,
    uth, utl, embs, gsrc, gbuf, ebuf,
    in_sem, send_sem, recv_sem, gsend_sem, grecv_sem, esend_sem, erecv_sem,
):
    a = lax.axis_index("gx")
    b = lax.axis_index("gy")

    def peer(k):
        dx, dy = OFFSETS[k]
        return (lax.rem(a + dx + columns, columns), b + dy)

    def when_valid(k, act, otherwise=None):
        dy = OFFSETS[k][1]
        if dy == 0:
            act()
            return
        good = (b > 0) if dy < 0 else (b < rows - 1)
        pl.when(good)(act)
        if otherwise is not None:
            pl.when(jnp.logical_not(good))(otherwise)

    def member(ph):
        axis, stride, size = phases[ph]
        index = a if axis == "gx" else b
        return lax.rem(index // stride, size)

    def energy_peer(ph, t):
        axis, stride, size = phases[ph]
        me = member(ph)
        step = (lax.rem(me + t, size) - me) * stride
        return (a + step, b) if axis == "gx" else (a, b + step)

    barrier = pltpu.get_barrier_semaphore()
    for k in range(8):
        when_valid(k, lambda k=k: pl.semaphore_signal(barrier, inc=1, device_id=peer(k), device_id_type=MESH))
    greeted = 0
    for ph in range(len(phases)):
        for t in range(1, phases[ph][2]):
            pl.semaphore_signal(barrier, inc=1, device_id=energy_peer(ph, t), device_id_type=MESH)
            greeted += 1

    fetched = [
        pltpu.make_async_copy(given, held, in_sem.at[i])
        for i, (given, held) in enumerate([
            (pos_in, pos_ref), (feat_in, feat_ref), (send_in, send_ref), (we_in, we_ref), (src_in, src_ref),
            (dst_in, dst_ref), (count_in, count_ref), (wv_in, wv_ref), (wu_in, wu_ref), (wo_in, wo_ref)])
    ]
    for copy in fetched:
        copy.start()
    for copy in fetched[0:4]:
        copy.wait()

    we_hi, we_lo = split(we_ref[:, 0 : 2 * C])
    we_both = jnp.concatenate(
        [jnp.concatenate([we_hi[:, 0:C], we_lo[:, 0:C]], axis=1),
         jnp.concatenate([we_hi[:, C : 2 * C], we_lo[:, C : 2 * C]], axis=1)], axis=0)
    feat = feat_ref[...]
    own = dot(we_both, jnp.concatenate([feat, feat], axis=0))
    own_src, own_dst = own[0:C], own[C : 2 * C]
    pos = pos_ref[...]
    send4 = jnp.concatenate([send_ref[...]] * 4, axis=1)
    st4 = (lax.broadcasted_iota(jnp.int32, (ATOMS, 128), 0) == send4).astype(F32).astype(BF16)
    exported = jnp.concatenate([own_src, pos, jnp.zeros((61, ATOMS), F32)], axis=0)
    e3 = split3(jnp.concatenate([exported, jnp.zeros((128, 128 - ATOMS), F32)], axis=1))
    st4_tall = jnp.concatenate([st4, jnp.zeros((128 - ATOMS, 128), BF16)], axis=0)
    payload = (dot(e3[2], st4_tall) + dot(e3[1], st4_tall)) + dot(e3[0], st4_tall)
    pay[...] = payload.T[0:GHOST, :]

    inner = jnp.logical_and(b > 0, b < rows - 1)
    pl.semaphore_wait(barrier, greeted + jnp.where(inner, 8, 5))

    def ghost_copy(k):
        return pltpu.make_async_remote_copy(
            src_ref=pay, dst_ref=table.at[7 - k], send_sem=send_sem.at[k], recv_sem=recv_sem.at[7 - k],
            device_id=peer(k), device_id_type=MESH,
        )

    for k in range(8):
        when_valid(k, lambda k=k: ghost_copy(k).start())
    for copy in fetched[4:]:
        copy.wait()

    def put_row(i, v):
        for j in range(8):
            row[i : i + 1, 128 * j : 128 * (j + 1)] = v[j : j + 1, :]

    def loop(count, act):
        for i in range(count):
            act(i)

    def tiles(act):
        loop(EDGES // TILE, lambda n: act(slice(n * TILE, (n + 1) * TILE)))

    src = src_ref[...]
    dst = dst_ref[...]
    block = (src - ATOMS) >> 5
    ghost = src >= ATOMS
    ox = jnp.zeros((8, 128), F32)
    oy = jnp.zeros((8, 128), F32)
    for k, (dx, dy) in enumerate(OFFSETS):
        here = jnp.logical_and(ghost, block == k)
        if dx:
            ox = jnp.where(here, WIDTH * dx, ox)
        if dy:
            oy = jnp.where(here, WIDTH * dy, oy)
    step_y = (oy * (1.0 / WIDTH)).astype(jnp.int32)
    reach = jnp.logical_and(b + step_y >= 0, b + step_y < rows)
    place = lax.broadcasted_iota(jnp.int32, (8, 128), 0) * 128 + lax.broadcasted_iota(jnp.int32, (8, 128), 1)
    live = jnp.where(jnp.logical_and(place < count_ref[...], reach), 1.0, 0.0)
    put_row(LIVE, live)
    slot = jnp.where(ghost, src - ATOMS, src + 8 * GHOST)
    def one_hot(j):
        lanes = slice(j * 128, (j + 1) * 128)
        oh[0:320, lanes] = (
            lax.broadcasted_iota(jnp.int32, (320, 128), 0) == slot[j : j + 1, :]).astype(F32).astype(BF16)
        hot = (lax.broadcasted_iota(jnp.int32, (ATOMS, 128), 0) == dst[j : j + 1, :]).astype(F32).astype(BF16)
        oh[320:384, lanes] = hot
        ah[512:576, lanes] = hot

    loop(8, one_hot)

    def four(x):
        hi, lo = split(x)
        return jnp.concatenate([hi, hi, lo, lo], axis=1)

    def weigh(layer):
        for i, d in enumerate((1, 2, 0)):
            env_hi, env_lo = split(wv_ref[layer, :, d * C : (d + 1) * C])
            upd = wu_ref[layer, :, (d + 1) * C : (d + 2) * C] * SCALE
            m = dot_t(four(upd), jnp.concatenate([env_hi, env_lo, env_hi, env_lo], axis=1))
            lhs[layer, 64 * i : 64 * (i + 1)] = four(m)
            lhs[3 - layer, 64 * i : 64 * (i + 1)] = four(m.T)
        own_w = wu_ref[layer, :, 0:C]
        for stage, x in ((layer, own_w), (3 - layer, own_w.T)):
            hi, lo = split(x)
            own_weights[stage] = jnp.concatenate([hi, hi, lo], axis=1)

    loop(LAYERS, weigh)
    wrt = we_ref[:, 2 * C : 2 * C + NB]
    wr = jnp.concatenate([wrt, jnp.zeros((C, 128 - NB), F32)], axis=1).T[0:NB, :]
    wr_low = wr - wr.astype(BF16).astype(F32)
    wr4 = jnp.concatenate([wr, wr, wr_low, jnp.zeros((104, C), F32)], axis=0).T.astype(BF16)
    wr2 = jnp.concatenate([wr, wr_low], axis=0)
    wr2 = jnp.concatenate([wr2, wr2], axis=1).astype(BF16)
    diagonal = lax.broadcasted_iota(jnp.int32, (C, C), 0) == lax.broadcasted_iota(jnp.int32, (C, C), 1)
    wo = jnp.sum(jnp.where(diagonal, wo_ref[...], 0.0), axis=1, keepdims=True)

    def blank(k):
        table[k] = jnp.zeros((GHOST, 128), F32)
        gbuf[k] = jnp.zeros((8, 128), F32)

    for k in range(8):
        when_valid(k, lambda k=k: ghost_copy(7 - k).wait_recv(), lambda k=k: blank(k))

    ghosts = jnp.concatenate([table[0:4].reshape(128, 128).T, table[4:8].reshape(128, 128).T], axis=1)
    own_pos = jnp.concatenate([pos, jnp.zeros((3, 64), F32)], axis=1)
    diff = []
    for i in range(3):
        at_ghost = ghosts[C + i : C + i + 1, :]
        mine = own_pos[i : i + 1, :]
        at_src = pick_lane([at_ghost[:, 0:128], at_ghost[:, 128:256], mine], slot)
        if i < 2:
            at_src = at_src + (ox, oy)[i]
        diff.append(at_src - pick_lane([mine], dst))
    dist = jnp.sqrt(diff[0] * diff[0] + diff[1] * diff[1] + diff[2] * diff[2] + 1.0)
    inv = 1.0 / dist
    ux, uy, uz = (v * inv for v in diff)
    root = math.sqrt(3.0)
    harm = [ux, uy, uz, root * ux * uy, root * uy * uz, 0.5 * (3.0 * uz * uz - 1.0), root * ux * uz,
            0.5 * root * (ux * ux - uy * uy)]
    short = jnp.maximum(1.0 - (dist * dist) * (1.0 / CUTOFF**2), 0.0)
    envelope = short * short
    gain = envelope * inv
    slope = (-4.0 / CUTOFF**2) * dist * short
    put_row(DIST, jnp.minimum(dist, CUTOFF) * (1.0 / CUTOFF))
    put_row(GAIN, gain)
    put_row(BEND, (slope - gain) * inv)
    put_row(CUT, live * envelope)
    put_row(SLOPE, live * slope)
    for i, v in ((UX, ux), (UY, uy), (UZ, uz), (INV, inv)):
        put_row(i, v)
    def map_edges(j):
        lanes = slice(j * 128, (j + 1) * 128)
        hot = ah[512:576, lanes]
        for m in range(8):
            high, low = split(jnp.broadcast_to(harm[m][j : j + 1, :], (16, 128)))
            ah[64 * m : 64 * (m + 1), lanes] = hot * jnp.concatenate([high] * 4, axis=0)
            al[64 * m : 64 * (m + 1), lanes] = hot * jnp.concatenate([low] * 4, axis=0)

    loop(8, map_edges)

    emb_hi, emb_lo = split(jnp.concatenate([ghosts[0:C, :], own_src, own_dst], axis=1))
    embs[...] = jnp.concatenate(
        [jnp.concatenate([emb_hi, wr4], axis=1), jnp.concatenate([emb_lo, jnp.zeros((C, 128), BF16)], axis=1)], axis=0)
    order = (lax.broadcasted_iota(jnp.int32, (NB, TILE), 0) + 1).astype(F32)

    def keep(lanes, place, x):
        hi, lo = split(x)
        vh[place : place + C, lanes] = hi
        vl[place : place + C, lanes] = lo
        ah[576:640, lanes] = hi
        ah[640:704, lanes] = lo
        ah[704:768, lanes] = hi

    def activate(lanes, stage, q):
        s = 1.0 / (1.0 + jnp.exp(-q))
        v = q * s
        cut = row[CUT : CUT + 1, lanes]
        value[stage, :, lanes] = v
        gain_cut[stage, :, lanes] = (s + v * (1.0 - s)) * cut
        return v * cut

    def embed(lanes):
        turns = order * row[DIST : DIST + 1, lanes]
        whole = jnp.floor(turns + 0.5)
        angle = (turns - whole) * math.pi
        sign = 1.0 - 2.0 * (whole - 2.0 * jnp.floor(whole * 0.5))
        sq = angle * angle
        sine = 1.0 / 39916800.0
        for c in (-1.0 / 362880.0, 1.0 / 5040.0, -1.0 / 120.0, 1.0 / 6.0, -1.0):
            sine = c + sq * sine
        sine = -(angle * sine) * sign
        cosine = 1.0 / 479001600.0
        for c in (-1.0 / 3628800.0, 1.0 / 40320.0, -1.0 / 720.0, 1.0 / 24.0, -0.5, 1.0):
            cosine = c + sq * cosine
        cosine = cosine * sign
        near = row[GAIN : GAIN + 1, lanes]
        radial = sine * near
        dradial_map[:, lanes] = order * (math.pi / CUTOFF) * cosine * near + sine * row[BEND : BEND + 1, lanes]
        low = radial - radial.astype(BF16).astype(F32)
        oh[384:512, lanes] = jnp.concatenate([radial, low, radial, jnp.zeros((104, TILE), F32)], axis=0).astype(BF16)
        both = dot(embs[...], oh[:, lanes])
        f = activate(lanes, 0, both[0:C] + both[C : 2 * C])
        df[:, lanes] = f
        keep(lanes, 192, f)

    degree = lax.broadcasted_iota(jnp.int32, (C, 512), 1) >= 192

    def mix(stage, place):
        sums = dot_t(ah[576:704, :], ah[0:576, :])
        sums = sums[0:C] + sums[C : 2 * C]
        hi, lo = split(sums[:, 0:512] + dot_t(ah[576:640, :], al[...]))
        every = dot(lhs[stage, 0:128], jnp.concatenate([hi, lo, hi, lo], axis=0))
        outer = jnp.where(degree, every[C : 2 * C], every[0:C])
        kept[place : place + C, :] = outer
        hi, lo = split(sums[:, 512:576])
        inner = dot(lhs[stage, 128:192], jnp.concatenate([hi, lo, hi, lo], axis=0))
        hi, lo = split(outer)
        flat[0:C, 0:512] = hi
        flat[C : 2 * C, 0:512] = lo
        hi, lo = split(inner)
        flat[0:C, 512:768] = jnp.concatenate([hi, own_weights[stage]], axis=1)
        flat[C : 2 * C, 512:768] = jnp.concatenate([lo, jnp.zeros((C, 192), BF16)], axis=1)

    def spread(lanes):
        both = dot(flat[...], ah[:, lanes])
        return both[0:C] + both[C : 2 * C] + dot(flat[0:C, 0:512], al[:, lanes])

    def back_map(place):
        hi, lo = split(kept[place : place + 128, :].T)
        uth[:, place : place + 128] = hi
        utl[:, place : place + 128] = lo

    def energy_copy(ph, t):
        me = member(ph)
        return pltpu.make_async_remote_copy(
            src_ref=ebuf.at[ph, me], dst_ref=ebuf.at[ph, me], send_sem=esend_sem.at[ph, t],
            recv_sem=erecv_sem.at[ph, t], device_id=energy_peer(ph, t), device_id_type=MESH,
        )

    def energy_out(ph, x):
        ebuf[ph, member(ph)] = x
        for t in range(1, phases[ph][2]):
            energy_copy(ph, t).start()

    def energy_in(ph):
        size = phases[ph][2]
        for t in range(1, size):
            came = lax.rem(member(ph) + size - t, size)
            pltpu.make_async_remote_copy(
                src_ref=ebuf.at[ph, came], dst_ref=ebuf.at[ph, came], send_sem=esend_sem.at[ph, t],
                recv_sem=erecv_sem.at[ph, t], device_id=energy_peer(ph, t), device_id_type=MESH,
            ).wait_recv()
        total = ebuf[ph, 0]
        for t in range(1, size):
            total = total + ebuf[ph, t]
        return total

    last = len(phases) - 1

    tiles(embed)

    def first_layer(lanes):
        f = df[:, lanes] + activate(lanes, 1, spread(lanes))
        df[:, lanes] = f
        keep(lanes, 64, f)

    folded[...] = jnp.zeros((8, TILE), F32)

    def turn(lanes):
        q = spread(lanes)
        s = 1.0 / (1.0 + jnp.exp(-q))
        v = q * s
        cut = row[CUT : CUT + 1, lanes]
        f = df[:, lanes] + v * cut
        g = wo * row[LIVE : LIVE + 1, lanes]
        per_edge = f * g
        piece = per_edge[0:8]
        for i in range(1, 8):
            piece = piece + per_edge[8 * i : 8 * i + 8]
        folded[...] += piece
        df[:, lanes] = g
        row[DCUT : DCUT + 1, lanes] = jnp.sum(g * v, axis=0, keepdims=True)
        keep(lanes, 0, g * ((s + v * (1.0 - s)) * cut))

    def back_first(lanes):
        g = df[:, lanes] + spread(lanes)
        df[:, lanes] = g
        row[DCUT : DCUT + 1, lanes] += jnp.sum(g * value[1, :, lanes], axis=0, keepdims=True)
        keep(lanes, 128, g * gain_cut[1, :, lanes])

    mix(0, 128)
    tiles(first_layer)
    mix(1, 0)
    tiles(turn)
    energy_out(0, folded[:, 0:128] + folded[:, 128:256])
    mix(2, 64)
    tiles(back_first)
    for ph in range(0, min(1, last)):
        energy_out(ph + 1, energy_in(ph))
    back_map(0)
    mix(3, 192)
    for ph in range(1, min(2, last)):
        energy_out(ph + 1, energy_in(ph))
    back_map(128)

    def back_embed(lanes):
        g = df[:, lanes] + spread(lanes)
        dcut = row[DCUT : DCUT + 1, lanes] + jnp.sum(g * value[0, :, lanes], axis=0, keepdims=True)
        both = dot(wr2, jnp.concatenate(split(g * gain_cut[0, :, lanes]), axis=0))
        dr = jnp.sum((both[0:8] + both[8:16]) * dradial_map[:, lanes], axis=0, keepdims=True)
        dr = dr + dcut * row[SLOPE : SLOPE + 1, lanes]
        right = vh[:, lanes]
        part = dot(uth[...], right) + dot(utl[...], right) + dot(uth[...], vl[:, lanes])
        hot = ah[512:576, lanes].astype(F32)
        g = [jnp.sum(hot * part[64 * m : 64 * (m + 1)], axis=0, keepdims=True) for m in range(8)]
        xr, yr, zr, ir = (row[i : i + 1, lanes] for i in (UX, UY, UZ, INV))
        dux = g[0] + root * (g[3] * yr + g[6] * zr + g[7] * xr)
        duy = g[1] + root * (g[3] * xr + g[4] * zr - g[7] * yr)
        duz = g[2] + root * (g[4] * yr + g[6] * xr) + 3.0 * g[5] * zr
        along = dr - (dux * xr + duy * yr + duz * zr) * ir
        dd = jnp.concatenate(
            [dux * ir + along * xr, duy * ir + along * yr, duz * ir + along * zr, jnp.zeros((5, TILE), F32)], axis=0)
        ddb[:, lanes] = jnp.concatenate([dd, dd - dd.astype(BF16).astype(F32)], axis=0).astype(BF16)

    tiles(back_embed)
    for ph in range(2, last):
        energy_out(ph + 1, energy_in(ph))
    scattered = dot_t(ddb[...], oh[0:384, :])
    scattered = scattered[0:8] + scattered[8:16]
    gsrc[0] = scattered[:, 0:128]
    gsrc[1] = scattered[:, 128:256]
    def force_copy(k):
        return pltpu.make_async_remote_copy(
            src_ref=gsrc.at[k // 4], dst_ref=gbuf.at[7 - k], send_sem=gsend_sem.at[k], recv_sem=grecv_sem.at[7 - k],
            device_id=peer(k), device_id_type=MESH,
        )

    for k in range(8):
        when_valid(k, lambda k=k: force_copy(k).start())
    at_own = scattered[:, 256:320] - scattered[:, 320:384]
    for k in range(8):
        when_valid(k, lambda k=k: force_copy(7 - k).wait_recv())
    group = lax.broadcasted_iota(jnp.int32, (8, 128), 1) >> 5
    acc = jnp.zeros((8, 128), F32)
    for k in range(8):
        acc = acc + jnp.where(group == (7 - k) % 4, gbuf[k], 0.0)
    acc_low = acc - acc.astype(BF16).astype(F32)
    returned = dot_t(jnp.concatenate([acc, acc_low], axis=0).astype(BF16), st4)
    returned = returned[0:8] + returned[8:16]
    forces_ref[...] = -(at_own + returned)[0:3, :]

    total = energy_in(last)
    energy_ref[...] = jnp.sum(jnp.sum(total, axis=0, keepdims=True), axis=1, keepdims=True)

    for k in range(8):
        when_valid(k, lambda k=k: (ghost_copy(k).wait_send(), force_copy(k).wait_send())[0])
    for ph in range(len(phases)):
        for t in range(1, phases[ph][2]):
            energy_copy(ph, t).wait_send()


def solution(mesh):
    columns, rows = mesh.shape["gx"], mesh.shape["gy"]
    phases = phases_of(columns, rows)
    most = max(size for _, _, size in phases)

    def per_device(positions, features, send_list, edge_src, edge_dst, edge_count, w_embed, w_env, w_update, w_out):
        def body(*refs):
            kernel(columns, rows, phases, *refs)

        vmem = pl.BlockSpec(memory_space=pltpu.VMEM)
        anywhere = pl.BlockSpec(memory_space=pl.ANY)
        forces, energy = pl.pallas_call(
            body,
            out_shape=(jax.ShapeDtypeStruct((3, ATOMS), F32), jax.ShapeDtypeStruct((1, 1), F32)),
            in_specs=[anywhere] * 10,
            out_specs=(vmem, vmem),
            scratch_shapes=[
                pltpu.VMEM((3, ATOMS), F32),
                pltpu.VMEM((C, ATOMS), BF16),
                pltpu.VMEM((1, GHOST), jnp.int32),
                pltpu.VMEM((8, 128), jnp.int32),
                pltpu.VMEM((8, 128), jnp.int32),
                pltpu.VMEM((1, 1), jnp.int32),
                pltpu.VMEM((C, 2 * C + NB), F32),
                pltpu.VMEM((LAYERS, C, 3 * C), F32),
                pltpu.VMEM((LAYERS, C, 4 * C), F32),
                pltpu.VMEM((1, C), F32),
                pltpu.VMEM((GHOST, 128), F32),
                pltpu.VMEM((8, GHOST, 128), F32),
                pltpu.VMEM((768, EDGES), BF16),
                pltpu.VMEM((512, EDGES), BF16),
                pltpu.VMEM((512, EDGES), BF16),
                pltpu.VMEM((256, EDGES), BF16),
                pltpu.VMEM((256, EDGES), BF16),
                pltpu.VMEM((16, EDGES), F32),
                pltpu.VMEM((2, C, EDGES), F32),
                pltpu.VMEM((2, C, EDGES), F32),
                pltpu.VMEM((C, EDGES), F32),
                pltpu.VMEM((NB, EDGES), F32),
                pltpu.VMEM((16, EDGES), BF16),
                pltpu.VMEM((2 * LAYERS, 192, 256), BF16),
                pltpu.VMEM((2 * LAYERS, C, 192), BF16),
                pltpu.VMEM((128, 768), BF16),
                pltpu.VMEM((256, 512), F32),
                pltpu.VMEM((8, TILE), F32),
                pltpu.VMEM((512, 256), BF16),
                pltpu.VMEM((512, 256), BF16),
                pltpu.VMEM((128, 512), BF16),
                pltpu.VMEM((2, 8, 128), F32),
                pltpu.VMEM((8, 8, 128), F32),
                pltpu.VMEM((len(phases), most, 8, 128), F32),
                pltpu.SemaphoreType.DMA((10,)),
                pltpu.SemaphoreType.DMA((8,)),
                pltpu.SemaphoreType.DMA((8,)),
                pltpu.SemaphoreType.DMA((8,)),
                pltpu.SemaphoreType.DMA((8,)),
                pltpu.SemaphoreType.DMA((len(phases), most)),
                pltpu.SemaphoreType.DMA((len(phases), most)),
            ],
            compiler_params=pltpu.CompilerParams(
                collective_id=0, has_side_effects=True, vmem_limit_bytes=60 * 1024 * 1024
            ),
        )(
            positions, features, send_list.reshape(1, GHOST), edge_src.reshape(8, 128), edge_dst.reshape(8, 128),
            edge_count.reshape(1, 1), w_embed.T, w_env, jnp.swapaxes(w_update, 1, 2), w_out.reshape(1, C),
        )
        return forces, energy.reshape(())

    placed = (
        P(None, ("gx", "gy")), P(None, ("gx", "gy")), P(("gx", "gy")), P(("gx", "gy")), P(("gx", "gy")),
        P(("gx", "gy")), P(), P(), P(), P(),
    )
    return jax.shard_map(
        per_device, mesh=mesh, in_specs=placed, out_specs=(P(None, ("gx", "gy")), P()), check_vma=False
    )
```

```python
import math

import jax
import jax.numpy as jnp
from jax import lax
from jax.experimental import pallas as pl
from jax.experimental.pallas import tpu as pltpu
from jax.sharding import PartitionSpec as P

C = 64
NB = 8
LAYERS = 2
ATOMS = 64
GHOST = 32
EDGES = 1024
SCALE = 16 ** (-0.5)
OFFSETS = ((-1, -1), (-1, 0), (-1, 1), (0, -1), (0, 1), (1, -1), (1, 0), (1, 1))
WIDTH = 6.0
CUTOFF = 5.0
F32 = jnp.float32
BF16 = jnp.bfloat16
MESH = pl.DeviceIdType.MESH
TILE = 256
CUT, LIVE, UX, UY, UZ, INV, DIST, GAIN, BEND, SLOPE, DCUT = 0, 1, 2, 3, 4, 5, 6, 7, 8, 9, 10


def split(x):
    hi = x.astype(BF16)
    return hi, (x - hi.astype(F32)).astype(BF16)


def split3(x):
    hi = x.astype(BF16)
    rest = x - hi.astype(F32)
    mid = rest.astype(BF16)
    return hi, mid, (rest - mid.astype(F32)).astype(BF16)


def dot(x, y):
    return lax.dot_general(x, y, (((1,), (0,)), ((), ())), preferred_element_type=F32)


def dot_t(x, y):
    return lax.dot_general(x, y, (((1,), (1,)), ((), ())), preferred_element_type=F32)


def pick_lane(tables, index):
    lane = index & 127
    which = index >> 7
    result = None
    for t, table in enumerate(tables):
        wide = jnp.broadcast_to(table, (8, 128))
        got = jnp.take_along_axis(wide, lane, axis=1, mode="promise_in_bounds")
        result = got if result is None else jnp.where(which == t, got, result)
    return result


def sizes_of(columns, rows):
    return (4 * rows, columns // 4)


def kernel(
    columns, rows, sizes,
    pos_in, feat_in, send_in, src_in, dst_in, count_in, we_in, wv_in, wu_in, wo_in,
    forces_ref, energy_ref,
    pos_ref, feat_ref, send_ref, src_ref, dst_ref, count_ref, we_ref, wv_ref, wu_ref, wo_ref,
    pay, table, ah, al, oh, vh, vl, row, value, gain_cut, df, dradial_map, ddb, lhs, own_weights, flat, kept, folded,
    uth, utl, embs, gsrc, gbuf, ebuf,
    in_sem, send_sem, recv_sem, gsend_sem, grecv_sem, esend_sem, erecv_sem,
):
    a = lax.axis_index("gx")
    b = lax.axis_index("gy")

    def peer(k):
        dx, dy = OFFSETS[k]
        return (lax.rem(a + dx + columns, columns), b + dy)

    def when_valid(k, act, otherwise=None):
        dy = OFFSETS[k][1]
        if dy == 0:
            act()
            return
        good = (b > 0) if dy < 0 else (b < rows - 1)
        pl.when(good)(act)
        if otherwise is not None:
            pl.when(jnp.logical_not(good))(otherwise)

    def member(ph):
        return lax.rem(a, 4) * rows + b if ph == 0 else a // 4

    def energy_peer(ph, t):
        other = lax.rem(member(ph) + t, sizes[ph])
        if ph == 0:
            return (a - lax.rem(a, 4) + other // rows, lax.rem(other, rows))
        return (lax.rem(a, 4) + 4 * other, b)

    barrier = pltpu.get_barrier_semaphore()
    for k in range(8):
        when_valid(k, lambda k=k: pl.semaphore_signal(barrier, inc=1, device_id=peer(k), device_id_type=MESH))
    greeted = 0
    for ph in range(2):
        for t in range(1, sizes[ph]):
            pl.semaphore_signal(barrier, inc=1, device_id=energy_peer(ph, t), device_id_type=MESH)
            greeted += 1

    fetched = [
        pltpu.make_async_copy(given, held, in_sem.at[i])
        for i, (given, held) in enumerate([
            (pos_in, pos_ref), (feat_in, feat_ref), (send_in, send_ref), (we_in, we_ref), (src_in, src_ref),
            (dst_in, dst_ref), (count_in, count_ref), (wv_in, wv_ref), (wu_in, wu_ref), (wo_in, wo_ref)])
    ]
    for copy in fetched:
        copy.start()
    for copy in fetched[0:4]:
        copy.wait()

    we_hi, we_lo = split(we_ref[:, 0 : 2 * C])
    we_both = jnp.concatenate(
        [jnp.concatenate([we_hi[:, 0:C], we_lo[:, 0:C]], axis=1),
         jnp.concatenate([we_hi[:, C : 2 * C], we_lo[:, C : 2 * C]], axis=1)], axis=0)
    feat = feat_ref[...]
    own = dot(we_both, jnp.concatenate([feat, feat], axis=0))
    own_src, own_dst = own[0:C], own[C : 2 * C]
    pos = pos_ref[...]
    send4 = jnp.concatenate([send_ref[...]] * 4, axis=1)
    st4 = (lax.broadcasted_iota(jnp.int32, (ATOMS, 128), 0) == send4).astype(F32).astype(BF16)
    exported = jnp.concatenate([own_src, pos, jnp.zeros((61, ATOMS), F32)], axis=0)
    e3 = split3(jnp.concatenate([exported, jnp.zeros((128, 128 - ATOMS), F32)], axis=1))
    st4_tall = jnp.concatenate([st4, jnp.zeros((128 - ATOMS, 128), BF16)], axis=0)
    payload = (dot(e3[2], st4_tall) + dot(e3[1], st4_tall)) + dot(e3[0], st4_tall)
    pay[...] = payload.T[0:GHOST, :]

    inner = jnp.logical_and(b > 0, b < rows - 1)
    pl.semaphore_wait(barrier, greeted + jnp.where(inner, 8, 5))

    def ghost_copy(k):
        return pltpu.make_async_remote_copy(
            src_ref=pay, dst_ref=table.at[7 - k], send_sem=send_sem.at[k], recv_sem=recv_sem.at[7 - k],
            device_id=peer(k), device_id_type=MESH,
        )

    for k in range(8):
        when_valid(k, lambda k=k: ghost_copy(k).start())
    for copy in fetched[4:]:
        copy.wait()

    def put_row(i, v):
        for j in range(8):
            row[i : i + 1, 128 * j : 128 * (j + 1)] = v[j : j + 1, :]

    def loop(count, act):
        for i in range(count):
            act(i)

    def tiles(act):
        loop(EDGES // TILE, lambda n: act(slice(n * TILE, (n + 1) * TILE)))

    src = src_ref[...]
    dst = dst_ref[...]
    block = (src - ATOMS) >> 5
    ghost = src >= ATOMS
    ox = jnp.zeros((8, 128), F32)
    oy = jnp.zeros((8, 128), F32)
    for k, (dx, dy) in enumerate(OFFSETS):
        here = jnp.logical_and(ghost, block == k)
        if dx:
            ox = jnp.where(here, WIDTH * dx, ox)
        if dy:
            oy = jnp.where(here, WIDTH * dy, oy)
    step_y = (oy * (1.0 / WIDTH)).astype(jnp.int32)
    reach = jnp.logical_and(b + step_y >= 0, b + step_y < rows)
    place = lax.broadcasted_iota(jnp.int32, (8, 128), 0) * 128 + lax.broadcasted_iota(jnp.int32, (8, 128), 1)
    live = jnp.where(jnp.logical_and(place < count_ref[...], reach), 1.0, 0.0)
    put_row(LIVE, live)
    slot = jnp.where(ghost, src - ATOMS, src + 8 * GHOST)
    def one_hot(j):
        lanes = slice(j * 128, (j + 1) * 128)
        oh[0:320, lanes] = (
            lax.broadcasted_iota(jnp.int32, (320, 128), 0) == slot[j : j + 1, :]).astype(F32).astype(BF16)
        hot = (lax.broadcasted_iota(jnp.int32, (ATOMS, 128), 0) == dst[j : j + 1, :]).astype(F32).astype(BF16)
        oh[320:384, lanes] = hot
        ah[512:576, lanes] = hot

    loop(8, one_hot)

    def four(x):
        hi, lo = split(x)
        return jnp.concatenate([hi, hi, lo, lo], axis=1)

    def weigh(layer):
        for i, d in enumerate((1, 2, 0)):
            env_hi, env_lo = split(wv_ref[layer, :, d * C : (d + 1) * C])
            upd = wu_ref[layer, :, (d + 1) * C : (d + 2) * C] * SCALE
            m = dot_t(four(upd), jnp.concatenate([env_hi, env_lo, env_hi, env_lo], axis=1))
            lhs[layer, 64 * i : 64 * (i + 1)] = four(m)
            lhs[3 - layer, 64 * i : 64 * (i + 1)] = four(m.T)
        own_w = wu_ref[layer, :, 0:C]
        for stage, x in ((layer, own_w), (3 - layer, own_w.T)):
            hi, lo = split(x)
            own_weights[stage] = jnp.concatenate([hi, hi, lo], axis=1)

    loop(LAYERS, weigh)
    wrt = we_ref[:, 2 * C : 2 * C + NB]
    wr = jnp.concatenate([wrt, jnp.zeros((C, 128 - NB), F32)], axis=1).T[0:NB, :]
    wr_low = wr - wr.astype(BF16).astype(F32)
    wr4 = jnp.concatenate([wr, wr, wr_low, jnp.zeros((104, C), F32)], axis=0).T.astype(BF16)
    wr2 = jnp.concatenate([wr, wr_low], axis=0)
    wr2 = jnp.concatenate([wr2, wr2], axis=1).astype(BF16)
    diagonal = lax.broadcasted_iota(jnp.int32, (C, C), 0) == lax.broadcasted_iota(jnp.int32, (C, C), 1)
    wo = jnp.sum(jnp.where(diagonal, wo_ref[...], 0.0), axis=1, keepdims=True)

    def blank(k):
        table[k] = jnp.zeros((GHOST, 128), F32)
        gbuf[k] = jnp.zeros((8, 128), F32)

    for k in range(8):
        when_valid(k, lambda k=k: ghost_copy(7 - k).wait_recv(), lambda k=k: blank(k))

    ghosts = jnp.concatenate([table[0:4].reshape(128, 128).T, table[4:8].reshape(128, 128).T], axis=1)
    own_pos = jnp.concatenate([pos, jnp.zeros((3, 64), F32)], axis=1)
    diff = []
    for i in range(3):
        at_ghost = ghosts[C + i : C + i + 1, :]
        mine = own_pos[i : i + 1, :]
        at_src = pick_lane([at_ghost[:, 0:128], at_ghost[:, 128:256], mine], slot)
        if i < 2:
            at_src = at_src + (ox, oy)[i]
        diff.append(at_src - pick_lane([mine], dst))
    dist = jnp.sqrt(diff[0] * diff[0] + diff[1] * diff[1] + diff[2] * diff[2] + 1.0)
    inv = 1.0 / dist
    ux, uy, uz = (v * inv for v in diff)
    root = math.sqrt(3.0)
    harm = [ux, uy, uz, root * ux * uy, root * uy * uz, 0.5 * (3.0 * uz * uz - 1.0), root * ux * uz,
            0.5 * root * (ux * ux - uy * uy)]
    short = jnp.maximum(1.0 - (dist * dist) * (1.0 / CUTOFF**2), 0.0)
    envelope = short * short
    gain = envelope * inv
    slope = (-4.0 / CUTOFF**2) * dist * short
    put_row(DIST, jnp.minimum(dist, CUTOFF) * (1.0 / CUTOFF))
    put_row(GAIN, gain)
    put_row(BEND, (slope - gain) * inv)
    put_row(CUT, live * envelope)
    put_row(SLOPE, live * slope)
    for i, v in ((UX, ux), (UY, uy), (UZ, uz), (INV, inv)):
        put_row(i, v)
    def map_edges(j):
        lanes = slice(j * 128, (j + 1) * 128)
        hot = ah[512:576, lanes]
        for m in range(8):
            high, low = split(jnp.broadcast_to(harm[m][j : j + 1, :], (16, 128)))
            ah[64 * m : 64 * (m + 1), lanes] = hot * jnp.concatenate([high] * 4, axis=0)
            al[64 * m : 64 * (m + 1), lanes] = hot * jnp.concatenate([low] * 4, axis=0)

    loop(8, map_edges)

    emb_hi, emb_lo = split(jnp.concatenate([ghosts[0:C, :], own_src, own_dst], axis=1))
    embs[...] = jnp.concatenate(
        [jnp.concatenate([emb_hi, wr4], axis=1), jnp.concatenate([emb_lo, jnp.zeros((C, 128), BF16)], axis=1)], axis=0)
    order = (lax.broadcasted_iota(jnp.int32, (NB, TILE), 0) + 1).astype(F32)

    def keep(lanes, place, x):
        hi, lo = split(x)
        vh[place : place + C, lanes] = hi
        vl[place : place + C, lanes] = lo
        ah[576:640, lanes] = hi
        ah[640:704, lanes] = lo
        ah[704:768, lanes] = hi

    def activate(lanes, stage, q):
        s = 1.0 / (1.0 + jnp.exp(-q))
        v = q * s
        cut = row[CUT : CUT + 1, lanes]
        value[stage, :, lanes] = v
        gain_cut[stage, :, lanes] = (s + v * (1.0 - s)) * cut
        return v * cut

    def embed(lanes):
        turns = order * row[DIST : DIST + 1, lanes]
        whole = jnp.floor(turns + 0.5)
        angle = (turns - whole) * math.pi
        sign = 1.0 - 2.0 * (whole - 2.0 * jnp.floor(whole * 0.5))
        sq = angle * angle
        sine = 1.0 / 39916800.0
        for c in (-1.0 / 362880.0, 1.0 / 5040.0, -1.0 / 120.0, 1.0 / 6.0, -1.0):
            sine = c + sq * sine
        sine = -(angle * sine) * sign
        cosine = 1.0 / 479001600.0
        for c in (-1.0 / 3628800.0, 1.0 / 40320.0, -1.0 / 720.0, 1.0 / 24.0, -0.5, 1.0):
            cosine = c + sq * cosine
        cosine = cosine * sign
        near = row[GAIN : GAIN + 1, lanes]
        radial = sine * near
        dradial_map[:, lanes] = order * (math.pi / CUTOFF) * cosine * near + sine * row[BEND : BEND + 1, lanes]
        low = radial - radial.astype(BF16).astype(F32)
        oh[384:512, lanes] = jnp.concatenate([radial, low, radial, jnp.zeros((104, TILE), F32)], axis=0).astype(BF16)
        both = dot(embs[...], oh[:, lanes])
        f = activate(lanes, 0, both[0:C] + both[C : 2 * C])
        df[:, lanes] = f
        keep(lanes, 192, f)

    degree = lax.broadcasted_iota(jnp.int32, (C, 512), 1) >= 192

    def mix(stage, place):
        sums = dot_t(ah[576:704, :], ah[0:576, :])
        sums = sums[0:C] + sums[C : 2 * C]
        hi, lo = split(sums[:, 0:512] + dot_t(ah[576:640, :], al[...]))
        every = dot(lhs[stage, 0:128], jnp.concatenate([hi, lo, hi, lo], axis=0))
        outer = jnp.where(degree, every[C : 2 * C], every[0:C])
        kept[place : place + C, :] = outer
        hi, lo = split(sums[:, 512:576])
        inner = dot(lhs[stage, 128:192], jnp.concatenate([hi, lo, hi, lo], axis=0))
        hi, lo = split(outer)
        flat[0:C, 0:512] = hi
        flat[C : 2 * C, 0:512] = lo
        hi, lo = split(inner)
        flat[0:C, 512:768] = jnp.concatenate([hi, own_weights[stage]], axis=1)
        flat[C : 2 * C, 512:768] = jnp.concatenate([lo, jnp.zeros((C, 192), BF16)], axis=1)

    def spread(lanes):
        both = dot(flat[...], ah[:, lanes])
        return both[0:C] + both[C : 2 * C] + dot(flat[0:C, 0:512], al[:, lanes])

    def back_map(place):
        hi, lo = split(kept[place : place + 128, :].T)
        uth[:, place : place + 128] = hi
        utl[:, place : place + 128] = lo

    def energy_copy(ph, t):
        me = member(ph)
        return pltpu.make_async_remote_copy(
            src_ref=ebuf.at[ph, me], dst_ref=ebuf.at[ph, me], send_sem=esend_sem.at[ph, t],
            recv_sem=erecv_sem.at[ph, t], device_id=energy_peer(ph, t), device_id_type=MESH,
        )

    def energy_out(ph, x):
        ebuf[ph, member(ph)] = x
        for t in range(1, sizes[ph]):
            energy_copy(ph, t).start()

    def energy_in(ph):
        size = sizes[ph]
        for t in range(1, size):
            came = lax.rem(member(ph) + size - t, size)
            pltpu.make_async_remote_copy(
                src_ref=ebuf.at[ph, came], dst_ref=ebuf.at[ph, came], send_sem=esend_sem.at[ph, t],
                recv_sem=erecv_sem.at[ph, t], device_id=energy_peer(ph, t), device_id_type=MESH,
            ).wait_recv()
        total = ebuf[ph, 0]
        for t in range(1, size):
            total = total + ebuf[ph, t]
        return total

    tiles(embed)

    def first_layer(lanes):
        f = df[:, lanes] + activate(lanes, 1, spread(lanes))
        df[:, lanes] = f
        keep(lanes, 64, f)

    folded[...] = jnp.zeros((8, TILE), F32)

    def turn(lanes):
        q = spread(lanes)
        s = 1.0 / (1.0 + jnp.exp(-q))
        v = q * s
        cut = row[CUT : CUT + 1, lanes]
        f = df[:, lanes] + v * cut
        g = wo * row[LIVE : LIVE + 1, lanes]
        per_edge = f * g
        piece = per_edge[0:8]
        for i in range(1, 8):
            piece = piece + per_edge[8 * i : 8 * i + 8]
        folded[...] += piece
        df[:, lanes] = g
        row[DCUT : DCUT + 1, lanes] = jnp.sum(g * v, axis=0, keepdims=True)
        keep(lanes, 0, g * ((s + v * (1.0 - s)) * cut))

    def back_first(lanes):
        g = df[:, lanes] + spread(lanes)
        df[:, lanes] = g
        row[DCUT : DCUT + 1, lanes] += jnp.sum(g * value[1, :, lanes], axis=0, keepdims=True)
        keep(lanes, 128, g * gain_cut[1, :, lanes])

    mix(0, 128)
    tiles(first_layer)
    mix(1, 0)
    tiles(turn)
    energy_out(0, folded[:, 0:128] + folded[:, 128:256])
    mix(2, 64)
    tiles(back_first)
    back_map(0)
    mix(3, 192)
    back_map(128)
    energy_out(1, energy_in(0))

    def back_embed(lanes):
        g = df[:, lanes] + spread(lanes)
        dcut = row[DCUT : DCUT + 1, lanes] + jnp.sum(g * value[0, :, lanes], axis=0, keepdims=True)
        both = dot(wr2, jnp.concatenate(split(g * gain_cut[0, :, lanes]), axis=0))
        dr = jnp.sum((both[0:8] + both[8:16]) * dradial_map[:, lanes], axis=0, keepdims=True)
        dr = dr + dcut * row[SLOPE : SLOPE + 1, lanes]
        right = vh[:, lanes]
        part = dot(uth[...], right) + dot(utl[...], right) + dot(uth[...], vl[:, lanes])
        hot = ah[512:576, lanes].astype(F32)
        g = [jnp.sum(hot * part[64 * m : 64 * (m + 1)], axis=0, keepdims=True) for m in range(8)]
        xr, yr, zr, ir = (row[i : i + 1, lanes] for i in (UX, UY, UZ, INV))
        dux = g[0] + root * (g[3] * yr + g[6] * zr + g[7] * xr)
        duy = g[1] + root * (g[3] * xr + g[4] * zr - g[7] * yr)
        duz = g[2] + root * (g[4] * yr + g[6] * xr) + 3.0 * g[5] * zr
        along = dr - (dux * xr + duy * yr + duz * zr) * ir
        dd = jnp.concatenate(
            [dux * ir + along * xr, duy * ir + along * yr, duz * ir + along * zr, jnp.zeros((5, TILE), F32)], axis=0)
        ddb[:, lanes] = jnp.concatenate([dd, dd - dd.astype(BF16).astype(F32)], axis=0).astype(BF16)

    tiles(back_embed)
    scattered = dot_t(ddb[...], oh[0:384, :])
    scattered = scattered[0:8] + scattered[8:16]
    gsrc[0] = scattered[:, 0:128]
    gsrc[1] = scattered[:, 128:256]
    def force_copy(k):
        return pltpu.make_async_remote_copy(
            src_ref=gsrc.at[k // 4], dst_ref=gbuf.at[7 - k], send_sem=gsend_sem.at[k], recv_sem=grecv_sem.at[7 - k],
            device_id=peer(k), device_id_type=MESH,
        )

    for k in range(8):
        when_valid(k, lambda k=k: force_copy(k).start())
    at_own = scattered[:, 256:320] - scattered[:, 320:384]
    for k in range(8):
        when_valid(k, lambda k=k: force_copy(7 - k).wait_recv())
    group = lax.broadcasted_iota(jnp.int32, (8, 128), 1) >> 5
    acc = jnp.zeros((8, 128), F32)
    for k in range(8):
        acc = acc + jnp.where(group == (7 - k) % 4, gbuf[k], 0.0)
    acc_low = acc - acc.astype(BF16).astype(F32)
    returned = dot_t(jnp.concatenate([acc, acc_low], axis=0).astype(BF16), st4)
    returned = returned[0:8] + returned[8:16]
    forces_ref[...] = -(at_own + returned)

    total = energy_in(1)
    energy_ref[...] = jnp.sum(jnp.sum(total, axis=0, keepdims=True), axis=1, keepdims=True)

    for k in range(8):
        when_valid(k, lambda k=k: (ghost_copy(k).wait_send(), force_copy(k).wait_send())[0])
    for ph in range(2):
        for t in range(1, sizes[ph]):
            energy_copy(ph, t).wait_send()


def solution(mesh):
    columns, rows = mesh.shape["gx"], mesh.shape["gy"]
    sizes = sizes_of(columns, rows)
    most = max(sizes)

    def per_device(positions, features, send_list, edge_src, edge_dst, edge_count, w_embed, w_env, w_update, w_out):
        def body(*refs):
            kernel(columns, rows, sizes, *refs)

        vmem = pl.BlockSpec(memory_space=pltpu.VMEM)
        anywhere = pl.BlockSpec(memory_space=pl.ANY)
        forces, energy = pl.pallas_call(
            body,
            out_shape=(jax.ShapeDtypeStruct((8, ATOMS), F32), jax.ShapeDtypeStruct((1, 1), F32)),
            in_specs=[anywhere] * 10,
            out_specs=(vmem, vmem),
            scratch_shapes=[
                pltpu.VMEM((3, ATOMS), F32),
                pltpu.VMEM((C, ATOMS), BF16),
                pltpu.VMEM((1, GHOST), jnp.int32),
                pltpu.VMEM((8, 128), jnp.int32),
                pltpu.VMEM((8, 128), jnp.int32),
                pltpu.VMEM((1, 1), jnp.int32),
                pltpu.VMEM((C, 2 * C + NB), F32),
                pltpu.VMEM((LAYERS, C, 3 * C), F32),
                pltpu.VMEM((LAYERS, C, 4 * C), F32),
                pltpu.VMEM((1, C), F32),
                pltpu.VMEM((GHOST, 128), F32),
                pltpu.VMEM((8, GHOST, 128), F32),
                pltpu.VMEM((768, EDGES), BF16),
                pltpu.VMEM((512, EDGES), BF16),
                pltpu.VMEM((512, EDGES), BF16),
                pltpu.VMEM((256, EDGES), BF16),
                pltpu.VMEM((256, EDGES), BF16),
                pltpu.VMEM((16, EDGES), F32),
                pltpu.VMEM((2, C, EDGES), F32),
                pltpu.VMEM((2, C, EDGES), F32),
                pltpu.VMEM((C, EDGES), F32),
                pltpu.VMEM((NB, EDGES), F32),
                pltpu.VMEM((16, EDGES), BF16),
                pltpu.VMEM((2 * LAYERS, 192, 256), BF16),
                pltpu.VMEM((2 * LAYERS, C, 192), BF16),
                pltpu.VMEM((128, 768), BF16),
                pltpu.VMEM((256, 512), F32),
                pltpu.VMEM((8, TILE), F32),
                pltpu.VMEM((512, 256), BF16),
                pltpu.VMEM((512, 256), BF16),
                pltpu.VMEM((128, 512), BF16),
                pltpu.VMEM((2, 8, 128), F32),
                pltpu.VMEM((8, 8, 128), F32),
                pltpu.VMEM((2, most, 8, 128), F32),
                pltpu.SemaphoreType.DMA((10,)),
                pltpu.SemaphoreType.DMA((8,)),
                pltpu.SemaphoreType.DMA((8,)),
                pltpu.SemaphoreType.DMA((8,)),
                pltpu.SemaphoreType.DMA((8,)),
                pltpu.SemaphoreType.DMA((2, most)),
                pltpu.SemaphoreType.DMA((2, most)),
            ],
            compiler_params=pltpu.CompilerParams(
                collective_id=0, has_side_effects=True, vmem_limit_bytes=60 * 1024 * 1024
            ),
        )(
            positions, features, send_list.reshape(1, GHOST), edge_src.reshape(8, 128), edge_dst.reshape(8, 128),
            edge_count.reshape(1, 1), w_embed.T, w_env, jnp.swapaxes(w_update, 1, 2), w_out.reshape(1, C),
        )
        return forces[0:3], energy.reshape(())

    placed = (
        P(None, ("gx", "gy")), P(None, ("gx", "gy")), P(("gx", "gy")), P(("gx", "gy")), P(("gx", "gy")),
        P(("gx", "gy")), P(), P(), P(), P(),
    )
    return jax.shard_map(
        per_device, mesh=mesh, in_specs=placed, out_specs=(P(None, ("gx", "gy")), P()), check_vma=False
    )
```

```python
import math

import jax
import jax.numpy as jnp
from jax import lax
from jax.experimental import pallas as pl
from jax.experimental.pallas import tpu as pltpu
from jax.sharding import PartitionSpec as P

C = 64
NB = 8
LAYERS = 2
ATOMS = 64
GHOST = 32
EDGES = 1024
SCALE = 16 ** (-0.5)
OFFSETS = ((-1, -1), (-1, 0), (-1, 1), (0, -1), (0, 1), (1, -1), (1, 0), (1, 1))
GROUPS = ((0, 3, 5), (1, 6), (2, 4, 7))
SPANS = ((0, 3), (3, 5), (5, 8))
PLACE = (0, 3, 5, 1, 6, 2, 4, 7)
WIDTH = 6.0
CUTOFF = 5.0
F32 = jnp.float32
BF16 = jnp.bfloat16
MESH = pl.DeviceIdType.MESH
TILE = 256
CUT, LIVE, UX, UY, UZ, INV, DIST, GAIN, BEND, SLOPE, DCUT = 0, 1, 2, 3, 4, 5, 6, 7, 8, 9, 10


def split(x):
    hi = x.astype(BF16)
    return hi, (x - hi.astype(F32)).astype(BF16)


def split3(x):
    hi = x.astype(BF16)
    rest = x - hi.astype(F32)
    mid = rest.astype(BF16)
    return hi, mid, (rest - mid.astype(F32)).astype(BF16)


def dot(x, y):
    return lax.dot_general(x, y, (((1,), (0,)), ((), ())), preferred_element_type=F32)


def dot_t(x, y):
    return lax.dot_general(x, y, (((1,), (1,)), ((), ())), preferred_element_type=F32)


def pick_lane(tables, index):
    lane = index & 127
    which = index >> 7
    result = None
    for t, table in enumerate(tables):
        wide = jnp.broadcast_to(table, (8, 128))
        got = jnp.take_along_axis(wide, lane, axis=1, mode="promise_in_bounds")
        result = got if result is None else jnp.where(which == t, got, result)
    return result


def sizes_of(columns, rows):
    return (2 * rows, max(columns // 8, 1), min(4, columns // 2))


def kernel(
    columns, rows, sizes,
    pos_in, feat_in, send_in, src_in, dst_in, count_in, we_in, wv_in, wu_in, wo_in,
    out_ref,
    pos_ref, feat_ref, send_ref, src_ref, dst_ref, count_ref, we_ref, wv_ref, wu_ref, wo_ref,
    pay, table, ah, al, oh, vh, vl, row, value, gain_cut, df, dradial_map, ddb, lhs, own_weights, flat, kept, folded,
    uth, utl, embs, gsrc, gbuf, ebuf,
    in_sem, send_sem, recv_sem, gsend_sem, grecv_sem, esend_sem, erecv_sem,
):
    a = lax.axis_index("gx")
    b = lax.axis_index("gy")

    def peer(k):
        dx, dy = OFFSETS[k]
        return (lax.rem(a + dx + columns, columns), b + dy)

    def group_of(k):
        return 1 + OFFSETS[k][1]

    def each_group(act, otherwise=None):
        act(1)
        for g, good in ((0, b > 0), (2, b < rows - 1)):
            pl.when(good)(lambda g=g: act(g))
            if otherwise is not None:
                pl.when(jnp.logical_not(good))(lambda g=g: otherwise(g))

    def member(ph):
        if ph == 0:
            return lax.rem(a, 2) * rows + b
        return a // 8 if ph == 1 else lax.rem(a // 2, sizes[2])

    def energy_peer(ph, t):
        me = member(ph)
        other = lax.rem(me + t, sizes[ph])
        if ph == 0:
            return (a - lax.rem(a, 2) + other // rows, lax.rem(other, rows))
        return (a + (8 if ph == 1 else 2) * (other - me), b)

    barrier = pltpu.get_barrier_semaphore()

    def greet(g):
        for k in GROUPS[g]:
            pl.semaphore_signal(barrier, inc=1, device_id=peer(k), device_id_type=MESH)

    each_group(greet)
    greeted = 0
    for ph in range(3):
        for t in range(1, sizes[ph]):
            pl.semaphore_signal(barrier, inc=1, device_id=energy_peer(ph, t), device_id_type=MESH)
            greeted += 1

    fetched = [
        pltpu.make_async_copy(given, held, in_sem.at[i])
        for i, (given, held) in enumerate([
            (pos_in, pos_ref), (feat_in, feat_ref), (send_in, send_ref), (we_in, we_ref), (src_in, src_ref),
            (dst_in, dst_ref), (count_in, count_ref), (wv_in, wv_ref), (wu_in, wu_ref), (wo_in, wo_ref)])
    ]
    for copy in fetched:
        copy.start()
    for copy in fetched[0:4]:
        copy.wait()

    we_hi, we_lo = split(we_ref[:, 0 : 2 * C])
    we_both = jnp.concatenate(
        [jnp.concatenate([we_hi[:, 0:C], we_lo[:, 0:C]], axis=1),
         jnp.concatenate([we_hi[:, C : 2 * C], we_lo[:, C : 2 * C]], axis=1)], axis=0)
    feat = feat_ref[...]
    own = dot(we_both, jnp.concatenate([feat, feat], axis=0))
    own_src, own_dst = own[0:C], own[C : 2 * C]
    pos = pos_ref[...]
    send4 = jnp.concatenate([send_ref[...]] * 4, axis=1)
    st4 = (lax.broadcasted_iota(jnp.int32, (ATOMS, 128), 0) == send4).astype(F32).astype(BF16)
    exported = jnp.concatenate([own_src, pos, jnp.zeros((61, ATOMS), F32)], axis=0)
    e3 = split3(jnp.concatenate([exported, jnp.zeros((128, 128 - ATOMS), F32)], axis=1))
    st4_tall = jnp.concatenate([st4, jnp.zeros((128 - ATOMS, 128), BF16)], axis=0)
    payload = (dot(e3[2], st4_tall) + dot(e3[1], st4_tall)) + dot(e3[0], st4_tall)
    pay[...] = payload.T[0:GHOST, :]

    inner = jnp.logical_and(b > 0, b < rows - 1)
    pl.semaphore_wait(barrier, greeted + jnp.where(inner, 8, 5))

    def ghost_copy(k):
        return pltpu.make_async_remote_copy(
            src_ref=pay, dst_ref=table.at[PLACE[7 - k]], send_sem=send_sem.at[group_of(k)],
            recv_sem=recv_sem.at[group_of(7 - k)], device_id=peer(k), device_id_type=MESH,
        )

    def ghost_group(g):
        held = table.at[pl.ds(SPANS[g][0], len(GROUPS[g]))]
        return pltpu.make_async_remote_copy(
            src_ref=held, dst_ref=held, send_sem=send_sem.at[g], recv_sem=recv_sem.at[g],
            device_id=peer(GROUPS[g][0]), device_id_type=MESH,
        )

    def ghosts_out(g):
        for k in GROUPS[g]:
            ghost_copy(k).start()

    each_group(ghosts_out)

    for copy in fetched[4:]:
        copy.wait()

    def put_row(i, v):
        for j in range(8):
            row[i : i + 1, 128 * j : 128 * (j + 1)] = v[j : j + 1, :]

    def loop(count, act):
        for i in range(count):
            act(i)

    def tiles(act):
        loop(EDGES // TILE, lambda n: act(slice(n * TILE, (n + 1) * TILE)))

    src = src_ref[...]
    dst = dst_ref[...]
    block = (src - ATOMS) >> 5
    ghost = src >= ATOMS
    ox = jnp.zeros((8, 128), F32)
    oy = jnp.zeros((8, 128), F32)
    block_place = jnp.zeros((8, 128), jnp.int32)
    for k, (dx, dy) in enumerate(OFFSETS):
        here = jnp.logical_and(ghost, block == k)
        if dx:
            ox = jnp.where(here, WIDTH * dx, ox)
        if dy:
            oy = jnp.where(here, WIDTH * dy, oy)
        block_place = jnp.where(here, PLACE[k], block_place)
    step_y = (oy * (1.0 / WIDTH)).astype(jnp.int32)
    reach = jnp.logical_and(b + step_y >= 0, b + step_y < rows)
    place = lax.broadcasted_iota(jnp.int32, (8, 128), 0) * 128 + lax.broadcasted_iota(jnp.int32, (8, 128), 1)
    live = jnp.where(jnp.logical_and(place < count_ref[...], reach), 1.0, 0.0)
    put_row(LIVE, live)
    slot = jnp.where(ghost, block_place * GHOST + (src & (GHOST - 1)), src + 8 * GHOST)
    def one_hot(j):
        lanes = slice(j * 128, (j + 1) * 128)
        oh[0:320, lanes] = (
            lax.broadcasted_iota(jnp.int32, (320, 128), 0) == slot[j : j + 1, :]).astype(F32).astype(BF16)
        hot = (lax.broadcasted_iota(jnp.int32, (ATOMS, 128), 0) == dst[j : j + 1, :]).astype(F32).astype(BF16)
        oh[320:384, lanes] = hot
        ah[512:576, lanes] = hot

    loop(8, one_hot)

    def four(x):
        hi, lo = split(x)
        return jnp.concatenate([hi, hi, lo, lo], axis=1)

    def weigh(stage):
        layer = min(stage, 3 - stage)
        for i, d in enumerate((1, 2, 0)):
            env_hi, env_lo = split(wv_ref[layer, :, d * C : (d + 1) * C])
            upd_hi, upd_lo = split(wu_ref[layer, :, (d + 1) * C : (d + 2) * C] * SCALE)
            env = [env_hi, env_lo, env_hi, env_lo]
            upd = [upd_hi, upd_hi, upd_lo, upd_lo]
            left, right = (upd, env) if stage < LAYERS else (env, upd)
            lhs[stage, 64 * i : 64 * (i + 1)] = four(
                dot_t(jnp.concatenate(left, axis=1), jnp.concatenate(right, axis=1)))
        own_w = wu_ref[layer, :, 0:C]
        hi, lo = split(own_w if stage < LAYERS else own_w.T)
        own_weights[stage] = jnp.concatenate([hi, hi, lo], axis=1)

    weigh(0)
    wrt = we_ref[:, 2 * C : 2 * C + NB]
    wr = jnp.concatenate([wrt, jnp.zeros((C, 128 - NB), F32)], axis=1).T[0:NB, :]
    wr_low = wr - wr.astype(BF16).astype(F32)
    wr4 = jnp.concatenate([wr, wr, wr_low, jnp.zeros((104, C), F32)], axis=0).T.astype(BF16)
    wr2 = jnp.concatenate([wr, wr_low], axis=0)
    wr2 = jnp.concatenate([wr2, wr2], axis=1).astype(BF16)
    diagonal = lax.broadcasted_iota(jnp.int32, (C, C), 0) == lax.broadcasted_iota(jnp.int32, (C, C), 1)
    wo = jnp.sum(jnp.where(diagonal, wo_ref[...], 0.0), axis=1, keepdims=True)

    def blank(g):
        for i in range(*SPANS[g]):
            table[i] = jnp.zeros((GHOST, 128), F32)
            gbuf[i] = jnp.zeros((8, 128), F32)

    each_group(lambda g: ghost_group(g).wait_recv(), blank)

    ghosts = jnp.concatenate([table[0:4].reshape(128, 128).T, table[4:8].reshape(128, 128).T], axis=1)
    own_pos = jnp.concatenate([pos, jnp.zeros((3, 64), F32)], axis=1)
    diff = []
    for i in range(3):
        at_ghost = ghosts[C + i : C + i + 1, :]
        mine = own_pos[i : i + 1, :]
        at_src = pick_lane([at_ghost[:, 0:128], at_ghost[:, 128:256], mine], slot)
        if i < 2:
            at_src = at_src + (ox, oy)[i]
        diff.append(at_src - pick_lane([mine], dst))
    dist = jnp.sqrt(diff[0] * diff[0] + diff[1] * diff[1] + diff[2] * diff[2] + 1.0)
    inv = 1.0 / dist
    ux, uy, uz = (v * inv for v in diff)
    root = math.sqrt(3.0)
    harm = [ux, uy, uz, root * ux * uy, root * uy * uz, 0.5 * (3.0 * uz * uz - 1.0), root * ux * uz,
            0.5 * root * (ux * ux - uy * uy)]
    short = jnp.maximum(1.0 - (dist * dist) * (1.0 / CUTOFF**2), 0.0)
    envelope = short * short
    gain = envelope * inv
    slope = (-4.0 / CUTOFF**2) * dist * short
    put_row(DIST, jnp.minimum(dist, CUTOFF) * (1.0 / CUTOFF))
    put_row(GAIN, gain)
    put_row(BEND, (slope - gain) * inv)
    put_row(CUT, live * envelope)
    put_row(SLOPE, live * slope)
    for i, v in ((UX, ux), (UY, uy), (UZ, uz), (INV, inv)):
        put_row(i, v)
    def map_edges(j):
        lanes = slice(j * 128, (j + 1) * 128)
        hot = ah[512:576, lanes]
        for m in range(8):
            high, low = split(jnp.broadcast_to(harm[m][j : j + 1, :], (16, 128)))
            ah[64 * m : 64 * (m + 1), lanes] = hot * jnp.concatenate([high] * 4, axis=0)
            al[64 * m : 64 * (m + 1), lanes] = hot * jnp.concatenate([low] * 4, axis=0)

    loop(8, map_edges)

    emb_hi, emb_lo = split(jnp.concatenate([ghosts[0:C, :], own_src, own_dst], axis=1))
    embs[...] = jnp.concatenate(
        [jnp.concatenate([emb_hi, wr4], axis=1), jnp.concatenate([emb_lo, jnp.zeros((C, 128), BF16)], axis=1)], axis=0)
    order = (lax.broadcasted_iota(jnp.int32, (NB, TILE), 0) + 1).astype(F32)

    def keep(lanes, place, x):
        hi, lo = split(x)
        vh[place : place + C, lanes] = hi
        vl[place : place + C, lanes] = lo
        ah[576:640, lanes] = hi
        ah[640:704, lanes] = lo
        ah[704:768, lanes] = hi

    def activate(lanes, stage, q):
        s = 1.0 / (1.0 + jnp.exp(-q))
        v = q * s
        cut = row[CUT : CUT + 1, lanes]
        value[stage, :, lanes] = v
        gain_cut[stage, :, lanes] = (s + v * (1.0 - s)) * cut
        return v * cut

    def embed(lanes):
        turns = order * row[DIST : DIST + 1, lanes]
        whole = jnp.floor(turns + 0.5)
        angle = (turns - whole) * math.pi
        sign = 1.0 - 2.0 * (whole - 2.0 * jnp.floor(whole * 0.5))
        sq = angle * angle
        sine = 1.0 / 39916800.0
        for c in (-1.0 / 362880.0, 1.0 / 5040.0, -1.0 / 120.0, 1.0 / 6.0, -1.0):
            sine = c + sq * sine
        sine = -(angle * sine) * sign
        cosine = 1.0 / 479001600.0
        for c in (-1.0 / 3628800.0, 1.0 / 40320.0, -1.0 / 720.0, 1.0 / 24.0, -0.5, 1.0):
            cosine = c + sq * cosine
        cosine = cosine * sign
        near = row[GAIN : GAIN + 1, lanes]
        radial = sine * near
        dradial_map[:, lanes] = order * (math.pi / CUTOFF) * cosine * near + sine * row[BEND : BEND + 1, lanes]
        low = radial - radial.astype(BF16).astype(F32)
        oh[384:512, lanes] = jnp.concatenate([radial, low, radial, jnp.zeros((104, TILE), F32)], axis=0).astype(BF16)
        both = dot(embs[...], oh[:, lanes])
        f = activate(lanes, 0, both[0:C] + both[C : 2 * C])
        df[:, lanes] = f
        keep(lanes, 192, f)

    degree = lax.broadcasted_iota(jnp.int32, (C, 512), 1) >= 192

    def mix(stage, place):
        sums = dot_t(ah[576:704, :], ah[0:576, :])
        sums = sums[0:C] + sums[C : 2 * C]
        hi, lo = split(sums[:, 0:512] + dot_t(ah[576:640, :], al[...]))
        every = dot(lhs[stage, 0:128], jnp.concatenate([hi, lo, hi, lo], axis=0))
        outer = jnp.where(degree, every[C : 2 * C], every[0:C])
        kept[place : place + C, :] = outer
        hi, lo = split(sums[:, 512:576])
        inner = dot(lhs[stage, 128:192], jnp.concatenate([hi, lo, hi, lo], axis=0))
        hi, lo = split(outer)
        flat[0:C, 0:512] = hi
        flat[C : 2 * C, 0:512] = lo
        hi, lo = split(inner)
        flat[0:C, 512:768] = jnp.concatenate([hi, own_weights[stage]], axis=1)
        flat[C : 2 * C, 512:768] = jnp.concatenate([lo, jnp.zeros((C, 192), BF16)], axis=1)

    def spread(lanes):
        both = dot(flat[...], ah[:, lanes])
        return both[0:C] + both[C : 2 * C] + dot(flat[0:C, 0:512], al[:, lanes])

    def back_map(place):
        hi, lo = split(kept[place : place + 128, :].T)
        uth[:, place : place + 128] = hi
        utl[:, place : place + 128] = lo

    def energy_out(ph, x):
        me = member(ph)
        ebuf[ph, me] = x
        for t in range(1, sizes[ph]):
            pltpu.make_async_remote_copy(
                src_ref=ebuf.at[ph, me], dst_ref=ebuf.at[ph, me], send_sem=esend_sem.at[ph], recv_sem=erecv_sem.at[ph],
                device_id=energy_peer(ph, t), device_id_type=MESH,
            ).start()

    def energy_group(ph):
        held = ebuf.at[ph, pl.ds(0, sizes[ph] - 1)]
        return pltpu.make_async_remote_copy(
            src_ref=held, dst_ref=held, send_sem=esend_sem.at[ph], recv_sem=erecv_sem.at[ph],
            device_id=energy_peer(ph, 1), device_id_type=MESH,
        )

    def energy_in(ph):
        if sizes[ph] > 1:
            energy_group(ph).wait_recv()
        total = ebuf[ph, 0]
        for t in range(1, sizes[ph]):
            total = total + ebuf[ph, t]
        return total

    weigh(1)
    tiles(embed)

    def first_layer(lanes):
        f = df[:, lanes] + activate(lanes, 1, spread(lanes))
        df[:, lanes] = f
        keep(lanes, 64, f)

    folded[...] = jnp.zeros((8, TILE), F32)

    def turn(lanes):
        q = spread(lanes)
        s = 1.0 / (1.0 + jnp.exp(-q))
        v = q * s
        cut = row[CUT : CUT + 1, lanes]
        f = df[:, lanes] + v * cut
        g = wo * row[LIVE : LIVE + 1, lanes]
        per_edge = f * g
        piece = per_edge[0:8]
        for i in range(1, 8):
            piece = piece + per_edge[8 * i : 8 * i + 8]
        folded[...] += piece
        df[:, lanes] = g
        row[DCUT : DCUT + 1, lanes] = jnp.sum(g * v, axis=0, keepdims=True)
        keep(lanes, 0, g * ((s + v * (1.0 - s)) * cut))

    def back_first(lanes):
        g = df[:, lanes] + spread(lanes)
        df[:, lanes] = g
        row[DCUT : DCUT + 1, lanes] += jnp.sum(g * value[1, :, lanes], axis=0, keepdims=True)
        keep(lanes, 128, g * gain_cut[1, :, lanes])

    mix(0, 128)
    weigh(2)
    tiles(first_layer)
    mix(1, 0)
    weigh(3)
    tiles(turn)
    energy_out(0, folded[:, 0:128] + folded[:, 128:256])
    mix(2, 64)
    tiles(back_first)
    back_map(0)
    mix(3, 192)
    back_map(128)
    energy_out(1, energy_in(0))

    def back_embed(lanes):
        g = df[:, lanes] + spread(lanes)
        dcut = row[DCUT : DCUT + 1, lanes] + jnp.sum(g * value[0, :, lanes], axis=0, keepdims=True)
        both = dot(wr2, jnp.concatenate(split(g * gain_cut[0, :, lanes]), axis=0))
        dr = jnp.sum((both[0:8] + both[8:16]) * dradial_map[:, lanes], axis=0, keepdims=True)
        dr = dr + dcut * row[SLOPE : SLOPE + 1, lanes]
        right = vh[:, lanes]
        part = dot(uth[...], right) + dot(utl[...], right) + dot(uth[...], vl[:, lanes])
        hot = ah[512:576, lanes].astype(F32)
        g = [jnp.sum(hot * part[64 * m : 64 * (m + 1)], axis=0, keepdims=True) for m in range(8)]
        xr, yr, zr, ir = (row[i : i + 1, lanes] for i in (UX, UY, UZ, INV))
        dux = g[0] + root * (g[3] * yr + g[6] * zr + g[7] * xr)
        duy = g[1] + root * (g[3] * xr + g[4] * zr - g[7] * yr)
        duz = g[2] + root * (g[4] * yr + g[6] * xr) + 3.0 * g[5] * zr
        along = dr - (dux * xr + duy * yr + duz * zr) * ir
        dd = jnp.concatenate(
            [dux * ir + along * xr, duy * ir + along * yr, duz * ir + along * zr, jnp.zeros((5, TILE), F32)], axis=0)
        ddb[:, lanes] = jnp.concatenate([dd, dd - dd.astype(BF16).astype(F32)], axis=0).astype(BF16)

    tiles(back_embed)
    scattered = dot_t(ddb[...], oh[0:384, :])
    scattered = scattered[0:8] + scattered[8:16]
    gsrc[0] = scattered[:, 0:128]
    gsrc[1] = scattered[:, 128:256]
    def force_copy(k):
        return pltpu.make_async_remote_copy(
            src_ref=gsrc.at[PLACE[k] // 4], dst_ref=gbuf.at[PLACE[7 - k]], send_sem=gsend_sem.at[group_of(k)],
            recv_sem=grecv_sem.at[group_of(7 - k)], device_id=peer(k), device_id_type=MESH,
        )

    def force_group(g):
        held = gbuf.at[pl.ds(SPANS[g][0], len(GROUPS[g]))]
        return pltpu.make_async_remote_copy(
            src_ref=held, dst_ref=held, send_sem=gsend_sem.at[g], recv_sem=grecv_sem.at[g],
            device_id=peer(GROUPS[g][0]), device_id_type=MESH,
        )

    def forces_out(g):
        for k in GROUPS[g]:
            force_copy(k).start()

    each_group(forces_out)
    energy_out(2, energy_in(1))
    at_own = scattered[:, 256:320] - scattered[:, 320:384]
    for ph in range(2):
        if sizes[ph] > 1:
            energy_group(ph).wait_send()
    each_group(lambda g: ghost_group(g).wait_send())

    def forces_in(g):
        force_group(g).wait_recv()
        force_group(g).wait_send()

    each_group(forces_in)
    lane_group = lax.broadcasted_iota(jnp.int32, (8, 128), 1) >> 5
    acc = jnp.zeros((8, 128), F32)
    for k in range(8):
        acc = acc + jnp.where(lane_group == PLACE[7 - k] % 4, gbuf[PLACE[k]], 0.0)
    acc_low = acc - acc.astype(BF16).astype(F32)
    returned = dot_t(jnp.concatenate([acc, acc_low], axis=0).astype(BF16), st4)
    forces = -(at_own + returned[0:8] + returned[8:16])

    total = energy_in(2)
    energy = jnp.sum(jnp.sum(total, axis=0, keepdims=True), axis=1, keepdims=True)
    out_ref[...] = jnp.where(lax.broadcasted_iota(jnp.int32, (8, ATOMS), 0) == 3, energy, forces)
    energy_group(2).wait_send()


def solution(mesh):
    columns, rows = mesh.shape["gx"], mesh.shape["gy"]
    sizes = sizes_of(columns, rows)
    most = max(sizes)

    def per_device(positions, features, send_list, edge_src, edge_dst, edge_count, w_embed, w_env, w_update, w_out):
        def body(*refs):
            kernel(columns, rows, sizes, *refs)

        vmem = pl.BlockSpec(memory_space=pltpu.VMEM)
        anywhere = pl.BlockSpec(memory_space=pl.ANY)
        out = pl.pallas_call(
            body,
            out_shape=jax.ShapeDtypeStruct((8, ATOMS), F32),
            in_specs=[anywhere] * 10,
            out_specs=vmem,
            scratch_shapes=[
                pltpu.VMEM((3, ATOMS), F32),
                pltpu.VMEM((C, ATOMS), BF16),
                pltpu.VMEM((1, GHOST), jnp.int32),
                pltpu.VMEM((8, 128), jnp.int32),
                pltpu.VMEM((8, 128), jnp.int32),
                pltpu.VMEM((1, 1), jnp.int32),
                pltpu.VMEM((C, 2 * C + NB), F32),
                pltpu.VMEM((LAYERS, C, 3 * C), F32),
                pltpu.VMEM((LAYERS, C, 4 * C), F32),
                pltpu.VMEM((1, C), F32),
                pltpu.VMEM((GHOST, 128), F32),
                pltpu.VMEM((8, GHOST, 128), F32),
                pltpu.VMEM((768, EDGES), BF16),
                pltpu.VMEM((512, EDGES), BF16),
                pltpu.VMEM((512, EDGES), BF16),
                pltpu.VMEM((256, EDGES), BF16),
                pltpu.VMEM((256, EDGES), BF16),
                pltpu.VMEM((16, EDGES), F32),
                pltpu.VMEM((2, C, EDGES), F32),
                pltpu.VMEM((2, C, EDGES), F32),
                pltpu.VMEM((C, EDGES), F32),
                pltpu.VMEM((NB, EDGES), F32),
                pltpu.VMEM((16, EDGES), BF16),
                pltpu.VMEM((2 * LAYERS, 192, 256), BF16),
                pltpu.VMEM((2 * LAYERS, C, 192), BF16),
                pltpu.VMEM((128, 768), BF16),
                pltpu.VMEM((256, 512), F32),
                pltpu.VMEM((8, TILE), F32),
                pltpu.VMEM((512, 256), BF16),
                pltpu.VMEM((512, 256), BF16),
                pltpu.VMEM((128, 512), BF16),
                pltpu.VMEM((2, 8, 128), F32),
                pltpu.VMEM((8, 8, 128), F32),
                pltpu.VMEM((3, most, 8, 128), F32),
                pltpu.SemaphoreType.DMA((10,)),
                pltpu.SemaphoreType.DMA((3,)),
                pltpu.SemaphoreType.DMA((3,)),
                pltpu.SemaphoreType.DMA((3,)),
                pltpu.SemaphoreType.DMA((3,)),
                pltpu.SemaphoreType.DMA((3,)),
                pltpu.SemaphoreType.DMA((3,)),
            ],
            compiler_params=pltpu.CompilerParams(
                collective_id=0, has_side_effects=True, vmem_limit_bytes=60 * 1024 * 1024
            ),
        )(
            positions, features, send_list.reshape(1, GHOST), edge_src.reshape(8, 128), edge_dst.reshape(8, 128),
            edge_count.reshape(1, 1), w_embed.T, w_env, jnp.swapaxes(w_update, 1, 2), w_out.reshape(1, C),
        )
        return out[0:3], out[3, 0]

    placed = (
        P(None, ("gx", "gy")), P(None, ("gx", "gy")), P(("gx", "gy")), P(("gx", "gy")), P(("gx", "gy")),
        P(("gx", "gy")), P(), P(), P(), P(),
    )
    return jax.shard_map(
        per_device, mesh=mesh, in_specs=placed, out_specs=(P(None, ("gx", "gy")), P()), check_vma=False
    )
```

```python
import math

import jax
import jax.numpy as jnp
from jax import lax
from jax.experimental import pallas as pl
from jax.experimental.pallas import tpu as pltpu
from jax.sharding import PartitionSpec as P

C = 64
NB = 8
LAYERS = 2
ATOMS = 64
GHOST = 32
EDGES = 1024
SCALE = 16 ** (-0.5)
OFFSETS = ((-1, -1), (-1, 0), (-1, 1), (0, -1), (0, 1), (1, -1), (1, 0), (1, 1))
GROUPS = ((0, 3, 5), (1, 6), (2, 4, 7))
SPANS = ((0, 3), (3, 5), (5, 8))
PLACE = (0, 3, 5, 1, 6, 2, 4, 7)
WIDTH = 6.0
CUTOFF = 5.0
F32 = jnp.float32
BF16 = jnp.bfloat16
MESH = pl.DeviceIdType.MESH
TILE = 256
CUT, LIVE, UX, UY, UZ, INV, DIST, GAIN, BEND, SLOPE, DCUT = 0, 1, 2, 3, 4, 5, 6, 7, 8, 9, 10


def split(x):
    hi = x.astype(BF16)
    return hi, (x - hi.astype(F32)).astype(BF16)


def split3(x):
    hi = x.astype(BF16)
    rest = x - hi.astype(F32)
    mid = rest.astype(BF16)
    return hi, mid, (rest - mid.astype(F32)).astype(BF16)


def dot(x, y):
    return lax.dot_general(x, y, (((1,), (0,)), ((), ())), preferred_element_type=F32)


def dot_t(x, y):
    return lax.dot_general(x, y, (((1,), (1,)), ((), ())), preferred_element_type=F32)


def pick_lane(tables, index):
    lane = index & 127
    which = index >> 7
    result = None
    for t, table in enumerate(tables):
        wide = jnp.broadcast_to(table, (8, 128))
        got = jnp.take_along_axis(wide, lane, axis=1, mode="promise_in_bounds")
        result = got if result is None else jnp.where(which == t, got, result)
    return result


def sizes_of(columns, rows):
    return (2 * rows, max(columns // 8, 1), min(4, columns // 2))


def kernel(
    columns, rows, sizes,
    pos_in, feat_in, send_in, src_in, dst_in, count_in, we_in, wv_in, wu_in, wo_in,
    forces_ref, energy_ref,
    pos_ref, feat_ref, send_ref, src_ref, dst_ref, count_ref, we_ref, wv_ref, wu_ref, wo_ref,
    pay, table, ah, al, oh, vh, vl, row, value, gain_cut, df, dradial_map, ddb, lhs, own_weights, flat, kept, folded,
    uth, utl, embs, gsrc, gbuf, ebuf,
    in_sem, send_sem, recv_sem, gsend_sem, grecv_sem, esend_sem, erecv_sem,
):
    a = lax.axis_index("gx")
    b = lax.axis_index("gy")

    def peer(k):
        dx, dy = OFFSETS[k]
        return (lax.rem(a + dx + columns, columns), b + dy)

    def group_of(k):
        return 1 + OFFSETS[k][1]

    def each_group(act, otherwise=None):
        act(1)
        for g, good in ((0, b > 0), (2, b < rows - 1)):
            pl.when(good)(lambda g=g: act(g))
            if otherwise is not None:
                pl.when(jnp.logical_not(good))(lambda g=g: otherwise(g))

    def member(ph):
        if ph == 0:
            return lax.rem(a, 2) * rows + b
        return a // 8 if ph == 1 else lax.rem(a // 2, sizes[2])

    def energy_peer(ph, t):
        me = member(ph)
        other = lax.rem(me + t, sizes[ph])
        if ph == 0:
            return (a - lax.rem(a, 2) + other // rows, lax.rem(other, rows))
        return (a + (8 if ph == 1 else 2) * (other - me), b)

    barrier = pltpu.get_barrier_semaphore()

    def greet(g):
        for k in GROUPS[g]:
            pl.semaphore_signal(barrier, inc=1, device_id=peer(k), device_id_type=MESH)

    each_group(greet)
    greeted = 0
    for ph in range(3):
        for t in range(1, sizes[ph]):
            pl.semaphore_signal(barrier, inc=1, device_id=energy_peer(ph, t), device_id_type=MESH)
            greeted += 1

    fetched = [
        pltpu.make_async_copy(given, held, in_sem.at[i])
        for i, (given, held) in enumerate([
            (pos_in, pos_ref), (feat_in, feat_ref), (send_in, send_ref), (we_in, we_ref), (src_in, src_ref),
            (dst_in, dst_ref), (count_in, count_ref), (wv_in, wv_ref), (wu_in, wu_ref), (wo_in, wo_ref)])
    ]
    for copy in fetched:
        copy.start()
    for copy in fetched[0:4]:
        copy.wait()

    we_hi, we_lo = split(we_ref[:, 0 : 2 * C])
    we_both = jnp.concatenate(
        [jnp.concatenate([we_hi[:, 0:C], we_lo[:, 0:C]], axis=1),
         jnp.concatenate([we_hi[:, C : 2 * C], we_lo[:, C : 2 * C]], axis=1)], axis=0)
    feat = feat_ref[...]
    own = dot(we_both, jnp.concatenate([feat, feat], axis=0))
    own_src, own_dst = own[0:C], own[C : 2 * C]
    pos = pos_ref[...]
    send4 = jnp.concatenate([send_ref[...]] * 4, axis=1)
    st4 = (lax.broadcasted_iota(jnp.int32, (ATOMS, 128), 0) == send4).astype(F32).astype(BF16)
    exported = jnp.concatenate([own_src, pos, jnp.zeros((61, ATOMS), F32)], axis=0)
    e3 = split3(jnp.concatenate([exported, jnp.zeros((128, 128 - ATOMS), F32)], axis=1))
    st4_tall = jnp.concatenate([st4, jnp.zeros((128 - ATOMS, 128), BF16)], axis=0)
    payload = (dot(e3[2], st4_tall) + dot(e3[1], st4_tall)) + dot(e3[0], st4_tall)
    lane_group = lax.broadcasted_iota(jnp.int32, (16, 128), 1) >> 5

    def by_group(parts):
        result = parts[0]
        for q in range(1, len(parts)):
            result = jnp.where(lane_group[0 : result.shape[0]] == q, parts[q], result)
        return result

    pay[0:16] = by_group([payload[16 * q : 16 * q + 16] for q in range(4)])
    pay[16:17] = by_group([payload[C + i : C + i + 1] for i in range(3)])

    inner = jnp.logical_and(b > 0, b < rows - 1)
    pl.semaphore_wait(barrier, greeted + jnp.where(inner, 8, 5))

    def ghost_copy(k):
        return pltpu.make_async_remote_copy(
            src_ref=pay, dst_ref=table.at[PLACE[7 - k]], send_sem=send_sem.at[group_of(k)],
            recv_sem=recv_sem.at[group_of(7 - k)], device_id=peer(k), device_id_type=MESH,
        )

    def ghost_group(g):
        held = table.at[pl.ds(SPANS[g][0], len(GROUPS[g]))]
        return pltpu.make_async_remote_copy(
            src_ref=held, dst_ref=held, send_sem=send_sem.at[g], recv_sem=recv_sem.at[g],
            device_id=peer(GROUPS[g][0]), device_id_type=MESH,
        )

    def ghosts_out(g):
        for k in GROUPS[g]:
            ghost_copy(k).start()

    each_group(ghosts_out)

    for copy in fetched[4:]:
        copy.wait()

    def put_row(i, v):
        for j in range(8):
            row[i : i + 1, 128 * j : 128 * (j + 1)] = v[j : j + 1, :]

    def loop(count, act):
        for i in range(count):
            act(i)

    def tiles(act):
        loop(EDGES // TILE, lambda n: act(slice(n * TILE, (n + 1) * TILE)))

    src = src_ref[...]
    dst = dst_ref[...]
    block = (src - ATOMS) >> 5
    ghost = src >= ATOMS
    ox = jnp.zeros((8, 128), F32)
    oy = jnp.zeros((8, 128), F32)
    block_place = jnp.zeros((8, 128), jnp.int32)
    for k, (dx, dy) in enumerate(OFFSETS):
        here = jnp.logical_and(ghost, block == k)
        if dx:
            ox = jnp.where(here, WIDTH * dx, ox)
        if dy:
            oy = jnp.where(here, WIDTH * dy, oy)
        block_place = jnp.where(here, PLACE[k], block_place)
    step_y = (oy * (1.0 / WIDTH)).astype(jnp.int32)
    reach = jnp.logical_and(b + step_y >= 0, b + step_y < rows)
    place = lax.broadcasted_iota(jnp.int32, (8, 128), 0) * 128 + lax.broadcasted_iota(jnp.int32, (8, 128), 1)
    live = jnp.where(jnp.logical_and(place < count_ref[...], reach), 1.0, 0.0)
    put_row(LIVE, live)
    slot = jnp.where(ghost, block_place * GHOST + (src & (GHOST - 1)), src + 8 * GHOST)
    def one_hot(j):
        lanes = slice(j * 128, (j + 1) * 128)
        oh[0:320, lanes] = (
            lax.broadcasted_iota(jnp.int32, (320, 128), 0) == slot[j : j + 1, :]).astype(F32).astype(BF16)
        hot = (lax.broadcasted_iota(jnp.int32, (ATOMS, 128), 0) == dst[j : j + 1, :]).astype(F32).astype(BF16)
        oh[320:384, lanes] = hot
        ah[512:576, lanes] = hot

    loop(8, one_hot)

    def four(x):
        hi, lo = split(x)
        return jnp.concatenate([hi, hi, lo, lo], axis=1)

    def weigh(stage):
        layer = min(stage, 3 - stage)
        for i, d in enumerate((1, 2, 0)):
            env_hi, env_lo = split(wv_ref[layer, :, d * C : (d + 1) * C])
            upd_hi, upd_lo = split(wu_ref[layer, :, (d + 1) * C : (d + 2) * C] * SCALE)
            env = [env_hi, env_lo, env_hi, env_lo]
            upd = [upd_hi, upd_hi, upd_lo, upd_lo]
            left, right = (upd, env) if stage < LAYERS else (env, upd)
            lhs[stage, 64 * i : 64 * (i + 1)] = four(
                dot_t(jnp.concatenate(left, axis=1), jnp.concatenate(right, axis=1)))
        own_w = wu_ref[layer, :, 0:C]
        hi, lo = split(own_w if stage < LAYERS else own_w.T)
        own_weights[stage] = jnp.concatenate([hi, hi, lo], axis=1)

    weigh(0)
    wrt = we_ref[:, 2 * C : 2 * C + NB]
    wr = jnp.concatenate([wrt, jnp.zeros((C, 128 - NB), F32)], axis=1).T[0:NB, :]
    wr_low = wr - wr.astype(BF16).astype(F32)
    wr4 = jnp.concatenate([wr, wr, wr_low, jnp.zeros((104, C), F32)], axis=0).T.astype(BF16)
    wr2 = jnp.concatenate([wr, wr_low], axis=0)
    wr2 = jnp.concatenate([wr2, wr2], axis=1).astype(BF16)
    diagonal = lax.broadcasted_iota(jnp.int32, (C, C), 0) == lax.broadcasted_iota(jnp.int32, (C, C), 1)
    wo = jnp.sum(jnp.where(diagonal, wo_ref[...], 0.0), axis=1, keepdims=True)

    def blank(g):
        for i in range(*SPANS[g]):
            table[i] = jnp.zeros((17, 128), F32)
            gbuf[i] = jnp.zeros((8, 128), F32)

    each_group(lambda g: ghost_group(g).wait_recv(), blank)

    def turned(x, groups):
        cut = 128 - 32 * (groups % 4)
        return x if groups % 4 == 0 else jnp.concatenate([x[:, cut:], x[:, :cut]], axis=1)

    channels, coords = [[], [], [], []], [[], [], []]
    for t in range(2):
        held = [table[4 * t + i] for i in range(4)]
        for q in range(4):
            around = [turned(held[i], i - q) for i in range(4)]
            channels[q].append(by_group([x[0:16] for x in around]))
            if q < 3:
                coords[q].append(by_group([x[16:17] for x in around]))
    ghosts = jnp.concatenate([jnp.concatenate(x, axis=1) for x in channels], axis=0)
    own_pos = jnp.concatenate([pos, jnp.zeros((3, 64), F32)], axis=1)
    diff = []
    for i in range(3):
        mine = own_pos[i : i + 1, :]
        at_src = pick_lane(coords[i] + [mine], slot)
        if i < 2:
            at_src = at_src + (ox, oy)[i]
        diff.append(at_src - pick_lane([mine], dst))
    dist = jnp.sqrt(diff[0] * diff[0] + diff[1] * diff[1] + diff[2] * diff[2] + 1.0)
    inv = 1.0 / dist
    ux, uy, uz = (v * inv for v in diff)
    root = math.sqrt(3.0)
    harm = [ux, uy, uz, root * ux * uy, root * uy * uz, 0.5 * (3.0 * uz * uz - 1.0), root * ux * uz,
            0.5 * root * (ux * ux - uy * uy)]
    short = jnp.maximum(1.0 - (dist * dist) * (1.0 / CUTOFF**2), 0.0)
    envelope = short * short
    gain = envelope * inv
    slope = (-4.0 / CUTOFF**2) * dist * short
    put_row(DIST, jnp.minimum(dist, CUTOFF) * (1.0 / CUTOFF))
    put_row(GAIN, gain)
    put_row(BEND, (slope - gain) * inv)
    put_row(CUT, live * envelope)
    put_row(SLOPE, live * slope)
    for i, v in ((UX, ux), (UY, uy), (UZ, uz), (INV, inv)):
        put_row(i, v)
    def map_edges(j):
        lanes = slice(j * 128, (j + 1) * 128)
        hot = ah[512:576, lanes]
        for m in range(8):
            high, low = split(jnp.broadcast_to(harm[m][j : j + 1, :], (16, 128)))
            ah[64 * m : 64 * (m + 1), lanes] = hot * jnp.concatenate([high] * 4, axis=0)
            al[64 * m : 64 * (m + 1), lanes] = hot * jnp.concatenate([low] * 4, axis=0)

    loop(8, map_edges)

    emb_hi, emb_lo = split(jnp.concatenate([ghosts, own_src, own_dst], axis=1))
    embs[...] = jnp.concatenate(
        [jnp.concatenate([emb_hi, wr4], axis=1), jnp.concatenate([emb_lo, jnp.zeros((C, 128), BF16)], axis=1)], axis=0)
    order = (lax.broadcasted_iota(jnp.int32, (NB, TILE), 0) + 1).astype(F32)

    def keep(lanes, place, x):
        hi, lo = split(x)
        vh[place : place + C, lanes] = hi
        vl[place : place + C, lanes] = lo
        ah[576:640, lanes] = hi
        ah[640:704, lanes] = lo
        ah[704:768, lanes] = hi

    def activate(lanes, stage, q):
        s = 1.0 / (1.0 + jnp.exp(-q))
        v = q * s
        cut = row[CUT : CUT + 1, lanes]
        value[stage, :, lanes] = v
        gain_cut[stage, :, lanes] = (s + v * (1.0 - s)) * cut
        return v * cut

    def embed(lanes):
        turns = order * row[DIST : DIST + 1, lanes]
        whole = jnp.floor(turns + 0.5)
        angle = (turns - whole) * math.pi
        sign = 1.0 - 2.0 * (whole - 2.0 * jnp.floor(whole * 0.5))
        sq = angle * angle
        sine = 1.0 / 39916800.0
        for c in (-1.0 / 362880.0, 1.0 / 5040.0, -1.0 / 120.0, 1.0 / 6.0, -1.0):
            sine = c + sq * sine
        sine = -(angle * sine) * sign
        cosine = 1.0 / 479001600.0
        for c in (-1.0 / 3628800.0, 1.0 / 40320.0, -1.0 / 720.0, 1.0 / 24.0, -0.5, 1.0):
            cosine = c + sq * cosine
        cosine = cosine * sign
        near = row[GAIN : GAIN + 1, lanes]
        radial = sine * near
        dradial_map[:, lanes] = order * (math.pi / CUTOFF) * cosine * near + sine * row[BEND : BEND + 1, lanes]
        low = radial - radial.astype(BF16).astype(F32)
        oh[384:512, lanes] = jnp.concatenate([radial, low, radial, jnp.zeros((104, TILE), F32)], axis=0).astype(BF16)
        both = dot(embs[...], oh[:, lanes])
        f = activate(lanes, 0, both[0:C] + both[C : 2 * C])
        df[:, lanes] = f
        keep(lanes, 192, f)

    degree = lax.broadcasted_iota(jnp.int32, (C, 512), 1) >= 192

    def mix(stage, place):
        sums = dot_t(ah[576:704, :], ah[0:576, :])
        sums = sums[0:C] + sums[C : 2 * C]
        hi, lo = split(sums[:, 0:512] + dot_t(ah[576:640, :], al[...]))
        every = dot(lhs[stage, 0:128], jnp.concatenate([hi, lo, hi, lo], axis=0))
        outer = jnp.where(degree, every[C : 2 * C], every[0:C])
        kept[place : place + C, :] = outer
        hi, lo = split(sums[:, 512:576])
        inner = dot(lhs[stage, 128:192], jnp.concatenate([hi, lo, hi, lo], axis=0))
        hi, lo = split(outer)
        flat[0:C, 0:512] = hi
        flat[C : 2 * C, 0:512] = lo
        hi, lo = split(inner)
        flat[0:C, 512:768] = jnp.concatenate([hi, own_weights[stage]], axis=1)
        flat[C : 2 * C, 512:768] = jnp.concatenate([lo, jnp.zeros((C, 192), BF16)], axis=1)

    def spread(lanes):
        both = dot(flat[...], ah[:, lanes])
        return both[0:C] + both[C : 2 * C] + dot(flat[0:C, 0:512], al[:, lanes])

    def back_map(place):
        hi, lo = split(kept[place : place + 128, :].T)
        uth[:, place : place + 128] = hi
        utl[:, place : place + 128] = lo

    def energy_out(ph, x):
        me = member(ph)
        ebuf[ph, me] = x
        for t in range(1, sizes[ph]):
            pltpu.make_async_remote_copy(
                src_ref=ebuf.at[ph, me], dst_ref=ebuf.at[ph, me], send_sem=esend_sem.at[ph], recv_sem=erecv_sem.at[ph],
                device_id=energy_peer(ph, t), device_id_type=MESH,
            ).start()

    def energy_group(ph):
        held = ebuf.at[ph, pl.ds(0, sizes[ph] - 1)]
        return pltpu.make_async_remote_copy(
            src_ref=held, dst_ref=held, send_sem=esend_sem.at[ph], recv_sem=erecv_sem.at[ph],
            device_id=energy_peer(ph, 1), device_id_type=MESH,
        )

    def energy_in(ph):
        if sizes[ph] > 1:
            energy_group(ph).wait_recv()
        total = ebuf[ph, 0]
        for t in range(1, sizes[ph]):
            total = total + ebuf[ph, t]
        return total

    weigh(1)
    tiles(embed)

    def first_layer(lanes):
        f = df[:, lanes] + activate(lanes, 1, spread(lanes))
        df[:, lanes] = f
        keep(lanes, 64, f)

    folded[...] = jnp.zeros((8, TILE), F32)

    def turn(lanes):
        q = spread(lanes)
        s = 1.0 / (1.0 + jnp.exp(-q))
        v = q * s
        cut = row[CUT : CUT + 1, lanes]
        f = df[:, lanes] + v * cut
        g = wo * row[LIVE : LIVE + 1, lanes]
        per_edge = f * g
        piece = per_edge[0:8]
        for i in range(1, 8):
            piece = piece + per_edge[8 * i : 8 * i + 8]
        folded[...] += piece
        df[:, lanes] = g
        row[DCUT : DCUT + 1, lanes] = jnp.sum(g * v, axis=0, keepdims=True)
        keep(lanes, 0, g * ((s + v * (1.0 - s)) * cut))

    def back_first(lanes):
        g = df[:, lanes] + spread(lanes)
        df[:, lanes] = g
        row[DCUT : DCUT + 1, lanes] += jnp.sum(g * value[1, :, lanes], axis=0, keepdims=True)
        keep(lanes, 128, g * gain_cut[1, :, lanes])

    mix(0, 128)
    weigh(2)
    tiles(first_layer)
    mix(1, 0)
    weigh(3)
    tiles(turn)
    energy_out(0, folded[:, 0:128] + folded[:, 128:256])
    mix(2, 64)
    tiles(back_first)
    back_map(0)
    mix(3, 192)
    back_map(128)
    energy_out(1, energy_in(0))

    def back_embed(lanes):
        g = df[:, lanes] + spread(lanes)
        dcut = row[DCUT : DCUT + 1, lanes] + jnp.sum(g * value[0, :, lanes], axis=0, keepdims=True)
        both = dot(wr2, jnp.concatenate(split(g * gain_cut[0, :, lanes]), axis=0))
        dr = jnp.sum((both[0:8] + both[8:16]) * dradial_map[:, lanes], axis=0, keepdims=True)
        dr = dr + dcut * row[SLOPE : SLOPE + 1, lanes]
        right = vh[:, lanes]
        part = dot(uth[...], right) + dot(utl[...], right) + dot(uth[...], vl[:, lanes])
        hot = ah[512:576, lanes].astype(F32)
        g = [jnp.sum(hot * part[64 * m : 64 * (m + 1)], axis=0, keepdims=True) for m in range(8)]
        xr, yr, zr, ir = (row[i : i + 1, lanes] for i in (UX, UY, UZ, INV))
        dux = g[0] + root * (g[3] * yr + g[6] * zr + g[7] * xr)
        duy = g[1] + root * (g[3] * xr + g[4] * zr - g[7] * yr)
        duz = g[2] + root * (g[4] * yr + g[6] * xr) + 3.0 * g[5] * zr
        along = dr - (dux * xr + duy * yr + duz * zr) * ir
        dd = jnp.concatenate(
            [dux * ir + along * xr, duy * ir + along * yr, duz * ir + along * zr, jnp.zeros((5, TILE), F32)], axis=0)
        ddb[:, lanes] = jnp.concatenate([dd, dd - dd.astype(BF16).astype(F32)], axis=0).astype(BF16)

    tiles(back_embed)
    scattered = dot_t(ddb[...], oh[0:384, :])
    scattered = scattered[0:8] + scattered[8:16]
    gsrc[0] = scattered[:, 0:128]
    gsrc[1] = scattered[:, 128:256]
    def force_copy(k):
        return pltpu.make_async_remote_copy(
            src_ref=gsrc.at[PLACE[k] // 4], dst_ref=gbuf.at[PLACE[7 - k]], send_sem=gsend_sem.at[group_of(k)],
            recv_sem=grecv_sem.at[group_of(7 - k)], device_id=peer(k), device_id_type=MESH,
        )

    def force_group(g):
        held = gbuf.at[pl.ds(SPANS[g][0], len(GROUPS[g]))]
        return pltpu.make_async_remote_copy(
            src_ref=held, dst_ref=held, send_sem=gsend_sem.at[g], recv_sem=grecv_sem.at[g],
            device_id=peer(GROUPS[g][0]), device_id_type=MESH,
        )

    def forces_out(g):
        for k in GROUPS[g]:
            force_copy(k).start()

    each_group(forces_out)
    energy_out(2, energy_in(1))
    at_own = scattered[:, 256:320] - scattered[:, 320:384]
    for ph in range(2):
        if sizes[ph] > 1:
            energy_group(ph).wait_send()
    each_group(lambda g: ghost_group(g).wait_send())

    def forces_in(g):
        force_group(g).wait_recv()
        force_group(g).wait_send()

    each_group(forces_in)
    acc = jnp.zeros((8, 128), F32)
    for k in range(8):
        acc = acc + jnp.where(lane_group[0:8] == PLACE[7 - k] % 4, gbuf[PLACE[k]], 0.0)
    acc_low = acc - acc.astype(BF16).astype(F32)
    returned = dot_t(jnp.concatenate([acc, acc_low], axis=0).astype(BF16), st4)
    forces_ref[...] = -(at_own + returned[0:8] + returned[8:16])[0:3]

    total = energy_in(2)
    energy_ref[...] = jnp.sum(jnp.sum(total, axis=0, keepdims=True), axis=1, keepdims=True)
    energy_group(2).wait_send()


def solution(mesh):
    columns, rows = mesh.shape["gx"], mesh.shape["gy"]
    sizes = sizes_of(columns, rows)
    most = max(sizes)

    def per_device(positions, features, send_list, edge_src, edge_dst, edge_count, w_embed, w_env, w_update, w_out):
        def body(*refs):
            kernel(columns, rows, sizes, *refs)

        vmem = pl.BlockSpec(memory_space=pltpu.VMEM)
        anywhere = pl.BlockSpec(memory_space=pl.ANY)
        forces, energy = pl.pallas_call(
            body,
            out_shape=(jax.ShapeDtypeStruct((3, ATOMS), F32), jax.ShapeDtypeStruct((1, 1), F32)),
            in_specs=[anywhere] * 10,
            out_specs=(vmem, vmem),
            scratch_shapes=[
                pltpu.VMEM((3, ATOMS), F32),
                pltpu.VMEM((C, ATOMS), BF16),
                pltpu.VMEM((1, GHOST), jnp.int32),
                pltpu.VMEM((8, 128), jnp.int32),
                pltpu.VMEM((8, 128), jnp.int32),
                pltpu.VMEM((1, 1), jnp.int32),
                pltpu.VMEM((C, 2 * C + NB), F32),
                pltpu.VMEM((LAYERS, C, 3 * C), F32),
                pltpu.VMEM((LAYERS, C, 4 * C), F32),
                pltpu.VMEM((1, C), F32),
                pltpu.VMEM((17, 128), F32),
                pltpu.VMEM((8, 17, 128), F32),
                pltpu.VMEM((768, EDGES), BF16),
                pltpu.VMEM((512, EDGES), BF16),
                pltpu.VMEM((512, EDGES), BF16),
                pltpu.VMEM((256, EDGES), BF16),
                pltpu.VMEM((256, EDGES), BF16),
                pltpu.VMEM((16, EDGES), F32),
                pltpu.VMEM((2, C, EDGES), F32),
                pltpu.VMEM((2, C, EDGES), F32),
                pltpu.VMEM((C, EDGES), F32),
                pltpu.VMEM((NB, EDGES), F32),
                pltpu.VMEM((16, EDGES), BF16),
                pltpu.VMEM((2 * LAYERS, 192, 256), BF16),
                pltpu.VMEM((2 * LAYERS, C, 192), BF16),
                pltpu.VMEM((128, 768), BF16),
                pltpu.VMEM((256, 512), F32),
                pltpu.VMEM((8, TILE), F32),
                pltpu.VMEM((512, 256), BF16),
                pltpu.VMEM((512, 256), BF16),
                pltpu.VMEM((128, 512), BF16),
                pltpu.VMEM((2, 8, 128), F32),
                pltpu.VMEM((8, 8, 128), F32),
                pltpu.VMEM((3, most, 8, 128), F32),
                pltpu.SemaphoreType.DMA((10,)),
                pltpu.SemaphoreType.DMA((3,)),
                pltpu.SemaphoreType.DMA((3,)),
                pltpu.SemaphoreType.DMA((3,)),
                pltpu.SemaphoreType.DMA((3,)),
                pltpu.SemaphoreType.DMA((3,)),
                pltpu.SemaphoreType.DMA((3,)),
            ],
            compiler_params=pltpu.CompilerParams(
                collective_id=0, has_side_effects=True, vmem_limit_bytes=60 * 1024 * 1024
            ),
        )(
            positions, features, send_list.reshape(1, GHOST), edge_src.reshape(8, 128), edge_dst.reshape(8, 128),
            edge_count.reshape(1, 1), w_embed.T, w_env, jnp.swapaxes(w_update, 1, 2), w_out.reshape(1, C),
        )
        return forces, energy.reshape(())

    placed = (
        P(None, ("gx", "gy")), P(None, ("gx", "gy")), P(("gx", "gy")), P(("gx", "gy")), P(("gx", "gy")),
        P(("gx", "gy")), P(), P(), P(), P(),
    )
    return jax.shard_map(
        per_device, mesh=mesh, in_specs=placed, out_specs=(P(None, ("gx", "gy")), P()), check_vma=False
    )
```

```python
import math

import jax
import jax.numpy as jnp
from jax import lax
from jax.experimental import pallas as pl
from jax.experimental.pallas import tpu as pltpu
from jax.sharding import PartitionSpec as P

C = 64
NB = 8
LAYERS = 2
ATOMS = 64
GHOST = 32
EDGES = 1024
SCALE = 16 ** (-0.5)
OFFSETS = ((-1, -1), (-1, 0), (-1, 1), (0, -1), (0, 1), (1, -1), (1, 0), (1, 1))
GROUPS = ((0, 3, 5), (1, 6), (2, 4, 7))
SPANS = ((0, 3), (3, 5), (5, 8))
PLACE = (0, 3, 5, 1, 6, 2, 4, 7)
WIDTH = 6.0
CUTOFF = 5.0
F32 = jnp.float32
BF16 = jnp.bfloat16
MESH = pl.DeviceIdType.MESH
TILE = 256
CUT, LIVE, UX, UY, UZ, INV, DIST, GAIN, BEND, SLOPE, DCUT = 0, 1, 2, 3, 4, 5, 6, 7, 8, 9, 10


def split(x):
    hi = x.astype(BF16)
    return hi, (x - hi.astype(F32)).astype(BF16)


def split3(x):
    hi = x.astype(BF16)
    rest = x - hi.astype(F32)
    mid = rest.astype(BF16)
    return hi, mid, (rest - mid.astype(F32)).astype(BF16)


def dot(x, y):
    return lax.dot_general(x, y, (((1,), (0,)), ((), ())), preferred_element_type=F32)


def dot_t(x, y):
    return lax.dot_general(x, y, (((1,), (1,)), ((), ())), preferred_element_type=F32)


def pick_lane(tables, index):
    lane = index & 127
    which = index >> 7
    result = None
    for t, table in enumerate(tables):
        wide = jnp.broadcast_to(table, (8, 128))
        got = jnp.take_along_axis(wide, lane, axis=1, mode="promise_in_bounds")
        result = got if result is None else jnp.where(which == t, got, result)
    return result


def sizes_of(columns, rows):
    return (2 * rows, max(columns // 8, 1), min(4, columns // 2))


def kernel(
    columns, rows, sizes,
    pos_in, feat_in, send_in, src_in, dst_in, count_in, we_in, wv_in, wu_in, wo_in,
    forces_ref, energy_ref,
    pos_ref, feat_ref, send_ref, src_ref, dst_ref, count_ref, we_ref, wv_ref, wu_ref, wo_ref,
    pay, table, ah, al, oh, vh, vl, row, value, gain_cut, df, dradial_map, ddb, lhs, own_weights, flat, kept, folded,
    uth, utl, embs, gsrc, gbuf, ebuf,
    in_sem, send_sem, recv_sem, gsend_sem, grecv_sem, esend_sem, erecv_sem,
):
    a = lax.axis_index("gx")
    b = lax.axis_index("gy")

    def peer(k):
        dx, dy = OFFSETS[k]
        return (lax.rem(a + dx + columns, columns), b + dy)

    def group_of(k):
        return 1 + OFFSETS[k][1]

    def each_group(act, otherwise=None):
        act(1)
        for g, good in ((0, b > 0), (2, b < rows - 1)):
            pl.when(good)(lambda g=g: act(g))
            if otherwise is not None:
                pl.when(jnp.logical_not(good))(lambda g=g: otherwise(g))

    def member(ph):
        if ph == 0:
            return lax.rem(a, 2) * rows + b
        return a // 8 if ph == 1 else lax.rem(a // 2, sizes[2])

    def energy_peer(ph, t):
        me = member(ph)
        other = lax.rem(me + t, sizes[ph])
        if ph == 0:
            return (a - lax.rem(a, 2) + other // rows, lax.rem(other, rows))
        return (a + (8 if ph == 1 else 2) * (other - me), b)

    barrier = pltpu.get_barrier_semaphore()

    def greet(g):
        for k in GROUPS[g]:
            pl.semaphore_signal(barrier, inc=1, device_id=peer(k), device_id_type=MESH)

    each_group(greet)
    greeted = 0
    for ph in range(3):
        for t in range(1, sizes[ph]):
            pl.semaphore_signal(barrier, inc=1, device_id=energy_peer(ph, t), device_id_type=MESH)
            greeted += 1

    fetched = [
        pltpu.make_async_copy(given, held, in_sem.at[i])
        for i, (given, held) in enumerate([
            (pos_in, pos_ref), (feat_in, feat_ref), (send_in, send_ref), (we_in, we_ref), (src_in, src_ref),
            (dst_in, dst_ref), (count_in, count_ref), (wv_in, wv_ref), (wu_in, wu_ref), (wo_in, wo_ref)])
    ]
    for copy in fetched:
        copy.start()
    for copy in fetched[0:4]:
        copy.wait()

    we_hi, we_lo = split(we_ref[:, 0 : 2 * C])
    we_both = jnp.concatenate(
        [jnp.concatenate([we_hi[:, 0:C], we_lo[:, 0:C]], axis=1),
         jnp.concatenate([we_hi[:, C : 2 * C], we_lo[:, C : 2 * C]], axis=1)], axis=0)
    feat = feat_ref[...]
    own = dot(we_both, jnp.concatenate([feat, feat], axis=0))
    own_src, own_dst = own[0:C], own[C : 2 * C]
    pos = pos_ref[...]
    send4 = jnp.concatenate([send_ref[...]] * 4, axis=1)
    st4 = (lax.broadcasted_iota(jnp.int32, (ATOMS, 128), 0) == send4).astype(F32).astype(BF16)
    exported = jnp.concatenate([own_src, pos, jnp.zeros((61, ATOMS), F32)], axis=0)
    e3 = split3(jnp.concatenate([exported, jnp.zeros((128, 128 - ATOMS), F32)], axis=1))
    st4_tall = jnp.concatenate([st4, jnp.zeros((128 - ATOMS, 128), BF16)], axis=0)
    payload = (dot(e3[2], st4_tall) + dot(e3[1], st4_tall)) + dot(e3[0], st4_tall)
    lane_group = lax.broadcasted_iota(jnp.int32, (16, 128), 1) >> 5

    def by_group(parts):
        result = parts[0]
        for q in range(1, len(parts)):
            result = jnp.where(lane_group[0 : result.shape[0]] == q, parts[q], result)
        return result

    pay[0:16] = by_group([payload[16 * q : 16 * q + 16] for q in range(4)])
    pay[16:17] = by_group([payload[C + i : C + i + 1] for i in range(3)])

    inner = jnp.logical_and(b > 0, b < rows - 1)
    pl.semaphore_wait(barrier, greeted + jnp.where(inner, 8, 5))

    def ghost_copy(k):
        return pltpu.make_async_remote_copy(
            src_ref=pay, dst_ref=table.at[PLACE[7 - k]], send_sem=send_sem.at[group_of(k)],
            recv_sem=recv_sem.at[group_of(7 - k)], device_id=peer(k), device_id_type=MESH,
        )

    def ghost_group(g):
        held = table.at[pl.ds(SPANS[g][0], len(GROUPS[g]))]
        return pltpu.make_async_remote_copy(
            src_ref=held, dst_ref=held, send_sem=send_sem.at[g], recv_sem=recv_sem.at[g],
            device_id=peer(GROUPS[g][0]), device_id_type=MESH,
        )

    def ghosts_out(g):
        for k in GROUPS[g]:
            ghost_copy(k).start()

    each_group(ghosts_out)

    for copy in fetched[4:]:
        copy.wait()

    def put_row(i, v):
        for j in range(8):
            row[i : i + 1, 128 * j : 128 * (j + 1)] = v[j : j + 1, :]

    def loop(count, act):
        for i in range(count):
            act(i)

    def tiles(act):
        loop(EDGES // TILE, lambda n: act(slice(n * TILE, (n + 1) * TILE)))

    src = src_ref[...]
    dst = dst_ref[...]
    block = (src - ATOMS) >> 5
    ghost = src >= ATOMS
    ox = jnp.zeros((8, 128), F32)
    oy = jnp.zeros((8, 128), F32)
    block_place = jnp.zeros((8, 128), jnp.int32)
    for k, (dx, dy) in enumerate(OFFSETS):
        here = jnp.logical_and(ghost, block == k)
        if dx:
            ox = jnp.where(here, WIDTH * dx, ox)
        if dy:
            oy = jnp.where(here, WIDTH * dy, oy)
        block_place = jnp.where(here, PLACE[k], block_place)
    step_y = (oy * (1.0 / WIDTH)).astype(jnp.int32)
    reach = jnp.logical_and(b + step_y >= 0, b + step_y < rows)
    place = lax.broadcasted_iota(jnp.int32, (8, 128), 0) * 128 + lax.broadcasted_iota(jnp.int32, (8, 128), 1)
    live = jnp.where(jnp.logical_and(place < count_ref[0], reach), 1.0, 0.0)
    put_row(LIVE, live)
    slot = jnp.where(ghost, block_place * GHOST + (src & (GHOST - 1)), src + 8 * GHOST)
    def one_hot(j):
        lanes = slice(j * 128, (j + 1) * 128)
        oh[0:320, lanes] = (
            lax.broadcasted_iota(jnp.int32, (320, 128), 0) == slot[j : j + 1, :]).astype(F32).astype(BF16)
        hot = (lax.broadcasted_iota(jnp.int32, (ATOMS, 128), 0) == dst[j : j + 1, :]).astype(F32).astype(BF16)
        oh[320:384, lanes] = hot
        ah[512:576, lanes] = hot

    loop(8, one_hot)

    def four(x):
        hi, lo = split(x)
        return jnp.concatenate([hi, hi, lo, lo], axis=1)

    def weigh(stage):
        layer = min(stage, 3 - stage)
        for i, d in enumerate((1, 2, 0)):
            env_hi, env_lo = split(wv_ref[layer, :, d * C : (d + 1) * C])
            upd_hi, upd_lo = split(wu_ref[layer, :, (d + 1) * C : (d + 2) * C] * SCALE)
            env = [env_hi, env_lo, env_hi, env_lo]
            upd = [upd_hi, upd_hi, upd_lo, upd_lo]
            left, right = (upd, env) if stage < LAYERS else (env, upd)
            lhs[stage, 64 * i : 64 * (i + 1)] = four(
                dot_t(jnp.concatenate(left, axis=1), jnp.concatenate(right, axis=1)))
        own_w = wu_ref[layer, :, 0:C]
        hi, lo = split(own_w if stage < LAYERS else own_w.T)
        own_weights[stage] = jnp.concatenate([hi, hi, lo], axis=1)

    weigh(0)
    wrt = we_ref[:, 2 * C : 2 * C + NB]
    wr = jnp.concatenate([wrt, jnp.zeros((C, 128 - NB), F32)], axis=1).T[0:NB, :]
    wr_low = wr - wr.astype(BF16).astype(F32)
    wr4 = jnp.concatenate([wr, wr, wr_low, jnp.zeros((104, C), F32)], axis=0).T.astype(BF16)
    wr2 = jnp.concatenate([wr, wr_low], axis=0)
    wr2 = jnp.concatenate([wr2, wr2], axis=1).astype(BF16)
    diagonal = lax.broadcasted_iota(jnp.int32, (C, C), 0) == lax.broadcasted_iota(jnp.int32, (C, C), 1)
    wo = jnp.sum(jnp.where(diagonal, wo_ref[...], 0.0), axis=1, keepdims=True)

    def blank(g):
        for i in range(*SPANS[g]):
            table[i] = jnp.zeros((17, 128), F32)
            gbuf[i] = jnp.zeros((8, 128), F32)

    each_group(lambda g: ghost_group(g).wait_recv(), blank)

    def turned(x, groups):
        cut = 128 - 32 * (groups % 4)
        return x if groups % 4 == 0 else jnp.concatenate([x[:, cut:], x[:, :cut]], axis=1)

    channels, coords = [[], [], [], []], [[], [], []]
    for t in range(2):
        held = [table[4 * t + i] for i in range(4)]
        for q in range(4):
            around = [turned(held[i], i - q) for i in range(4)]
            channels[q].append(by_group([x[0:16] for x in around]))
            if q < 3:
                coords[q].append(by_group([x[16:17] for x in around]))
    ghosts = jnp.concatenate([jnp.concatenate(x, axis=1) for x in channels], axis=0)
    own_pos = jnp.concatenate([pos, jnp.zeros((3, 64), F32)], axis=1)
    diff = []
    for i in range(3):
        mine = own_pos[i : i + 1, :]
        at_src = pick_lane(coords[i] + [mine], slot)
        if i < 2:
            at_src = at_src + (ox, oy)[i]
        diff.append(at_src - pick_lane([mine], dst))
    dist = jnp.sqrt(diff[0] * diff[0] + diff[1] * diff[1] + diff[2] * diff[2] + 1.0)
    inv = 1.0 / dist
    ux, uy, uz = (v * inv for v in diff)
    root = math.sqrt(3.0)
    harm = [ux, uy, uz, root * ux * uy, root * uy * uz, 0.5 * (3.0 * uz * uz - 1.0), root * ux * uz,
            0.5 * root * (ux * ux - uy * uy)]
    short = jnp.maximum(1.0 - (dist * dist) * (1.0 / CUTOFF**2), 0.0)
    envelope = short * short
    gain = envelope * inv
    slope = (-4.0 / CUTOFF**2) * dist * short
    put_row(DIST, jnp.minimum(dist, CUTOFF) * (1.0 / CUTOFF))
    put_row(GAIN, gain)
    put_row(BEND, (slope - gain) * inv)
    put_row(CUT, live * envelope)
    put_row(SLOPE, live * slope)
    for i, v in ((UX, ux), (UY, uy), (UZ, uz), (INV, inv)):
        put_row(i, v)
    def map_edges(j):
        lanes = slice(j * 128, (j + 1) * 128)
        hot = ah[512:576, lanes]
        for m in range(8):
            high, low = split(jnp.broadcast_to(harm[m][j : j + 1, :], (16, 128)))
            ah[64 * m : 64 * (m + 1), lanes] = hot * jnp.concatenate([high] * 4, axis=0)
            al[64 * m : 64 * (m + 1), lanes] = hot * jnp.concatenate([low] * 4, axis=0)

    loop(8, map_edges)

    emb_hi, emb_lo = split(jnp.concatenate([ghosts, own_src, own_dst], axis=1))
    embs[...] = jnp.concatenate(
        [jnp.concatenate([emb_hi, wr4], axis=1), jnp.concatenate([emb_lo, jnp.zeros((C, 128), BF16)], axis=1)], axis=0)
    order = (lax.broadcasted_iota(jnp.int32, (NB, TILE), 0) + 1).astype(F32)

    def keep(lanes, place, x):
        hi, lo = split(x)
        vh[place : place + C, lanes] = hi
        vl[place : place + C, lanes] = lo
        ah[576:640, lanes] = hi
        ah[640:704, lanes] = lo
        ah[704:768, lanes] = hi

    def activate(lanes, stage, q):
        s = 1.0 / (1.0 + jnp.exp(-q))
        v = q * s
        cut = row[CUT : CUT + 1, lanes]
        value[stage, :, lanes] = v
        gain_cut[stage, :, lanes] = (s + v * (1.0 - s)) * cut
        return v * cut

    def embed(lanes):
        turns = order * row[DIST : DIST + 1, lanes]
        whole = jnp.floor(turns + 0.5)
        angle = (turns - whole) * math.pi
        sign = 1.0 - 2.0 * (whole - 2.0 * jnp.floor(whole * 0.5))
        sq = angle * angle
        sine = 1.0 / 39916800.0
        for c in (-1.0 / 362880.0, 1.0 / 5040.0, -1.0 / 120.0, 1.0 / 6.0, -1.0):
            sine = c + sq * sine
        sine = -(angle * sine) * sign
        cosine = 1.0 / 479001600.0
        for c in (-1.0 / 3628800.0, 1.0 / 40320.0, -1.0 / 720.0, 1.0 / 24.0, -0.5, 1.0):
            cosine = c + sq * cosine
        cosine = cosine * sign
        near = row[GAIN : GAIN + 1, lanes]
        radial = sine * near
        dradial_map[:, lanes] = order * (math.pi / CUTOFF) * cosine * near + sine * row[BEND : BEND + 1, lanes]
        low = radial - radial.astype(BF16).astype(F32)
        oh[384:512, lanes] = jnp.concatenate([radial, low, radial, jnp.zeros((104, TILE), F32)], axis=0).astype(BF16)
        both = dot(embs[...], oh[:, lanes])
        f = activate(lanes, 0, both[0:C] + both[C : 2 * C])
        df[:, lanes] = f
        keep(lanes, 192, f)

    degree = lax.broadcasted_iota(jnp.int32, (C, 512), 1) >= 192

    def mix(stage, place):
        sums = dot_t(ah[576:704, :], ah[0:576, :])
        sums = sums[0:C] + sums[C : 2 * C]
        hi, lo = split(sums[:, 0:512] + dot_t(ah[576:640, :], al[...]))
        every = dot(lhs[stage, 0:128], jnp.concatenate([hi, lo, hi, lo], axis=0))
        outer = jnp.where(degree, every[C : 2 * C], every[0:C])
        kept[place : place + C, :] = outer
        hi, lo = split(sums[:, 512:576])
        inner = dot(lhs[stage, 128:192], jnp.concatenate([hi, lo, hi, lo], axis=0))
        hi, lo = split(outer)
        flat[0:C, 0:512] = hi
        flat[C : 2 * C, 0:512] = lo
        hi, lo = split(inner)
        flat[0:C, 512:768] = jnp.concatenate([hi, own_weights[stage]], axis=1)
        flat[C : 2 * C, 512:768] = jnp.concatenate([lo, jnp.zeros((C, 192), BF16)], axis=1)

    def spread(lanes):
        both = dot(flat[...], ah[:, lanes])
        return both[0:C] + both[C : 2 * C] + dot(flat[0:C, 0:512], al[:, lanes])

    def back_map(place):
        hi, lo = split(kept[place : place + 128, :].T)
        uth[:, place : place + 128] = hi
        utl[:, place : place + 128] = lo

    def energy_out(ph, x):
        me = member(ph)
        ebuf[ph, me] = x
        for t in range(1, sizes[ph]):
            pltpu.make_async_remote_copy(
                src_ref=ebuf.at[ph, me], dst_ref=ebuf.at[ph, me], send_sem=esend_sem.at[ph], recv_sem=erecv_sem.at[ph],
                device_id=energy_peer(ph, t), device_id_type=MESH,
            ).start()

    def energy_group(ph):
        held = ebuf.at[ph, pl.ds(0, sizes[ph] - 1)]
        return pltpu.make_async_remote_copy(
            src_ref=held, dst_ref=held, send_sem=esend_sem.at[ph], recv_sem=erecv_sem.at[ph],
            device_id=energy_peer(ph, 1), device_id_type=MESH,
        )

    def energy_in(ph):
        if sizes[ph] > 1:
            energy_group(ph).wait_recv()
        total = ebuf[ph, 0]
        for t in range(1, sizes[ph]):
            total = total + ebuf[ph, t]
        return total

    weigh(1)
    tiles(embed)

    def first_layer(lanes):
        f = df[:, lanes] + activate(lanes, 1, spread(lanes))
        df[:, lanes] = f
        keep(lanes, 64, f)

    folded[...] = jnp.zeros((8, TILE), F32)

    def turn(lanes):
        q = spread(lanes)
        s = 1.0 / (1.0 + jnp.exp(-q))
        v = q * s
        cut = row[CUT : CUT + 1, lanes]
        f = df[:, lanes] + v * cut
        g = wo * row[LIVE : LIVE + 1, lanes]
        per_edge = f * g
        piece = per_edge[0:8]
        for i in range(1, 8):
            piece = piece + per_edge[8 * i : 8 * i + 8]
        folded[...] += piece
        df[:, lanes] = g
        row[DCUT : DCUT + 1, lanes] = jnp.sum(g * v, axis=0, keepdims=True)
        keep(lanes, 0, g * ((s + v * (1.0 - s)) * cut))

    def back_first(lanes):
        g = df[:, lanes] + spread(lanes)
        df[:, lanes] = g
        row[DCUT : DCUT + 1, lanes] += jnp.sum(g * value[1, :, lanes], axis=0, keepdims=True)
        keep(lanes, 128, g * gain_cut[1, :, lanes])

    mix(0, 128)
    weigh(2)
    tiles(first_layer)
    mix(1, 0)
    weigh(3)
    tiles(turn)
    energy_out(0, folded[:, 0:128] + folded[:, 128:256])
    mix(2, 64)
    tiles(back_first)
    back_map(0)
    mix(3, 192)
    back_map(128)
    energy_out(1, energy_in(0))

    def back_embed(lanes):
        g = df[:, lanes] + spread(lanes)
        dcut = row[DCUT : DCUT + 1, lanes] + jnp.sum(g * value[0, :, lanes], axis=0, keepdims=True)
        both = dot(wr2, jnp.concatenate(split(g * gain_cut[0, :, lanes]), axis=0))
        dr = jnp.sum((both[0:8] + both[8:16]) * dradial_map[:, lanes], axis=0, keepdims=True)
        dr = dr + dcut * row[SLOPE : SLOPE + 1, lanes]
        right = vh[:, lanes]
        part = dot(uth[...], right) + dot(utl[...], right) + dot(uth[...], vl[:, lanes])
        hot = ah[512:576, lanes].astype(F32)
        g = [jnp.sum(hot * part[64 * m : 64 * (m + 1)], axis=0, keepdims=True) for m in range(8)]
        xr, yr, zr, ir = (row[i : i + 1, lanes] for i in (UX, UY, UZ, INV))
        dux = g[0] + root * (g[3] * yr + g[6] * zr + g[7] * xr)
        duy = g[1] + root * (g[3] * xr + g[4] * zr - g[7] * yr)
        duz = g[2] + root * (g[4] * yr + g[6] * xr) + 3.0 * g[5] * zr
        along = dr - (dux * xr + duy * yr + duz * zr) * ir
        dd = jnp.concatenate(
            [dux * ir + along * xr, duy * ir + along * yr, duz * ir + along * zr, jnp.zeros((5, TILE), F32)], axis=0)
        ddb[:, lanes] = jnp.concatenate([dd, dd - dd.astype(BF16).astype(F32)], axis=0).astype(BF16)

    tiles(back_embed)
    scattered = dot_t(ddb[...], oh[0:384, :])
    scattered = scattered[0:8] + scattered[8:16]
    gsrc[0] = scattered[:, 0:128]
    gsrc[1] = scattered[:, 128:256]
    def force_copy(k):
        return pltpu.make_async_remote_copy(
            src_ref=gsrc.at[PLACE[k] // 4], dst_ref=gbuf.at[PLACE[7 - k]], send_sem=gsend_sem.at[group_of(k)],
            recv_sem=grecv_sem.at[group_of(7 - k)], device_id=peer(k), device_id_type=MESH,
        )

    def force_group(g):
        held = gbuf.at[pl.ds(SPANS[g][0], len(GROUPS[g]))]
        return pltpu.make_async_remote_copy(
            src_ref=held, dst_ref=held, send_sem=gsend_sem.at[g], recv_sem=grecv_sem.at[g],
            device_id=peer(GROUPS[g][0]), device_id_type=MESH,
        )

    def forces_out(g):
        for k in GROUPS[g]:
            force_copy(k).start()

    each_group(forces_out)
    energy_out(2, energy_in(1))
    at_own = scattered[:, 256:320] - scattered[:, 320:384]
    for ph in range(2):
        if sizes[ph] > 1:
            energy_group(ph).wait_send()
    each_group(lambda g: ghost_group(g).wait_send())

    def forces_in(g):
        force_group(g).wait_recv()
        force_group(g).wait_send()

    each_group(forces_in)
    acc = jnp.zeros((8, 128), F32)
    for k in range(8):
        acc = acc + jnp.where(lane_group[0:8] == PLACE[7 - k] % 4, gbuf[PLACE[k]], 0.0)
    acc_low = acc - acc.astype(BF16).astype(F32)
    returned = dot_t(jnp.concatenate([acc, acc_low], axis=0).astype(BF16), st4)
    forces_ref[...] = -(at_own + returned[0:8] + returned[8:16])[0:3]

    total = energy_in(2)
    energy_ref[...] = jnp.sum(total, axis=0, keepdims=True)
    energy_group(2).wait_send()


def solution(mesh):
    columns, rows = mesh.shape["gx"], mesh.shape["gy"]
    sizes = sizes_of(columns, rows)
    most = max(sizes)

    def per_device(positions, features, send_list, edge_src, edge_dst, edge_count, w_embed, w_env, w_update, w_out):
        def body(*refs):
            kernel(columns, rows, sizes, *refs)

        vmem = pl.BlockSpec(memory_space=pltpu.VMEM)
        anywhere = pl.BlockSpec(memory_space=pl.ANY)
        forces, energy = pl.pallas_call(
            body,
            out_shape=(jax.ShapeDtypeStruct((3, ATOMS), F32), jax.ShapeDtypeStruct((1, 128), F32)),
            in_specs=[anywhere] * 10,
            out_specs=(vmem, vmem),
            scratch_shapes=[
                pltpu.VMEM((3, ATOMS), F32),
                pltpu.VMEM((C, ATOMS), BF16),
                pltpu.VMEM((1, GHOST), jnp.int32),
                pltpu.VMEM((8, 128), jnp.int32),
                pltpu.VMEM((8, 128), jnp.int32),
                pltpu.SMEM((1,), jnp.int32),
                pltpu.VMEM((C, 2 * C + NB), F32),
                pltpu.VMEM((LAYERS, C, 3 * C), F32),
                pltpu.VMEM((LAYERS, C, 4 * C), F32),
                pltpu.VMEM((1, C), F32),
                pltpu.VMEM((17, 128), F32),
                pltpu.VMEM((8, 17, 128), F32),
                pltpu.VMEM((768, EDGES), BF16),
                pltpu.VMEM((512, EDGES), BF16),
                pltpu.VMEM((512, EDGES), BF16),
                pltpu.VMEM((256, EDGES), BF16),
                pltpu.VMEM((256, EDGES), BF16),
                pltpu.VMEM((16, EDGES), F32),
                pltpu.VMEM((2, C, EDGES), F32),
                pltpu.VMEM((2, C, EDGES), F32),
                pltpu.VMEM((C, EDGES), F32),
                pltpu.VMEM((NB, EDGES), F32),
                pltpu.VMEM((16, EDGES), BF16),
                pltpu.VMEM((2 * LAYERS, 192, 256), BF16),
                pltpu.VMEM((2 * LAYERS, C, 192), BF16),
                pltpu.VMEM((128, 768), BF16),
                pltpu.VMEM((256, 512), F32),
                pltpu.VMEM((8, TILE), F32),
                pltpu.VMEM((512, 256), BF16),
                pltpu.VMEM((512, 256), BF16),
                pltpu.VMEM((128, 512), BF16),
                pltpu.VMEM((2, 8, 128), F32),
                pltpu.VMEM((8, 8, 128), F32),
                pltpu.VMEM((3, most, 8, 128), F32),
                pltpu.SemaphoreType.DMA((10,)),
                pltpu.SemaphoreType.DMA((3,)),
                pltpu.SemaphoreType.DMA((3,)),
                pltpu.SemaphoreType.DMA((3,)),
                pltpu.SemaphoreType.DMA((3,)),
                pltpu.SemaphoreType.DMA((3,)),
                pltpu.SemaphoreType.DMA((3,)),
            ],
            compiler_params=pltpu.CompilerParams(
                collective_id=0, has_side_effects=True, vmem_limit_bytes=60 * 1024 * 1024
            ),
        )(
            positions, features, send_list.reshape(1, GHOST), edge_src.reshape(8, 128), edge_dst.reshape(8, 128),
            edge_count, w_embed.T, w_env, jnp.swapaxes(w_update, 1, 2), w_out.reshape(1, C),
        )
        return forces, jnp.sum(energy)

    placed = (
        P(None, ("gx", "gy")), P(None, ("gx", "gy")), P(("gx", "gy")), P(("gx", "gy")), P(("gx", "gy")),
        P(("gx", "gy")), P(), P(), P(), P(),
    )
    return jax.shard_map(
        per_device, mesh=mesh, in_specs=placed, out_specs=(P(None, ("gx", "gy")), P()), check_vma=False
    )
```

```python
import math

import jax
import jax.numpy as jnp
from jax import lax
from jax.experimental import pallas as pl
from jax.experimental.pallas import tpu as pltpu
from jax.sharding import PartitionSpec as P

C = 64
NB = 8
LAYERS = 2
ATOMS = 64
GHOST = 32
EDGES = 1024
SCALE = 16 ** (-0.5)
OFFSETS = ((-1, -1), (-1, 0), (-1, 1), (0, -1), (0, 1), (1, -1), (1, 0), (1, 1))
GROUPS = ((0, 3, 5), (1, 6), (2, 4, 7))
SPANS = ((0, 3), (3, 5), (5, 8))
PLACE = (0, 3, 5, 1, 6, 2, 4, 7)
WIDTH = 6.0
CUTOFF = 5.0
F32 = jnp.float32
BF16 = jnp.bfloat16
MESH = pl.DeviceIdType.MESH
TILE = 256
CUT, LIVE, UX, UY, UZ, INV, DIST, GAIN, BEND, SLOPE, DCUT = 0, 1, 2, 3, 4, 5, 6, 7, 8, 9, 10


def split(x):
    hi = x.astype(BF16)
    return hi, (x - hi.astype(F32)).astype(BF16)


def split3(x):
    hi = x.astype(BF16)
    rest = x - hi.astype(F32)
    mid = rest.astype(BF16)
    return hi, mid, (rest - mid.astype(F32)).astype(BF16)


def dot(x, y):
    return lax.dot_general(x, y, (((1,), (0,)), ((), ())), preferred_element_type=F32)


def dot_t(x, y):
    return lax.dot_general(x, y, (((1,), (1,)), ((), ())), preferred_element_type=F32)


def pick_lane(tables, index):
    lane = index & 127
    which = index >> 7
    result = None
    for t, table in enumerate(tables):
        wide = jnp.broadcast_to(table, (8, 128))
        got = jnp.take_along_axis(wide, lane, axis=1, mode="promise_in_bounds")
        result = got if result is None else jnp.where(which == t, got, result)
    return result


def sizes_of(columns, rows):
    return (2 * rows, max(columns // 8, 1), min(4, columns // 2))


def kernel(
    columns, rows, sizes,
    pos_in, feat_in, send_in, src_in, dst_in, count_in, we_in, wv_in, wu_in, wo_in,
    forces_ref, energy_ref,
    pos_ref, feat_ref, send_ref, src_ref, dst_ref, count_ref, we_ref, wv_ref, wu_ref, wo_ref,
    pay, table, ah, al, oh, vh, vl, row, value, gain_cut, df, dradial_map, ddb, lhs, own_weights, flat, kept, folded,
    uth, utl, embs, gsrc, gbuf, ebuf,
    in_sem, send_sem, recv_sem, gsend_sem, grecv_sem, esend_sem, erecv_sem,
):
    a = lax.axis_index("gx")
    b = lax.axis_index("gy")

    def peer(k):
        dx, dy = OFFSETS[k]
        return (lax.rem(a + dx + columns, columns), b + dy)

    def group_of(k):
        return 1 + OFFSETS[k][1]

    def each_group(act, otherwise=None):
        act(1)
        for g, good in ((0, b > 0), (2, b < rows - 1)):
            pl.when(good)(lambda g=g: act(g))
            if otherwise is not None:
                pl.when(jnp.logical_not(good))(lambda g=g: otherwise(g))

    def member(ph):
        if ph == 0:
            return lax.rem(a, 2) * rows + b
        return a // 8 if ph == 1 else lax.rem(a // 2, sizes[2])

    def energy_peer(ph, t):
        me = member(ph)
        other = lax.rem(me + t, sizes[ph])
        if ph == 0:
            return (a - lax.rem(a, 2) + other // rows, lax.rem(other, rows))
        return (a + (8 if ph == 1 else 2) * (other - me), b)

    barrier = pltpu.get_barrier_semaphore()

    def greet(g):
        for k in GROUPS[g]:
            pl.semaphore_signal(barrier, inc=1, device_id=peer(k), device_id_type=MESH)

    each_group(greet)
    greeted = 0
    for ph in range(3):
        for t in range(1, sizes[ph]):
            pl.semaphore_signal(barrier, inc=1, device_id=energy_peer(ph, t), device_id_type=MESH)
            greeted += 1

    fetched = [
        pltpu.make_async_copy(given, held, in_sem.at[i])
        for i, (given, held) in enumerate([
            (pos_in, pos_ref), (feat_in, feat_ref), (send_in, send_ref), (we_in, we_ref), (src_in, src_ref),
            (dst_in, dst_ref), (count_in, count_ref), (wv_in, wv_ref), (wu_in, wu_ref), (wo_in, wo_ref)])
    ]
    for copy in fetched:
        copy.start()
    for copy in fetched[0:4]:
        copy.wait()

    we_hi, we_lo = split(we_ref[:, 0 : 2 * C])
    we_both = jnp.concatenate(
        [jnp.concatenate([we_hi[:, 0:C], we_lo[:, 0:C]], axis=1),
         jnp.concatenate([we_hi[:, C : 2 * C], we_lo[:, C : 2 * C]], axis=1)], axis=0)
    feat = feat_ref[...]
    own = dot(we_both, jnp.concatenate([feat, feat], axis=0))
    own_src, own_dst = own[0:C], own[C : 2 * C]
    pos = pos_ref[...]
    send4 = jnp.concatenate([send_ref[...]] * 4, axis=1)
    st4 = (lax.broadcasted_iota(jnp.int32, (ATOMS, 128), 0) == send4).astype(F32).astype(BF16)
    exported = jnp.concatenate([own_src, pos, jnp.zeros((61, ATOMS), F32)], axis=0)
    e3 = split3(jnp.concatenate([exported, jnp.zeros((128, 128 - ATOMS), F32)], axis=1))
    st4_tall = jnp.concatenate([st4, jnp.zeros((128 - ATOMS, 128), BF16)], axis=0)
    payload = (dot(e3[2], st4_tall) + dot(e3[1], st4_tall)) + dot(e3[0], st4_tall)
    lane_group = lax.broadcasted_iota(jnp.int32, (16, 128), 1) >> 5

    def by_group(parts):
        result = parts[0]
        for q in range(1, len(parts)):
            result = jnp.where(lane_group[0 : result.shape[0]] == q, parts[q], result)
        return result

    pay[0:16] = by_group([payload[16 * q : 16 * q + 16] for q in range(4)])
    pay[16:17] = by_group([payload[C + i : C + i + 1] for i in range(3)])

    inner = jnp.logical_and(b > 0, b < rows - 1)
    pl.semaphore_wait(barrier, greeted + jnp.where(inner, 8, 5))

    def ghost_copy(k):
        return pltpu.make_async_remote_copy(
            src_ref=pay, dst_ref=table.at[PLACE[7 - k]], send_sem=send_sem.at[group_of(k)],
            recv_sem=recv_sem.at[group_of(7 - k)], device_id=peer(k), device_id_type=MESH,
        )

    def ghost_group(g):
        held = table.at[pl.ds(SPANS[g][0], len(GROUPS[g]))]
        return pltpu.make_async_remote_copy(
            src_ref=held, dst_ref=held, send_sem=send_sem.at[g], recv_sem=recv_sem.at[g],
            device_id=peer(GROUPS[g][0]), device_id_type=MESH,
        )

    def ghosts_out(g):
        for k in GROUPS[g]:
            ghost_copy(k).start()

    each_group(ghosts_out)

    for copy in fetched[4:]:
        copy.wait()

    def put_row(i, v):
        for j in range(8):
            row[i : i + 1, 128 * j : 128 * (j + 1)] = v[j : j + 1, :]

    def loop(count, act):
        for i in range(count):
            act(i)

    def tiles(act):
        loop(EDGES // TILE, lambda n: act(slice(n * TILE, (n + 1) * TILE)))

    src = src_ref[...]
    dst = dst_ref[...]
    block = (src - ATOMS) >> 5
    ghost = src >= ATOMS
    ox = jnp.zeros((8, 128), F32)
    oy = jnp.zeros((8, 128), F32)
    block_place = jnp.zeros((8, 128), jnp.int32)
    for k, (dx, dy) in enumerate(OFFSETS):
        here = jnp.logical_and(ghost, block == k)
        if dx:
            ox = jnp.where(here, WIDTH * dx, ox)
        if dy:
            oy = jnp.where(here, WIDTH * dy, oy)
        block_place = jnp.where(here, PLACE[k], block_place)
    step_y = (oy * (1.0 / WIDTH)).astype(jnp.int32)
    reach = jnp.logical_and(b + step_y >= 0, b + step_y < rows)
    place = lax.broadcasted_iota(jnp.int32, (8, 128), 0) * 128 + lax.broadcasted_iota(jnp.int32, (8, 128), 1)
    live = jnp.where(jnp.logical_and(place < count_ref[0], reach), 1.0, 0.0)
    put_row(LIVE, live)
    slot = jnp.where(ghost, block_place * GHOST + (src & (GHOST - 1)), src + 8 * GHOST)
    def one_hot(j):
        lanes = slice(j * 128, (j + 1) * 128)
        oh[0:320, lanes] = (
            lax.broadcasted_iota(jnp.int32, (320, 128), 0) == slot[j : j + 1, :]).astype(F32).astype(BF16)
        hot = (lax.broadcasted_iota(jnp.int32, (ATOMS, 128), 0) == dst[j : j + 1, :]).astype(F32).astype(BF16)
        oh[320:384, lanes] = hot
        ah[512:576, lanes] = hot

    loop(8, one_hot)

    def four(x):
        hi, lo = split(x)
        return jnp.concatenate([hi, hi, lo, lo], axis=1)

    def weigh(stage):
        layer = min(stage, 3 - stage)
        for i, d in enumerate((1, 2, 0)):
            env_hi, env_lo = split(wv_ref[layer, :, d * C : (d + 1) * C])
            upd_hi, upd_lo = split(wu_ref[layer, :, (d + 1) * C : (d + 2) * C] * SCALE)
            env = [env_hi, env_lo, env_hi, env_lo]
            upd = [upd_hi, upd_hi, upd_lo, upd_lo]
            left, right = (upd, env) if stage < LAYERS else (env, upd)
            lhs[stage, 64 * i : 64 * (i + 1)] = four(
                dot_t(jnp.concatenate(left, axis=1), jnp.concatenate(right, axis=1)))
        own_w = wu_ref[layer, :, 0:C]
        hi, lo = split(own_w if stage < LAYERS else own_w.T)
        own_weights[stage] = jnp.concatenate([hi, hi, lo], axis=1)

    weigh(0)
    wrt = we_ref[:, 2 * C : 2 * C + NB]
    wr = jnp.concatenate([wrt, jnp.zeros((C, 128 - NB), F32)], axis=1).T[0:NB, :]
    wr_low = wr - wr.astype(BF16).astype(F32)
    wr4 = jnp.concatenate([wr, wr, wr_low, jnp.zeros((104, C), F32)], axis=0).T.astype(BF16)
    wr2 = jnp.concatenate([wr, wr_low], axis=0)
    wr2 = jnp.concatenate([wr2, wr2], axis=1).astype(BF16)
    diagonal = lax.broadcasted_iota(jnp.int32, (C, C), 0) == lax.broadcasted_iota(jnp.int32, (C, C), 1)
    wo = jnp.sum(jnp.where(diagonal, wo_ref[...], 0.0), axis=1, keepdims=True)

    def blank(g):
        for i in range(*SPANS[g]):
            table[i] = jnp.zeros((17, 128), F32)
            gbuf[i] = jnp.zeros((8, 128), F32)

    each_group(lambda g: ghost_group(g).wait_recv(), blank)

    def turned(x, groups):
        cut = 128 - 32 * (groups % 4)
        return x if groups % 4 == 0 else jnp.concatenate([x[:, cut:], x[:, :cut]], axis=1)

    channels, coords = [[], [], [], []], [[], [], []]
    for t in range(2):
        held = [table[4 * t + i] for i in range(4)]
        for q in range(4):
            around = [turned(held[i], i - q) for i in range(4)]
            channels[q].append(by_group([x[0:16] for x in around]))
            if q < 3:
                coords[q].append(by_group([x[16:17] for x in around]))
    ghosts = jnp.concatenate([jnp.concatenate(x, axis=1) for x in channels], axis=0)
    own_pos = jnp.concatenate([pos, jnp.zeros((3, 64), F32)], axis=1)
    diff = []
    for i in range(3):
        mine = own_pos[i : i + 1, :]
        at_src = pick_lane(coords[i] + [mine], slot)
        if i < 2:
            at_src = at_src + (ox, oy)[i]
        diff.append(at_src - pick_lane([mine], dst))
    dist = jnp.sqrt(diff[0] * diff[0] + diff[1] * diff[1] + diff[2] * diff[2] + 1.0)
    inv = 1.0 / dist
    ux, uy, uz = (v * inv for v in diff)
    root = math.sqrt(3.0)
    harm = [ux, uy, uz, root * ux * uy, root * uy * uz, 0.5 * (3.0 * uz * uz - 1.0), root * ux * uz,
            0.5 * root * (ux * ux - uy * uy)]
    short = jnp.maximum(1.0 - (dist * dist) * (1.0 / CUTOFF**2), 0.0)
    envelope = short * short
    gain = envelope * inv
    slope = (-4.0 / CUTOFF**2) * dist * short
    put_row(DIST, jnp.minimum(dist, CUTOFF) * (1.0 / CUTOFF))
    put_row(GAIN, gain)
    put_row(BEND, (slope - gain) * inv)
    put_row(CUT, live * envelope)
    put_row(SLOPE, live * slope)
    for i, v in ((UX, ux), (UY, uy), (UZ, uz), (INV, inv)):
        put_row(i, v)
    def map_edges(j):
        lanes = slice(j * 128, (j + 1) * 128)
        hot = ah[512:576, lanes]
        for m in range(8):
            high, low = split(jnp.broadcast_to(harm[m][j : j + 1, :], (16, 128)))
            ah[64 * m : 64 * (m + 1), lanes] = hot * jnp.concatenate([high] * 4, axis=0)
            al[64 * m : 64 * (m + 1), lanes] = hot * jnp.concatenate([low] * 4, axis=0)

    loop(8, map_edges)

    emb_hi, emb_lo = split(jnp.concatenate([ghosts, own_src, own_dst], axis=1))
    embs[...] = jnp.concatenate(
        [jnp.concatenate([emb_hi, wr4], axis=1), jnp.concatenate([emb_lo, jnp.zeros((C, 128), BF16)], axis=1)], axis=0)
    order = (lax.broadcasted_iota(jnp.int32, (NB, TILE), 0) + 1).astype(F32)

    def keep(lanes, place, x):
        hi, lo = split(x)
        vh[place : place + C, lanes] = hi
        vl[place : place + C, lanes] = lo
        ah[576:640, lanes] = hi
        ah[640:704, lanes] = lo
        ah[704:768, lanes] = hi

    def activate(lanes, stage, q):
        s = 1.0 / (1.0 + jnp.exp(-q))
        v = q * s
        cut = row[CUT : CUT + 1, lanes]
        value[stage, :, lanes] = v
        gain_cut[stage, :, lanes] = (s + v * (1.0 - s)) * cut
        return v * cut

    def embed(lanes):
        turns = order * row[DIST : DIST + 1, lanes]
        whole = jnp.floor(turns + 0.5)
        angle = (turns - whole) * math.pi
        sign = 1.0 - 2.0 * (whole - 2.0 * jnp.floor(whole * 0.5))
        sq = angle * angle
        sine = 1.0 / 39916800.0
        for c in (-1.0 / 362880.0, 1.0 / 5040.0, -1.0 / 120.0, 1.0 / 6.0, -1.0):
            sine = c + sq * sine
        sine = -(angle * sine) * sign
        cosine = 1.0 / 479001600.0
        for c in (-1.0 / 3628800.0, 1.0 / 40320.0, -1.0 / 720.0, 1.0 / 24.0, -0.5, 1.0):
            cosine = c + sq * cosine
        cosine = cosine * sign
        near = row[GAIN : GAIN + 1, lanes]
        radial = sine * near
        dradial_map[:, lanes] = order * (math.pi / CUTOFF) * cosine * near + sine * row[BEND : BEND + 1, lanes]
        low = radial - radial.astype(BF16).astype(F32)
        oh[384:512, lanes] = jnp.concatenate([radial, low, radial, jnp.zeros((104, TILE), F32)], axis=0).astype(BF16)
        both = dot(embs[...], oh[:, lanes])
        f = activate(lanes, 0, both[0:C] + both[C : 2 * C])
        df[:, lanes] = f
        keep(lanes, 192, f)

    degree = lax.broadcasted_iota(jnp.int32, (C, 512), 1) >= 192

    def mix(stage, place):
        sums = dot_t(ah[576:704, :], ah[0:576, :])
        sums = sums[0:C] + sums[C : 2 * C]
        hi, lo = split(sums[:, 0:512] + dot_t(ah[576:640, :], al[...]))
        every = dot(lhs[stage, 0:128], jnp.concatenate([hi, lo, hi, lo], axis=0))
        outer = jnp.where(degree, every[C : 2 * C], every[0:C])
        kept[place : place + C, :] = outer
        hi, lo = split(sums[:, 512:576])
        inner = dot(lhs[stage, 128:192], jnp.concatenate([hi, lo, hi, lo], axis=0))
        hi, lo = split(outer)
        flat[0:C, 0:512] = hi
        flat[C : 2 * C, 0:512] = lo
        hi, lo = split(inner)
        flat[0:C, 512:768] = jnp.concatenate([hi, own_weights[stage]], axis=1)
        flat[C : 2 * C, 512:768] = jnp.concatenate([lo, jnp.zeros((C, 192), BF16)], axis=1)

    def spread(lanes):
        both = dot(flat[...], ah[:, lanes])
        return both[0:C] + both[C : 2 * C] + dot(flat[0:C, 0:512], al[:, lanes])

    def back_map(place):
        hi, lo = split(kept[place : place + 128, :].T)
        uth[:, place : place + 128] = hi
        utl[:, place : place + 128] = lo

    def energy_out(ph, x):
        me = member(ph)
        ebuf[ph, me] = x
        for t in range(1, sizes[ph]):
            pltpu.make_async_remote_copy(
                src_ref=ebuf.at[ph, me], dst_ref=ebuf.at[ph, me], send_sem=esend_sem.at[ph], recv_sem=erecv_sem.at[ph],
                device_id=energy_peer(ph, t), device_id_type=MESH,
            ).start()

    def energy_group(ph):
        held = ebuf.at[ph, pl.ds(0, sizes[ph] - 1)]
        return pltpu.make_async_remote_copy(
            src_ref=held, dst_ref=held, send_sem=esend_sem.at[ph], recv_sem=erecv_sem.at[ph],
            device_id=energy_peer(ph, 1), device_id_type=MESH,
        )

    def energy_in(ph):
        if sizes[ph] > 1:
            energy_group(ph).wait_recv()
        total = ebuf[ph, 0]
        for t in range(1, sizes[ph]):
            total = total + ebuf[ph, t]
        return total

    weigh(1)
    tiles(embed)

    def first_layer(lanes):
        f = df[:, lanes] + activate(lanes, 1, spread(lanes))
        df[:, lanes] = f
        keep(lanes, 64, f)

    folded[...] = jnp.zeros((8, TILE), F32)

    def turn(lanes):
        q = spread(lanes)
        s = 1.0 / (1.0 + jnp.exp(-q))
        v = q * s
        cut = row[CUT : CUT + 1, lanes]
        f = df[:, lanes] + v * cut
        g = wo * row[LIVE : LIVE + 1, lanes]
        per_edge = f * g
        piece = per_edge[0:8]
        for i in range(1, 8):
            piece = piece + per_edge[8 * i : 8 * i + 8]
        folded[...] += piece
        df[:, lanes] = g
        row[DCUT : DCUT + 1, lanes] = jnp.sum(g * v, axis=0, keepdims=True)
        keep(lanes, 0, g * ((s + v * (1.0 - s)) * cut))

    def back_first(lanes):
        g = df[:, lanes] + spread(lanes)
        df[:, lanes] = g
        row[DCUT : DCUT + 1, lanes] += jnp.sum(g * value[1, :, lanes], axis=0, keepdims=True)
        keep(lanes, 128, g * gain_cut[1, :, lanes])

    mix(0, 128)
    weigh(2)
    tiles(first_layer)
    mix(1, 0)
    weigh(3)
    tiles(turn)
    energy_out(0, folded[:, 0:128] + folded[:, 128:256])
    mix(2, 64)
    tiles(back_first)
    back_map(0)
    mix(3, 192)
    back_map(128)
    energy_out(1, energy_in(0))

    def back_embed(lanes):
        g = df[:, lanes] + spread(lanes)
        dcut = row[DCUT : DCUT + 1, lanes] + jnp.sum(g * value[0, :, lanes], axis=0, keepdims=True)
        both = dot(wr2, jnp.concatenate(split(g * gain_cut[0, :, lanes]), axis=0))
        dr = jnp.sum((both[0:8] + both[8:16]) * dradial_map[:, lanes], axis=0, keepdims=True)
        dr = dr + dcut * row[SLOPE : SLOPE + 1, lanes]
        right = vh[:, lanes]
        part = dot(uth[...], right) + dot(utl[...], right) + dot(uth[...], vl[:, lanes])
        hot = ah[512:576, lanes].astype(F32)
        g = [jnp.sum(hot * part[64 * m : 64 * (m + 1)], axis=0, keepdims=True) for m in range(8)]
        xr, yr, zr, ir = (row[i : i + 1, lanes] for i in (UX, UY, UZ, INV))
        dux = g[0] + root * (g[3] * yr + g[6] * zr + g[7] * xr)
        duy = g[1] + root * (g[3] * xr + g[4] * zr - g[7] * yr)
        duz = g[2] + root * (g[4] * yr + g[6] * xr) + 3.0 * g[5] * zr
        along = dr - (dux * xr + duy * yr + duz * zr) * ir
        dd = jnp.concatenate(
            [dux * ir + along * xr, duy * ir + along * yr, duz * ir + along * zr, jnp.zeros((5, TILE), F32)], axis=0)
        ddb[:, lanes] = jnp.concatenate([dd, dd - dd.astype(BF16).astype(F32)], axis=0).astype(BF16)

    tiles(back_embed)
    scattered = dot_t(ddb[...], oh[0:384, :])
    scattered = scattered[0:8] + scattered[8:16]
    gsrc[0] = scattered[:, 0:128]
    gsrc[1] = scattered[:, 128:256]
    def force_copy(k):
        return pltpu.make_async_remote_copy(
            src_ref=gsrc.at[PLACE[k] // 4], dst_ref=gbuf.at[PLACE[7 - k]], send_sem=gsend_sem.at[group_of(k)],
            recv_sem=grecv_sem.at[group_of(7 - k)], device_id=peer(k), device_id_type=MESH,
        )

    def force_group(g):
        held = gbuf.at[pl.ds(SPANS[g][0], len(GROUPS[g]))]
        return pltpu.make_async_remote_copy(
            src_ref=held, dst_ref=held, send_sem=gsend_sem.at[g], recv_sem=grecv_sem.at[g],
            device_id=peer(GROUPS[g][0]), device_id_type=MESH,
        )

    def forces_out(g):
        for k in GROUPS[g]:
            force_copy(k).start()

    each_group(forces_out)
    energy_out(2, energy_in(1))
    at_own = scattered[:, 256:320] - scattered[:, 320:384]
    for ph in range(2):
        if sizes[ph] > 1:
            energy_group(ph).wait_send()
    each_group(lambda g: ghost_group(g).wait_send())

    def forces_in(g):
        force_group(g).wait_recv()
        force_group(g).wait_send()

    each_group(forces_in)
    acc = jnp.zeros((8, 128), F32)
    for k in range(8):
        acc = acc + jnp.where(lane_group[0:8] == PLACE[7 - k] % 4, gbuf[PLACE[k]], 0.0)
    acc_low = acc - acc.astype(BF16).astype(F32)
    returned = dot_t(jnp.concatenate([acc, acc_low], axis=0).astype(BF16), st4)
    forces_ref[...] = -(at_own + returned[0:8] + returned[8:16])[0:3]

    total = energy_in(2)
    energy_ref[...] = jnp.sum(total, axis=0, keepdims=True)
    energy_group(2).wait_send()


def solution(mesh):
    columns, rows = mesh.shape["gx"], mesh.shape["gy"]
    sizes = sizes_of(columns, rows)
    most = max(sizes)

    def per_device(positions, features, send_list, edge_src, edge_dst, edge_count, w_embed, w_env, w_update, w_out):
        def body(*refs):
            kernel(columns, rows, sizes, *refs)

        vmem = pl.BlockSpec(memory_space=pltpu.VMEM)
        anywhere = pl.BlockSpec(memory_space=pl.ANY)
        forces, energy = pl.pallas_call(
            body,
            out_shape=(jax.ShapeDtypeStruct((3, ATOMS), F32), jax.ShapeDtypeStruct((1, 128), F32)),
            in_specs=[anywhere] * 10,
            out_specs=(vmem, vmem),
            scratch_shapes=[
                pltpu.VMEM((3, ATOMS), F32),
                pltpu.VMEM((C, ATOMS), BF16),
                pltpu.VMEM((1, GHOST), jnp.int32),
                pltpu.VMEM((8, 128), jnp.int32),
                pltpu.VMEM((8, 128), jnp.int32),
                pltpu.SMEM((1,), jnp.int32),
                pltpu.VMEM((C, 2 * C + NB), F32),
                pltpu.VMEM((LAYERS, C, 3 * C), F32),
                pltpu.VMEM((LAYERS, C, 4 * C), F32),
                pltpu.VMEM((1, C), F32),
                pltpu.VMEM((17, 128), F32),
                pltpu.VMEM((8, 17, 128), F32),
                pltpu.VMEM((768, EDGES), BF16),
                pltpu.VMEM((512, EDGES), BF16),
                pltpu.VMEM((512, EDGES), BF16),
                pltpu.VMEM((256, EDGES), BF16),
                pltpu.VMEM((256, EDGES), BF16),
                pltpu.VMEM((16, EDGES), F32),
                pltpu.VMEM((2, C, EDGES), F32),
                pltpu.VMEM((2, C, EDGES), F32),
                pltpu.VMEM((C, EDGES), F32),
                pltpu.VMEM((NB, EDGES), F32),
                pltpu.VMEM((16, EDGES), BF16),
                pltpu.VMEM((2 * LAYERS, 192, 256), BF16),
                pltpu.VMEM((2 * LAYERS, C, 192), BF16),
                pltpu.VMEM((128, 768), BF16),
                pltpu.VMEM((256, 512), F32),
                pltpu.VMEM((8, TILE), F32),
                pltpu.VMEM((512, 256), BF16),
                pltpu.VMEM((512, 256), BF16),
                pltpu.VMEM((128, 512), BF16),
                pltpu.VMEM((2, 8, 128), F32),
                pltpu.VMEM((8, 8, 128), F32),
                pltpu.VMEM((3, most, 8, 128), F32),
                pltpu.SemaphoreType.DMA((10,)),
                pltpu.SemaphoreType.DMA((3,)),
                pltpu.SemaphoreType.DMA((3,)),
                pltpu.SemaphoreType.DMA((3,)),
                pltpu.SemaphoreType.DMA((3,)),
                pltpu.SemaphoreType.DMA((3,)),
                pltpu.SemaphoreType.DMA((3,)),
            ],
            compiler_params=pltpu.CompilerParams(
                collective_id=0, has_side_effects=True, vmem_limit_bytes=55216 * 1024
            ),
        )(
            positions, features, send_list.reshape(1, GHOST), edge_src.reshape(8, 128), edge_dst.reshape(8, 128),
            edge_count, w_embed.T, w_env, jnp.swapaxes(w_update, 1, 2), w_out.reshape(1, C),
        )
        return forces, jnp.sum(energy)

    placed = (
        P(None, ("gx", "gy")), P(None, ("gx", "gy")), P(("gx", "gy")), P(("gx", "gy")), P(("gx", "gy")),
        P(("gx", "gy")), P(), P(), P(), P(),
    )
    return jax.shard_map(
        per_device, mesh=mesh, in_specs=placed, out_specs=(P(None, ("gx", "gy")), P()), check_vma=False
    )
```

```python
import math

import jax
import jax.numpy as jnp
from jax import lax
from jax.experimental import pallas as pl
from jax.experimental.pallas import tpu as pltpu
from jax.sharding import PartitionSpec as P

C = 64
NB = 8
LAYERS = 2
ATOMS = 64
GHOST = 32
EDGES = 1024
SCALE = 16 ** (-0.5)
OFFSETS = ((-1, -1), (-1, 0), (-1, 1), (0, -1), (0, 1), (1, -1), (1, 0), (1, 1))
GROUPS = ((0, 3, 5), (1, 6), (2, 4, 7))
SPANS = ((0, 3), (3, 5), (5, 8))
PLACE = (0, 3, 5, 1, 6, 2, 4, 7)
WIDTH = 6.0
CUTOFF = 5.0
F32 = jnp.float32
BF16 = jnp.bfloat16
MESH = pl.DeviceIdType.MESH
TILE = 256
CUT, LIVE, UX, UY, UZ, INV, DIST, GAIN, BEND, SLOPE, DCUT = 0, 1, 2, 3, 4, 5, 6, 7, 8, 9, 10


def split(x):
    hi = x.astype(BF16)
    return hi, (x - hi.astype(F32)).astype(BF16)


def split3(x):
    hi = x.astype(BF16)
    rest = x - hi.astype(F32)
    mid = rest.astype(BF16)
    return hi, mid, (rest - mid.astype(F32)).astype(BF16)


def dot(x, y):
    return lax.dot_general(x, y, (((1,), (0,)), ((), ())), preferred_element_type=F32)


def dot_t(x, y):
    return lax.dot_general(x, y, (((1,), (1,)), ((), ())), preferred_element_type=F32)


def pick_lane(tables, index):
    lane = index & 127
    which = index >> 7
    result = None
    for t, table in enumerate(tables):
        wide = jnp.broadcast_to(table, (8, 128))
        got = jnp.take_along_axis(wide, lane, axis=1, mode="promise_in_bounds")
        result = got if result is None else jnp.where(which == t, got, result)
    return result


def sizes_of(columns, rows):
    return (2 * rows, max(columns // 8, 1), min(4, columns // 2))


def kernel(
    columns, rows, sizes,
    pos_in, feat_in, send_in, src_in, dst_in, count_in, we_in, wv_in, wu_in, wo_in,
    forces_ref, energy_ref,
    pos_ref, feat_ref, send_ref, src_ref, dst_ref, count_ref, we_ref, wv_ref, wu_ref, wo_ref,
    pay, table, ah, al, oh, vh, vl, row, value, gain_cut, df, dradial_map, ddb, lhs, own_weights, flat, kept, folded,
    uth, utl, embs, gsrc, gbuf, ebuf,
    in_sem, send_sem, recv_sem, gsend_sem, grecv_sem, esend_sem, erecv_sem,
):
    a = lax.axis_index("gx")
    b = lax.axis_index("gy")

    def peer(k):
        dx, dy = OFFSETS[k]
        return (lax.rem(a + dx + columns, columns), b + dy)

    def group_of(k):
        return 1 + OFFSETS[k][1]

    def each_group(act, otherwise=None):
        act(1)
        for g, good in ((0, b > 0), (2, b < rows - 1)):
            pl.when(good)(lambda g=g: act(g))
            if otherwise is not None:
                pl.when(jnp.logical_not(good))(lambda g=g: otherwise(g))

    def member(ph):
        if ph == 0:
            return lax.rem(a, 2) * rows + b
        return a // 8 if ph == 1 else lax.rem(a // 2, sizes[2])

    def energy_peer(ph, t):
        me = member(ph)
        other = lax.rem(me + t, sizes[ph])
        if ph == 0:
            return (a - lax.rem(a, 2) + other // rows, lax.rem(other, rows))
        return (a + (8 if ph == 1 else 2) * (other - me), b)

    barrier = pltpu.get_barrier_semaphore()

    def greet(g):
        for k in GROUPS[g]:
            pl.semaphore_signal(barrier, inc=1, device_id=peer(k), device_id_type=MESH)

    each_group(greet)
    greeted = 0
    for ph in range(3):
        for t in range(1, sizes[ph]):
            pl.semaphore_signal(barrier, inc=1, device_id=energy_peer(ph, t), device_id_type=MESH)
            greeted += 1

    fetched = [
        pltpu.make_async_copy(given, held, in_sem.at[i])
        for i, (given, held) in enumerate([
            (pos_in, pos_ref), (feat_in, feat_ref), (send_in, send_ref), (we_in, we_ref), (src_in, src_ref),
            (dst_in, dst_ref), (count_in, count_ref), (wv_in, wv_ref), (wu_in, wu_ref), (wo_in, wo_ref)])
    ]
    for copy in fetched:
        copy.start()
    for copy in fetched[0:4]:
        copy.wait()

    we_hi, we_lo = split(we_ref[:, 0 : 2 * C])
    we_both = jnp.concatenate(
        [jnp.concatenate([we_hi[:, 0:C], we_lo[:, 0:C]], axis=1),
         jnp.concatenate([we_hi[:, C : 2 * C], we_lo[:, C : 2 * C]], axis=1)], axis=0)
    feat = feat_ref[...]
    own = dot(we_both, jnp.concatenate([feat, feat], axis=0))
    own_src, own_dst = own[0:C], own[C : 2 * C]
    pos = pos_ref[...]
    send4 = jnp.concatenate([send_ref[...]] * 4, axis=1)
    st4 = (lax.broadcasted_iota(jnp.int32, (ATOMS, 128), 0) == send4).astype(F32).astype(BF16)
    exported = jnp.concatenate([own_src, pos, jnp.zeros((61, ATOMS), F32)], axis=0)
    e3 = split3(jnp.concatenate([exported, jnp.zeros((128, 128 - ATOMS), F32)], axis=1))
    st4_tall = jnp.concatenate([st4, jnp.zeros((128 - ATOMS, 128), BF16)], axis=0)
    payload = (dot(e3[2], st4_tall) + dot(e3[1], st4_tall)) + dot(e3[0], st4_tall)
    lane_group = lax.broadcasted_iota(jnp.int32, (16, 128), 1) >> 5

    def by_group(parts):
        result = parts[0]
        for q in range(1, len(parts)):
            result = jnp.where(lane_group[0 : result.shape[0]] == q, parts[q], result)
        return result

    pay[0:16] = by_group([payload[16 * q : 16 * q + 16] for q in range(4)])
    pay[16:17] = by_group([payload[C + i : C + i + 1] for i in range(3)])

    inner = jnp.logical_and(b > 0, b < rows - 1)
    pl.semaphore_wait(barrier, greeted + jnp.where(inner, 8, 5))

    def ghost_copy(k):
        return pltpu.make_async_remote_copy(
            src_ref=pay, dst_ref=table.at[PLACE[7 - k]], send_sem=send_sem.at[group_of(k)],
            recv_sem=recv_sem.at[group_of(7 - k)], device_id=peer(k), device_id_type=MESH,
        )

    def ghost_group(g):
        held = table.at[pl.ds(SPANS[g][0], len(GROUPS[g]))]
        return pltpu.make_async_remote_copy(
            src_ref=held, dst_ref=held, send_sem=send_sem.at[g], recv_sem=recv_sem.at[g],
            device_id=peer(GROUPS[g][0]), device_id_type=MESH,
        )

    def ghosts_out(g):
        for k in GROUPS[g]:
            ghost_copy(k).start()

    each_group(ghosts_out)

    for copy in fetched[4:]:
        copy.wait()

    def put_row(i, v):
        for j in range(8):
            row[i : i + 1, 128 * j : 128 * (j + 1)] = v[j : j + 1, :]

    def loop(count, act):
        for i in range(count):
            act(i)

    def tiles(act):
        loop(EDGES // TILE, lambda n: act(slice(n * TILE, (n + 1) * TILE)))

    src = src_ref[...]
    dst = dst_ref[...]
    block = (src - ATOMS) >> 5
    ghost = src >= ATOMS
    ox = jnp.zeros((8, 128), F32)
    oy = jnp.zeros((8, 128), F32)
    block_place = jnp.zeros((8, 128), jnp.int32)
    for k, (dx, dy) in enumerate(OFFSETS):
        here = jnp.logical_and(ghost, block == k)
        if dx:
            ox = jnp.where(here, WIDTH * dx, ox)
        if dy:
            oy = jnp.where(here, WIDTH * dy, oy)
        block_place = jnp.where(here, PLACE[k], block_place)
    step_y = (oy * (1.0 / WIDTH)).astype(jnp.int32)
    reach = jnp.logical_and(b + step_y >= 0, b + step_y < rows)
    place = lax.broadcasted_iota(jnp.int32, (8, 128), 0) * 128 + lax.broadcasted_iota(jnp.int32, (8, 128), 1)
    live = jnp.where(jnp.logical_and(place < count_ref[0], reach), 1.0, 0.0)
    put_row(LIVE, live)
    slot = jnp.where(ghost, block_place * GHOST + (src & (GHOST - 1)), src + 8 * GHOST)
    def one_hot(j):
        lanes = slice(j * 128, (j + 1) * 128)
        oh[0:320, lanes] = (
            lax.broadcasted_iota(jnp.int32, (320, 128), 0) == slot[j : j + 1, :]).astype(F32).astype(BF16)
        hot = (lax.broadcasted_iota(jnp.int32, (ATOMS, 128), 0) == dst[j : j + 1, :]).astype(F32).astype(BF16)
        oh[320:384, lanes] = hot
        ah[512:576, lanes] = hot

    loop(8, one_hot)

    def four(x):
        hi, lo = split(x)
        return jnp.concatenate([hi, hi, lo, lo], axis=1)

    def weigh(stage):
        layer = min(stage, 3 - stage)
        for i, d in enumerate((1, 2, 0)):
            env_hi, env_lo = split(wv_ref[layer, :, d * C : (d + 1) * C])
            upd_hi, upd_lo = split(wu_ref[layer, :, (d + 1) * C : (d + 2) * C] * SCALE)
            env = [env_hi, env_lo, env_hi, env_lo]
            upd = [upd_hi, upd_hi, upd_lo, upd_lo]
            left, right = (upd, env) if stage < LAYERS else (env, upd)
            lhs[stage, 64 * i : 64 * (i + 1)] = four(
                dot_t(jnp.concatenate(left, axis=1), jnp.concatenate(right, axis=1)))
        own_w = wu_ref[layer, :, 0:C]
        hi, lo = split(own_w if stage < LAYERS else own_w.T)
        own_weights[stage] = jnp.concatenate([hi, hi, lo], axis=1)

    weigh(0)
    wrt = we_ref[:, 2 * C : 2 * C + NB]
    wr = jnp.concatenate([wrt, jnp.zeros((C, 128 - NB), F32)], axis=1).T[0:NB, :]
    wr_low = wr - wr.astype(BF16).astype(F32)
    wr4 = jnp.concatenate([wr, wr, wr_low, jnp.zeros((104, C), F32)], axis=0).T.astype(BF16)
    wr2 = jnp.concatenate([wr, wr_low], axis=0)
    wr2 = jnp.concatenate([wr2, wr2], axis=1).astype(BF16)
    diagonal = lax.broadcasted_iota(jnp.int32, (C, C), 0) == lax.broadcasted_iota(jnp.int32, (C, C), 1)
    wo = jnp.sum(jnp.where(diagonal, wo_ref[...], 0.0), axis=1, keepdims=True)

    def blank(g):
        for i in range(*SPANS[g]):
            table[i] = jnp.zeros((17, 128), F32)
            gbuf[i] = jnp.zeros((8, 128), F32)

    each_group(lambda g: ghost_group(g).wait_recv(), blank)

    def turned(x, groups):
        cut = 128 - 32 * (groups % 4)
        return x if groups % 4 == 0 else jnp.concatenate([x[:, cut:], x[:, :cut]], axis=1)

    channels, coords = [[], [], [], []], [[], [], []]
    for t in range(2):
        held = [table[4 * t + i] for i in range(4)]
        for q in range(4):
            around = [turned(held[i], i - q) for i in range(4)]
            channels[q].append(by_group([x[0:16] for x in around]))
            if q < 3:
                coords[q].append(by_group([x[16:17] for x in around]))
    ghosts = jnp.concatenate([jnp.concatenate(x, axis=1) for x in channels], axis=0)
    own_pos = jnp.concatenate([pos, jnp.zeros((3, 64), F32)], axis=1)
    diff = []
    for i in range(3):
        mine = own_pos[i : i + 1, :]
        at_src = pick_lane(coords[i] + [mine], slot)
        if i < 2:
            at_src = at_src + (ox, oy)[i]
        diff.append(at_src - pick_lane([mine], dst))
    dist = jnp.sqrt(diff[0] * diff[0] + diff[1] * diff[1] + diff[2] * diff[2] + 1.0)
    inv = 1.0 / dist
    ux, uy, uz = (v * inv for v in diff)
    root = math.sqrt(3.0)
    harm = [ux, uy, uz, root * ux * uy, root * uy * uz, 0.5 * (3.0 * uz * uz - 1.0), root * ux * uz,
            0.5 * root * (ux * ux - uy * uy)]
    short = jnp.maximum(1.0 - (dist * dist) * (1.0 / CUTOFF**2), 0.0)
    envelope = short * short
    gain = envelope * inv
    slope = (-4.0 / CUTOFF**2) * dist * short
    put_row(DIST, jnp.minimum(dist, CUTOFF) * (1.0 / CUTOFF))
    put_row(GAIN, gain)
    put_row(BEND, (slope - gain) * inv)
    put_row(CUT, live * envelope)
    put_row(SLOPE, live * slope)
    for i, v in ((UX, ux), (UY, uy), (UZ, uz), (INV, inv)):
        put_row(i, v)
    def map_edges(j):
        lanes = slice(j * 128, (j + 1) * 128)
        hot = ah[512:576, lanes]
        for m in range(8):
            high, low = split(jnp.broadcast_to(harm[m][j : j + 1, :], (16, 128)))
            ah[64 * m : 64 * (m + 1), lanes] = hot * jnp.concatenate([high] * 4, axis=0)
            al[64 * m : 64 * (m + 1), lanes] = hot * jnp.concatenate([low] * 4, axis=0)

    loop(8, map_edges)

    emb_hi, emb_lo = split(jnp.concatenate([ghosts, own_src, own_dst], axis=1))
    embs[...] = jnp.concatenate(
        [jnp.concatenate([emb_hi, wr4], axis=1), jnp.concatenate([emb_lo, jnp.zeros((C, 128), BF16)], axis=1)], axis=0)
    order = (lax.broadcasted_iota(jnp.int32, (NB, TILE), 0) + 1).astype(F32)

    def keep(lanes, place, x):
        hi, lo = split(x)
        vh[place : place + C, lanes] = hi
        vl[place : place + C, lanes] = lo
        ah[576:640, lanes] = hi
        ah[640:704, lanes] = lo
        ah[704:768, lanes] = hi

    def activate(lanes, stage, q):
        s = 1.0 / (1.0 + jnp.exp(-q))
        v = q * s
        cut = row[CUT : CUT + 1, lanes]
        value[stage, :, lanes] = v
        gain_cut[stage, :, lanes] = (s + v * (1.0 - s)) * cut
        return v * cut

    def embed(lanes):
        turns = order * row[DIST : DIST + 1, lanes]
        whole = jnp.floor(turns + 0.5)
        angle = (turns - whole) * math.pi
        sign = 1.0 - 2.0 * (whole - 2.0 * jnp.floor(whole * 0.5))
        sq = angle * angle
        sine = 1.0 / 39916800.0
        for c in (-1.0 / 362880.0, 1.0 / 5040.0, -1.0 / 120.0, 1.0 / 6.0, -1.0):
            sine = c + sq * sine
        sine = -(angle * sine) * sign
        cosine = 1.0 / 479001600.0
        for c in (-1.0 / 3628800.0, 1.0 / 40320.0, -1.0 / 720.0, 1.0 / 24.0, -0.5, 1.0):
            cosine = c + sq * cosine
        cosine = cosine * sign
        near = row[GAIN : GAIN + 1, lanes]
        radial = sine * near
        dradial_map[:, lanes] = order * (math.pi / CUTOFF) * cosine * near + sine * row[BEND : BEND + 1, lanes]
        low = radial - radial.astype(BF16).astype(F32)
        oh[384:512, lanes] = jnp.concatenate([radial, low, radial, jnp.zeros((104, TILE), F32)], axis=0).astype(BF16)
        both = dot(embs[...], oh[:, lanes])
        f = activate(lanes, 0, both[0:C] + both[C : 2 * C])
        df[:, lanes] = f
        keep(lanes, 192, f)

    degree = lax.broadcasted_iota(jnp.int32, (C, 512), 1) >= 192

    def mix(stage, place):
        sums = dot_t(ah[576:704, :], ah[0:576, :])
        sums = sums[0:C] + sums[C : 2 * C]
        hi, lo = split(sums[:, 0:512] + dot_t(ah[576:640, :], al[...]))
        every = dot(lhs[stage, 0:128], jnp.concatenate([hi, lo, hi, lo], axis=0))
        outer = jnp.where(degree, every[C : 2 * C], every[0:C])
        kept[place : place + C, :] = outer
        hi, lo = split(sums[:, 512:576])
        inner = dot(lhs[stage, 128:192], jnp.concatenate([hi, lo, hi, lo], axis=0))
        hi, lo = split(outer)
        flat[0:C, 0:512] = hi
        flat[C : 2 * C, 0:512] = lo
        hi, lo = split(inner)
        flat[0:C, 512:768] = jnp.concatenate([hi, own_weights[stage]], axis=1)
        flat[C : 2 * C, 512:768] = jnp.concatenate([lo, jnp.zeros((C, 192), BF16)], axis=1)

    def spread(lanes):
        both = dot(flat[...], ah[:, lanes])
        return both[0:C] + both[C : 2 * C] + dot(flat[0:C, 0:512], al[:, lanes])

    def back_map(place):
        hi, lo = split(kept[place : place + 128, :].T)
        uth[:, place : place + 128] = hi
        utl[:, place : place + 128] = lo

    def energy_out(ph, x):
        me = member(ph)
        ebuf[ph, me] = x
        for t in range(1, sizes[ph]):
            pltpu.make_async_remote_copy(
                src_ref=ebuf.at[ph, me], dst_ref=ebuf.at[ph, me], send_sem=esend_sem.at[ph], recv_sem=erecv_sem.at[ph],
                device_id=energy_peer(ph, t), device_id_type=MESH,
            ).start()

    def energy_group(ph):
        held = ebuf.at[ph, pl.ds(0, sizes[ph] - 1)]
        return pltpu.make_async_remote_copy(
            src_ref=held, dst_ref=held, send_sem=esend_sem.at[ph], recv_sem=erecv_sem.at[ph],
            device_id=energy_peer(ph, 1), device_id_type=MESH,
        )

    def energy_in(ph):
        if sizes[ph] > 1:
            energy_group(ph).wait_recv()
        total = ebuf[ph, 0]
        for t in range(1, sizes[ph]):
            total = total + ebuf[ph, t]
        return total

    weigh(1)
    tiles(embed)

    def first_layer(lanes):
        f = df[:, lanes] + activate(lanes, 1, spread(lanes))
        df[:, lanes] = f
        keep(lanes, 64, f)

    folded[...] = jnp.zeros((8, TILE), F32)

    def turn(lanes):
        q = spread(lanes)
        s = 1.0 / (1.0 + jnp.exp(-q))
        v = q * s
        cut = row[CUT : CUT + 1, lanes]
        f = df[:, lanes] + v * cut
        g = wo * row[LIVE : LIVE + 1, lanes]
        per_edge = f * g
        piece = per_edge[0:8]
        for i in range(1, 8):
            piece = piece + per_edge[8 * i : 8 * i + 8]
        folded[...] += piece
        df[:, lanes] = g
        row[DCUT : DCUT + 1, lanes] = jnp.sum(g * v, axis=0, keepdims=True)
        keep(lanes, 0, g * ((s + v * (1.0 - s)) * cut))

    def back_first(lanes):
        g = df[:, lanes] + spread(lanes)
        df[:, lanes] = g
        row[DCUT : DCUT + 1, lanes] += jnp.sum(g * value[1, :, lanes], axis=0, keepdims=True)
        keep(lanes, 128, g * gain_cut[1, :, lanes])

    mix(0, 128)
    weigh(2)
    tiles(first_layer)
    mix(1, 0)
    weigh(3)
    tiles(turn)
    energy_out(0, folded[:, 0:128] + folded[:, 128:256])
    mix(2, 64)
    tiles(back_first)
    energy_out(1, energy_in(0))
    back_map(0)
    mix(3, 192)
    back_map(128)

    def back_embed(lanes):
        g = df[:, lanes] + spread(lanes)
        dcut = row[DCUT : DCUT + 1, lanes] + jnp.sum(g * value[0, :, lanes], axis=0, keepdims=True)
        both = dot(wr2, jnp.concatenate(split(g * gain_cut[0, :, lanes]), axis=0))
        dr = jnp.sum((both[0:8] + both[8:16]) * dradial_map[:, lanes], axis=0, keepdims=True)
        dr = dr + dcut * row[SLOPE : SLOPE + 1, lanes]
        right = vh[:, lanes]
        part = dot(uth[...], right) + dot(utl[...], right) + dot(uth[...], vl[:, lanes])
        hot = ah[512:576, lanes].astype(F32)
        g = [jnp.sum(hot * part[64 * m : 64 * (m + 1)], axis=0, keepdims=True) for m in range(8)]
        xr, yr, zr, ir = (row[i : i + 1, lanes] for i in (UX, UY, UZ, INV))
        dux = g[0] + root * (g[3] * yr + g[6] * zr + g[7] * xr)
        duy = g[1] + root * (g[3] * xr + g[4] * zr - g[7] * yr)
        duz = g[2] + root * (g[4] * yr + g[6] * xr) + 3.0 * g[5] * zr
        along = dr - (dux * xr + duy * yr + duz * zr) * ir
        dd = jnp.concatenate(
            [dux * ir + along * xr, duy * ir + along * yr, duz * ir + along * zr, jnp.zeros((5, TILE), F32)], axis=0)
        ddb[:, lanes] = jnp.concatenate([dd, dd - dd.astype(BF16).astype(F32)], axis=0).astype(BF16)

    tiles(back_embed)
    scattered = dot_t(ddb[...], oh[0:384, :])
    scattered = scattered[0:8] + scattered[8:16]
    gsrc[0] = scattered[:, 0:128]
    gsrc[1] = scattered[:, 128:256]
    def force_copy(k):
        return pltpu.make_async_remote_copy(
            src_ref=gsrc.at[PLACE[k] // 4], dst_ref=gbuf.at[PLACE[7 - k]], send_sem=gsend_sem.at[group_of(k)],
            recv_sem=grecv_sem.at[group_of(7 - k)], device_id=peer(k), device_id_type=MESH,
        )

    def force_group(g):
        held = gbuf.at[pl.ds(SPANS[g][0], len(GROUPS[g]))]
        return pltpu.make_async_remote_copy(
            src_ref=held, dst_ref=held, send_sem=gsend_sem.at[g], recv_sem=grecv_sem.at[g],
            device_id=peer(GROUPS[g][0]), device_id_type=MESH,
        )

    def forces_out(g):
        for k in GROUPS[g]:
            force_copy(k).start()

    each_group(forces_out)
    energy_out(2, energy_in(1))
    at_own = scattered[:, 256:320] - scattered[:, 320:384]
    for ph in range(2):
        if sizes[ph] > 1:
            energy_group(ph).wait_send()
    each_group(lambda g: ghost_group(g).wait_send())

    def forces_in(g):
        force_group(g).wait_recv()
        force_group(g).wait_send()

    each_group(forces_in)
    acc = jnp.zeros((8, 128), F32)
    for k in range(8):
        acc = acc + jnp.where(lane_group[0:8] == PLACE[7 - k] % 4, gbuf[PLACE[k]], 0.0)
    acc_low = acc - acc.astype(BF16).astype(F32)
    returned = dot_t(jnp.concatenate([acc, acc_low], axis=0).astype(BF16), st4)
    forces_ref[...] = -(at_own + returned[0:8] + returned[8:16])[0:3]

    total = energy_in(2)
    energy_ref[...] = jnp.sum(total, axis=0, keepdims=True)
    energy_group(2).wait_send()


def solution(mesh):
    columns, rows = mesh.shape["gx"], mesh.shape["gy"]
    sizes = sizes_of(columns, rows)
    most = max(sizes)

    def per_device(positions, features, send_list, edge_src, edge_dst, edge_count, w_embed, w_env, w_update, w_out):
        def body(*refs):
            kernel(columns, rows, sizes, *refs)

        vmem = pl.BlockSpec(memory_space=pltpu.VMEM)
        anywhere = pl.BlockSpec(memory_space=pl.ANY)
        forces, energy = pl.pallas_call(
            body,
            out_shape=(jax.ShapeDtypeStruct((3, ATOMS), F32), jax.ShapeDtypeStruct((1, 128), F32)),
            in_specs=[anywhere] * 10,
            out_specs=(vmem, vmem),
            scratch_shapes=[
                pltpu.VMEM((3, ATOMS), F32),
                pltpu.VMEM((C, ATOMS), BF16),
                pltpu.VMEM((1, GHOST), jnp.int32),
                pltpu.VMEM((8, 128), jnp.int32),
                pltpu.VMEM((8, 128), jnp.int32),
                pltpu.SMEM((1,), jnp.int32),
                pltpu.VMEM((C, 2 * C + NB), F32),
                pltpu.VMEM((LAYERS, C, 3 * C), F32),
                pltpu.VMEM((LAYERS, C, 4 * C), F32),
                pltpu.VMEM((1, C), F32),
                pltpu.VMEM((17, 128), F32),
                pltpu.VMEM((8, 17, 128), F32),
                pltpu.VMEM((768, EDGES), BF16),
                pltpu.VMEM((512, EDGES), BF16),
                pltpu.VMEM((512, EDGES), BF16),
                pltpu.VMEM((256, EDGES), BF16),
                pltpu.VMEM((256, EDGES), BF16),
                pltpu.VMEM((16, EDGES), F32),
                pltpu.VMEM((2, C, EDGES), F32),
                pltpu.VMEM((2, C, EDGES), F32),
                pltpu.VMEM((C, EDGES), F32),
                pltpu.VMEM((NB, EDGES), F32),
                pltpu.VMEM((16, EDGES), BF16),
                pltpu.VMEM((2 * LAYERS, 192, 256), BF16),
                pltpu.VMEM((2 * LAYERS, C, 192), BF16),
                pltpu.VMEM((128, 768), BF16),
                pltpu.VMEM((256, 512), F32),
                pltpu.VMEM((8, TILE), F32),
                pltpu.VMEM((512, 256), BF16),
                pltpu.VMEM((512, 256), BF16),
                pltpu.VMEM((128, 512), BF16),
                pltpu.VMEM((2, 8, 128), F32),
                pltpu.VMEM((8, 8, 128), F32),
                pltpu.VMEM((3, most, 8, 128), F32),
                pltpu.SemaphoreType.DMA((10,)),
                pltpu.SemaphoreType.DMA((3,)),
                pltpu.SemaphoreType.DMA((3,)),
                pltpu.SemaphoreType.DMA((3,)),
                pltpu.SemaphoreType.DMA((3,)),
                pltpu.SemaphoreType.DMA((3,)),
                pltpu.SemaphoreType.DMA((3,)),
            ],
            compiler_params=pltpu.CompilerParams(
                collective_id=0, has_side_effects=True, vmem_limit_bytes=55216 * 1024
            ),
        )(
            positions, features, send_list.reshape(1, GHOST), edge_src.reshape(8, 128), edge_dst.reshape(8, 128),
            edge_count, w_embed.T, w_env, jnp.swapaxes(w_update, 1, 2), w_out.reshape(1, C),
        )
        return forces, jnp.sum(energy)

    placed = (
        P(None, ("gx", "gy")), P(None, ("gx", "gy")), P(("gx", "gy")), P(("gx", "gy")), P(("gx", "gy")),
        P(("gx", "gy")), P(), P(), P(), P(),
    )
    return jax.shard_map(
        per_device, mesh=mesh, in_specs=placed, out_specs=(P(None, ("gx", "gy")), P()), check_vma=False
    )
```

```python
import math

import jax
import jax.numpy as jnp
from jax import lax
from jax.experimental import pallas as pl
from jax.experimental.pallas import tpu as pltpu
from jax.sharding import PartitionSpec as P

C = 64
NB = 8
LAYERS = 2
ATOMS = 64
GHOST = 32
EDGES = 1024
SCALE = 16 ** (-0.5)
OFFSETS = ((-1, -1), (-1, 0), (-1, 1), (0, -1), (0, 1), (1, -1), (1, 0), (1, 1))
GROUPS = ((0, 3, 5), (1, 6), (2, 4, 7))
SPANS = ((0, 3), (3, 5), (5, 8))
PLACE = (0, 3, 5, 1, 6, 2, 4, 7)
WIDTH = 6.0
CUTOFF = 5.0
F32 = jnp.float32
BF16 = jnp.bfloat16
MESH = pl.DeviceIdType.MESH
TILE = 512
CUT, LIVE, UX, UY, UZ, INV, DIST, GAIN, BEND, SLOPE, DCUT = 0, 1, 2, 3, 4, 5, 6, 7, 8, 9, 10


def split(x):
    hi = x.astype(BF16)
    return hi, (x - hi.astype(F32)).astype(BF16)


def split3(x):
    hi = x.astype(BF16)
    rest = x - hi.astype(F32)
    mid = rest.astype(BF16)
    return hi, mid, (rest - mid.astype(F32)).astype(BF16)


def dot(x, y):
    return lax.dot_general(x, y, (((1,), (0,)), ((), ())), preferred_element_type=F32)


def dot_t(x, y):
    return lax.dot_general(x, y, (((1,), (1,)), ((), ())), preferred_element_type=F32)


def pick_lane(tables, index):
    lane = index & 127
    which = index >> 7
    result = None
    for t, table in enumerate(tables):
        wide = jnp.broadcast_to(table, (8, 128))
        got = jnp.take_along_axis(wide, lane, axis=1, mode="promise_in_bounds")
        result = got if result is None else jnp.where(which == t, got, result)
    return result


def sizes_of(columns, rows):
    return (2 * rows, max(columns // 8, 1), min(4, columns // 2))


def kernel(
    columns, rows, sizes,
    pos_in, feat_in, send_in, src_in, dst_in, count_in, we_in, wv_in, wu_in, wo_in,
    forces_ref, energy_ref,
    pos_ref, feat_ref, send_ref, src_ref, dst_ref, count_ref, we_ref, wv_ref, wu_ref, wo_ref,
    pay, table, ah, al, oh, vh, vl, row, value, gain_cut, df, dradial_map, ddb, lhs, own_weights, flat, kept, folded,
    uth, utl, embs, gsrc, gbuf, ebuf,
    in_sem, send_sem, recv_sem, gsend_sem, grecv_sem, esend_sem, erecv_sem,
):
    a = lax.axis_index("gx")
    b = lax.axis_index("gy")

    def peer(k):
        dx, dy = OFFSETS[k]
        return (lax.rem(a + dx + columns, columns), b + dy)

    def group_of(k):
        return 1 + OFFSETS[k][1]

    def each_group(act, otherwise=None):
        act(1)
        for g, good in ((0, b > 0), (2, b < rows - 1)):
            pl.when(good)(lambda g=g: act(g))
            if otherwise is not None:
                pl.when(jnp.logical_not(good))(lambda g=g: otherwise(g))

    def member(ph):
        if ph == 0:
            return lax.rem(a, 2) * rows + b
        return a // 8 if ph == 1 else lax.rem(a // 2, sizes[2])

    def energy_peer(ph, t):
        me = member(ph)
        other = lax.rem(me + t, sizes[ph])
        if ph == 0:
            return (a - lax.rem(a, 2) + other // rows, lax.rem(other, rows))
        return (a + (8 if ph == 1 else 2) * (other - me), b)

    barrier = pltpu.get_barrier_semaphore()

    def greet(g):
        for k in GROUPS[g]:
            pl.semaphore_signal(barrier, inc=1, device_id=peer(k), device_id_type=MESH)

    each_group(greet)
    greeted = 0
    for ph in range(3):
        for t in range(1, sizes[ph]):
            pl.semaphore_signal(barrier, inc=1, device_id=energy_peer(ph, t), device_id_type=MESH)
            greeted += 1

    fetched = [
        pltpu.make_async_copy(given, held, in_sem.at[i])
        for i, (given, held) in enumerate([
            (pos_in, pos_ref), (feat_in, feat_ref), (send_in, send_ref), (we_in, we_ref), (src_in, src_ref),
            (dst_in, dst_ref), (count_in, count_ref), (wv_in, wv_ref), (wu_in, wu_ref), (wo_in, wo_ref)])
    ]
    for copy in fetched:
        copy.start()
    for copy in fetched[0:4]:
        copy.wait()

    we_hi, we_lo = split(we_ref[:, 0 : 2 * C])
    we_both = jnp.concatenate(
        [jnp.concatenate([we_hi[:, 0:C], we_lo[:, 0:C]], axis=1),
         jnp.concatenate([we_hi[:, C : 2 * C], we_lo[:, C : 2 * C]], axis=1)], axis=0)
    feat = feat_ref[...]
    own = dot(we_both, jnp.concatenate([feat, feat], axis=0))
    own_src, own_dst = own[0:C], own[C : 2 * C]
    pos = pos_ref[...]
    send4 = jnp.concatenate([send_ref[...]] * 4, axis=1)
    st4 = (lax.broadcasted_iota(jnp.int32, (ATOMS, 128), 0) == send4).astype(F32).astype(BF16)
    exported = jnp.concatenate([own_src, pos, jnp.zeros((61, ATOMS), F32)], axis=0)
    e3 = split3(jnp.concatenate([exported, jnp.zeros((128, 128 - ATOMS), F32)], axis=1))
    st4_tall = jnp.concatenate([st4, jnp.zeros((128 - ATOMS, 128), BF16)], axis=0)
    payload = (dot(e3[2], st4_tall) + dot(e3[1], st4_tall)) + dot(e3[0], st4_tall)
    lane_group = lax.broadcasted_iota(jnp.int32, (16, 128), 1) >> 5

    def by_group(parts):
        result = parts[0]
        for q in range(1, len(parts)):
            result = jnp.where(lane_group[0 : result.shape[0]] == q, parts[q], result)
        return result

    pay[0:16] = by_group([payload[16 * q : 16 * q + 16] for q in range(4)])
    pay[16:17] = by_group([payload[C + i : C + i + 1] for i in range(3)])

    inner = jnp.logical_and(b > 0, b < rows - 1)
    pl.semaphore_wait(barrier, greeted + jnp.where(inner, 8, 5))

    def ghost_copy(k):
        return pltpu.make_async_remote_copy(
            src_ref=pay, dst_ref=table.at[PLACE[7 - k]], send_sem=send_sem.at[group_of(k)],
            recv_sem=recv_sem.at[group_of(7 - k)], device_id=peer(k), device_id_type=MESH,
        )

    def ghost_group(g):
        held = table.at[pl.ds(SPANS[g][0], len(GROUPS[g]))]
        return pltpu.make_async_remote_copy(
            src_ref=held, dst_ref=held, send_sem=send_sem.at[g], recv_sem=recv_sem.at[g],
            device_id=peer(GROUPS[g][0]), device_id_type=MESH,
        )

    def ghosts_out(g):
        for k in GROUPS[g]:
            ghost_copy(k).start()

    each_group(ghosts_out)

    for copy in fetched[4:]:
        copy.wait()

    def put_row(i, v):
        for j in range(8):
            row[i : i + 1, 128 * j : 128 * (j + 1)] = v[j : j + 1, :]

    def loop(count, act):
        for i in range(count):
            act(i)

    def tiles(act):
        loop(EDGES // TILE, lambda n: act(slice(n * TILE, (n + 1) * TILE)))

    src = src_ref[...]
    dst = dst_ref[...]
    block = (src - ATOMS) >> 5
    ghost = src >= ATOMS
    ox = jnp.zeros((8, 128), F32)
    oy = jnp.zeros((8, 128), F32)
    block_place = jnp.zeros((8, 128), jnp.int32)
    for k, (dx, dy) in enumerate(OFFSETS):
        here = jnp.logical_and(ghost, block == k)
        if dx:
            ox = jnp.where(here, WIDTH * dx, ox)
        if dy:
            oy = jnp.where(here, WIDTH * dy, oy)
        block_place = jnp.where(here, PLACE[k], block_place)
    step_y = (oy * (1.0 / WIDTH)).astype(jnp.int32)
    reach = jnp.logical_and(b + step_y >= 0, b + step_y < rows)
    place = lax.broadcasted_iota(jnp.int32, (8, 128), 0) * 128 + lax.broadcasted_iota(jnp.int32, (8, 128), 1)
    live = jnp.where(jnp.logical_and(place < count_ref[0], reach), 1.0, 0.0)
    put_row(LIVE, live)
    slot = jnp.where(ghost, block_place * GHOST + (src & (GHOST - 1)), src + 8 * GHOST)
    def one_hot(j):
        lanes = slice(j * 128, (j + 1) * 128)
        oh[0:320, lanes] = (
            lax.broadcasted_iota(jnp.int32, (320, 128), 0) == slot[j : j + 1, :]).astype(F32).astype(BF16)
        hot = (lax.broadcasted_iota(jnp.int32, (ATOMS, 128), 0) == dst[j : j + 1, :]).astype(F32).astype(BF16)
        oh[320:384, lanes] = hot
        ah[512:576, lanes] = hot

    loop(8, one_hot)

    def four(x):
        hi, lo = split(x)
        return jnp.concatenate([hi, hi, lo, lo], axis=1)

    def weigh(stage):
        layer = min(stage, 3 - stage)
        for i, d in enumerate((1, 2, 0)):
            env_hi, env_lo = split(wv_ref[layer, :, d * C : (d + 1) * C])
            upd_hi, upd_lo = split(wu_ref[layer, :, (d + 1) * C : (d + 2) * C] * SCALE)
            env = [env_hi, env_lo, env_hi, env_lo]
            upd = [upd_hi, upd_hi, upd_lo, upd_lo]
            left, right = (upd, env) if stage < LAYERS else (env, upd)
            lhs[stage, 64 * i : 64 * (i + 1)] = four(
                dot_t(jnp.concatenate(left, axis=1), jnp.concatenate(right, axis=1)))
        own_w = wu_ref[layer, :, 0:C]
        hi, lo = split(own_w if stage < LAYERS else own_w.T)
        own_weights[stage] = jnp.concatenate([hi, hi, lo], axis=1)

    weigh(0)
    wrt = we_ref[:, 2 * C : 2 * C + NB]
    wr = jnp.concatenate([wrt, jnp.zeros((C, 128 - NB), F32)], axis=1).T[0:NB, :]
    wr_low = wr - wr.astype(BF16).astype(F32)
    wr4 = jnp.concatenate([wr, wr, wr_low, jnp.zeros((104, C), F32)], axis=0).T.astype(BF16)
    wr2 = jnp.concatenate([wr, wr_low], axis=0)
    wr2 = jnp.concatenate([wr2, wr2], axis=1).astype(BF16)
    diagonal = lax.broadcasted_iota(jnp.int32, (C, C), 0) == lax.broadcasted_iota(jnp.int32, (C, C), 1)
    wo = jnp.sum(jnp.where(diagonal, wo_ref[...], 0.0), axis=1, keepdims=True)

    def blank(g):
        for i in range(*SPANS[g]):
            table[i] = jnp.zeros((17, 128), F32)
            gbuf[i] = jnp.zeros((8, 128), F32)

    each_group(lambda g: ghost_group(g).wait_recv(), blank)

    def turned(x, groups):
        cut = 128 - 32 * (groups % 4)
        return x if groups % 4 == 0 else jnp.concatenate([x[:, cut:], x[:, :cut]], axis=1)

    channels, coords = [[], [], [], []], [[], [], []]
    for t in range(2):
        held = [table[4 * t + i] for i in range(4)]
        for q in range(4):
            around = [turned(held[i], i - q) for i in range(4)]
            channels[q].append(by_group([x[0:16] for x in around]))
            if q < 3:
                coords[q].append(by_group([x[16:17] for x in around]))
    ghosts = jnp.concatenate([jnp.concatenate(x, axis=1) for x in channels], axis=0)
    own_pos = jnp.concatenate([pos, jnp.zeros((3, 64), F32)], axis=1)
    diff = []
    for i in range(3):
        mine = own_pos[i : i + 1, :]
        at_src = pick_lane(coords[i] + [mine], slot)
        if i < 2:
            at_src = at_src + (ox, oy)[i]
        diff.append(at_src - pick_lane([mine], dst))
    dist = jnp.sqrt(diff[0] * diff[0] + diff[1] * diff[1] + diff[2] * diff[2] + 1.0)
    inv = 1.0 / dist
    ux, uy, uz = (v * inv for v in diff)
    root = math.sqrt(3.0)
    harm = [ux, uy, uz, root * ux * uy, root * uy * uz, 0.5 * (3.0 * uz * uz - 1.0), root * ux * uz,
            0.5 * root * (ux * ux - uy * uy)]
    short = jnp.maximum(1.0 - (dist * dist) * (1.0 / CUTOFF**2), 0.0)
    envelope = short * short
    gain = envelope * inv
    slope = (-4.0 / CUTOFF**2) * dist * short
    put_row(DIST, jnp.minimum(dist, CUTOFF) * (1.0 / CUTOFF))
    put_row(GAIN, gain)
    put_row(BEND, (slope - gain) * inv)
    put_row(CUT, live * envelope)
    put_row(SLOPE, live * slope)
    for i, v in ((UX, ux), (UY, uy), (UZ, uz), (INV, inv)):
        put_row(i, v)
    def map_edges(j):
        lanes = slice(j * 128, (j + 1) * 128)
        hot = ah[512:576, lanes]
        for m in range(8):
            high, low = split(jnp.broadcast_to(harm[m][j : j + 1, :], (16, 128)))
            ah[64 * m : 64 * (m + 1), lanes] = hot * jnp.concatenate([high] * 4, axis=0)
            al[64 * m : 64 * (m + 1), lanes] = hot * jnp.concatenate([low] * 4, axis=0)

    loop(8, map_edges)

    emb_hi, emb_lo = split(jnp.concatenate([ghosts, own_src, own_dst], axis=1))
    embs[...] = jnp.concatenate(
        [jnp.concatenate([emb_hi, wr4], axis=1), jnp.concatenate([emb_lo, jnp.zeros((C, 128), BF16)], axis=1)], axis=0)
    order = (lax.broadcasted_iota(jnp.int32, (NB, TILE), 0) + 1).astype(F32)

    def keep(lanes, place, x):
        hi, lo = split(x)
        vh[place : place + C, lanes] = hi
        vl[place : place + C, lanes] = lo
        ah[576:640, lanes] = hi
        ah[640:704, lanes] = lo
        ah[704:768, lanes] = hi

    def activate(lanes, stage, q):
        s = 1.0 / (1.0 + jnp.exp(-q))
        v = q * s
        cut = row[CUT : CUT + 1, lanes]
        value[stage, :, lanes] = v
        gain_cut[stage, :, lanes] = (s + v * (1.0 - s)) * cut
        return v * cut

    def embed(lanes):
        turns = order * row[DIST : DIST + 1, lanes]
        whole = jnp.floor(turns + 0.5)
        angle = (turns - whole) * math.pi
        sign = 1.0 - 2.0 * (whole - 2.0 * jnp.floor(whole * 0.5))
        sq = angle * angle
        sine = 1.0 / 39916800.0
        for c in (-1.0 / 362880.0, 1.0 / 5040.0, -1.0 / 120.0, 1.0 / 6.0, -1.0):
            sine = c + sq * sine
        sine = -(angle * sine) * sign
        cosine = 1.0 / 479001600.0
        for c in (-1.0 / 3628800.0, 1.0 / 40320.0, -1.0 / 720.0, 1.0 / 24.0, -0.5, 1.0):
            cosine = c + sq * cosine
        cosine = cosine * sign
        near = row[GAIN : GAIN + 1, lanes]
        radial = sine * near
        dradial_map[:, lanes] = order * (math.pi / CUTOFF) * cosine * near + sine * row[BEND : BEND + 1, lanes]
        low = radial - radial.astype(BF16).astype(F32)
        oh[384:512, lanes] = jnp.concatenate([radial, low, radial, jnp.zeros((104, TILE), F32)], axis=0).astype(BF16)
        both = dot(embs[...], oh[:, lanes])
        f = activate(lanes, 0, both[0:C] + both[C : 2 * C])
        df[:, lanes] = f
        keep(lanes, 192, f)

    degree = lax.broadcasted_iota(jnp.int32, (C, 512), 1) >= 192

    def mix(stage, place):
        sums = dot_t(ah[576:704, :], ah[0:576, :])
        sums = sums[0:C] + sums[C : 2 * C]
        hi, lo = split(sums[:, 0:512] + dot_t(ah[576:640, :], al[...]))
        every = dot(lhs[stage, 0:128], jnp.concatenate([hi, lo, hi, lo], axis=0))
        outer = jnp.where(degree, every[C : 2 * C], every[0:C])
        kept[place : place + C, :] = outer
        hi, lo = split(sums[:, 512:576])
        inner = dot(lhs[stage, 128:192], jnp.concatenate([hi, lo, hi, lo], axis=0))
        hi, lo = split(outer)
        flat[0:C, 0:512] = hi
        flat[C : 2 * C, 0:512] = lo
        hi, lo = split(inner)
        flat[0:C, 512:768] = jnp.concatenate([hi, own_weights[stage]], axis=1)
        flat[C : 2 * C, 512:768] = jnp.concatenate([lo, jnp.zeros((C, 192), BF16)], axis=1)

    def spread(lanes):
        both = dot(flat[...], ah[:, lanes])
        return both[0:C] + both[C : 2 * C] + dot(flat[0:C, 0:512], al[:, lanes])

    def back_map(place):
        hi, lo = split(kept[place : place + 128, :].T)
        uth[:, place : place + 128] = hi
        utl[:, place : place + 128] = lo

    def energy_out(ph, x):
        me = member(ph)
        ebuf[ph, me] = x
        for t in range(1, sizes[ph]):
            pltpu.make_async_remote_copy(
                src_ref=ebuf.at[ph, me], dst_ref=ebuf.at[ph, me], send_sem=esend_sem.at[ph], recv_sem=erecv_sem.at[ph],
                device_id=energy_peer(ph, t), device_id_type=MESH,
            ).start()

    def energy_group(ph):
        held = ebuf.at[ph, pl.ds(0, sizes[ph] - 1)]
        return pltpu.make_async_remote_copy(
            src_ref=held, dst_ref=held, send_sem=esend_sem.at[ph], recv_sem=erecv_sem.at[ph],
            device_id=energy_peer(ph, 1), device_id_type=MESH,
        )

    def energy_in(ph):
        if sizes[ph] > 1:
            energy_group(ph).wait_recv()
        total = ebuf[ph, 0]
        for t in range(1, sizes[ph]):
            total = total + ebuf[ph, t]
        return total

    weigh(1)
    tiles(embed)

    def first_layer(lanes):
        f = df[:, lanes] + activate(lanes, 1, spread(lanes))
        df[:, lanes] = f
        keep(lanes, 64, f)

    folded[...] = jnp.zeros((8, TILE), F32)

    def turn(lanes):
        q = spread(lanes)
        s = 1.0 / (1.0 + jnp.exp(-q))
        v = q * s
        cut = row[CUT : CUT + 1, lanes]
        f = df[:, lanes] + v * cut
        g = wo * row[LIVE : LIVE + 1, lanes]
        per_edge = f * g
        piece = per_edge[0:8]
        for i in range(1, 8):
            piece = piece + per_edge[8 * i : 8 * i + 8]
        folded[...] += piece
        df[:, lanes] = g
        row[DCUT : DCUT + 1, lanes] = jnp.sum(g * v, axis=0, keepdims=True)
        keep(lanes, 0, g * ((s + v * (1.0 - s)) * cut))

    def back_first(lanes):
        g = df[:, lanes] + spread(lanes)
        df[:, lanes] = g
        row[DCUT : DCUT + 1, lanes] += jnp.sum(g * value[1, :, lanes], axis=0, keepdims=True)
        keep(lanes, 128, g * gain_cut[1, :, lanes])

    mix(0, 128)
    weigh(2)
    tiles(first_layer)
    mix(1, 0)
    weigh(3)
    tiles(turn)
    energy_out(0, sum(folded[:, 128 * j : 128 * (j + 1)] for j in range(TILE // 128)))
    mix(2, 64)
    tiles(back_first)
    back_map(0)
    mix(3, 192)
    back_map(128)
    energy_out(1, energy_in(0))

    def back_embed(lanes):
        g = df[:, lanes] + spread(lanes)
        dcut = row[DCUT : DCUT + 1, lanes] + jnp.sum(g * value[0, :, lanes], axis=0, keepdims=True)
        both = dot(wr2, jnp.concatenate(split(g * gain_cut[0, :, lanes]), axis=0))
        dr = jnp.sum((both[0:8] + both[8:16]) * dradial_map[:, lanes], axis=0, keepdims=True)
        dr = dr + dcut * row[SLOPE : SLOPE + 1, lanes]
        right = vh[:, lanes]
        part = dot(uth[...], right) + dot(utl[...], right) + dot(uth[...], vl[:, lanes])
        hot = ah[512:576, lanes].astype(F32)
        g = [jnp.sum(hot * part[64 * m : 64 * (m + 1)], axis=0, keepdims=True) for m in range(8)]
        xr, yr, zr, ir = (row[i : i + 1, lanes] for i in (UX, UY, UZ, INV))
        dux = g[0] + root * (g[3] * yr + g[6] * zr + g[7] * xr)
        duy = g[1] + root * (g[3] * xr + g[4] * zr - g[7] * yr)
        duz = g[2] + root * (g[4] * yr + g[6] * xr) + 3.0 * g[5] * zr
        along = dr - (dux * xr + duy * yr + duz * zr) * ir
        dd = jnp.concatenate(
            [dux * ir + along * xr, duy * ir + along * yr, duz * ir + along * zr, jnp.zeros((5, TILE), F32)], axis=0)
        ddb[:, lanes] = jnp.concatenate([dd, dd - dd.astype(BF16).astype(F32)], axis=0).astype(BF16)

    tiles(back_embed)
    scattered = dot_t(ddb[...], oh[0:384, :])
    scattered = scattered[0:8] + scattered[8:16]
    gsrc[0] = scattered[:, 0:128]
    gsrc[1] = scattered[:, 128:256]
    def force_copy(k):
        return pltpu.make_async_remote_copy(
            src_ref=gsrc.at[PLACE[k] // 4], dst_ref=gbuf.at[PLACE[7 - k]], send_sem=gsend_sem.at[group_of(k)],
            recv_sem=grecv_sem.at[group_of(7 - k)], device_id=peer(k), device_id_type=MESH,
        )

    def force_group(g):
        held = gbuf.at[pl.ds(SPANS[g][0], len(GROUPS[g]))]
        return pltpu.make_async_remote_copy(
            src_ref=held, dst_ref=held, send_sem=gsend_sem.at[g], recv_sem=grecv_sem.at[g],
            device_id=peer(GROUPS[g][0]), device_id_type=MESH,
        )

    def forces_out(g):
        for k in GROUPS[g]:
            force_copy(k).start()

    each_group(forces_out)
    energy_out(2, energy_in(1))
    at_own = scattered[:, 256:320] - scattered[:, 320:384]
    for ph in range(2):
        if sizes[ph] > 1:
            energy_group(ph).wait_send()
    each_group(lambda g: ghost_group(g).wait_send())

    def forces_in(g):
        force_group(g).wait_recv()
        force_group(g).wait_send()

    each_group(forces_in)
    acc = jnp.zeros((8, 128), F32)
    for k in range(8):
        acc = acc + jnp.where(lane_group[0:8] == PLACE[7 - k] % 4, gbuf[PLACE[k]], 0.0)
    acc_low = acc - acc.astype(BF16).astype(F32)
    returned = dot_t(jnp.concatenate([acc, acc_low], axis=0).astype(BF16), st4)
    forces_ref[...] = -(at_own + returned[0:8] + returned[8:16])[0:3]

    total = energy_in(2)
    energy_ref[...] = jnp.sum(total, axis=0, keepdims=True)
    energy_group(2).wait_send()


def solution(mesh):
    columns, rows = mesh.shape["gx"], mesh.shape["gy"]
    sizes = sizes_of(columns, rows)
    most = max(sizes)

    def per_device(positions, features, send_list, edge_src, edge_dst, edge_count, w_embed, w_env, w_update, w_out):
        def body(*refs):
            kernel(columns, rows, sizes, *refs)

        vmem = pl.BlockSpec(memory_space=pltpu.VMEM)
        anywhere = pl.BlockSpec(memory_space=pl.ANY)
        forces, energy = pl.pallas_call(
            body,
            out_shape=(jax.ShapeDtypeStruct((3, ATOMS), F32), jax.ShapeDtypeStruct((1, 128), F32)),
            in_specs=[anywhere] * 10,
            out_specs=(vmem, vmem),
            scratch_shapes=[
                pltpu.VMEM((3, ATOMS), F32),
                pltpu.VMEM((C, ATOMS), BF16),
                pltpu.VMEM((1, GHOST), jnp.int32),
                pltpu.VMEM((8, 128), jnp.int32),
                pltpu.VMEM((8, 128), jnp.int32),
                pltpu.SMEM((1,), jnp.int32),
                pltpu.VMEM((C, 2 * C + NB), F32),
                pltpu.VMEM((LAYERS, C, 3 * C), F32),
                pltpu.VMEM((LAYERS, C, 4 * C), F32),
                pltpu.VMEM((1, C), F32),
                pltpu.VMEM((17, 128), F32),
                pltpu.VMEM((8, 17, 128), F32),
                pltpu.VMEM((768, EDGES), BF16),
                pltpu.VMEM((512, EDGES), BF16),
                pltpu.VMEM((512, EDGES), BF16),
                pltpu.VMEM((256, EDGES), BF16),
                pltpu.VMEM((256, EDGES), BF16),
                pltpu.VMEM((16, EDGES), F32),
                pltpu.VMEM((2, C, EDGES), F32),
                pltpu.VMEM((2, C, EDGES), F32),
                pltpu.VMEM((C, EDGES), F32),
                pltpu.VMEM((NB, EDGES), F32),
                pltpu.VMEM((16, EDGES), BF16),
                pltpu.VMEM((2 * LAYERS, 192, 256), BF16),
                pltpu.VMEM((2 * LAYERS, C, 192), BF16),
                pltpu.VMEM((128, 768), BF16),
                pltpu.VMEM((256, 512), F32),
                pltpu.VMEM((8, TILE), F32),
                pltpu.VMEM((512, 256), BF16),
                pltpu.VMEM((512, 256), BF16),
                pltpu.VMEM((128, 512), BF16),
                pltpu.VMEM((2, 8, 128), F32),
                pltpu.VMEM((8, 8, 128), F32),
                pltpu.VMEM((3, most, 8, 128), F32),
                pltpu.SemaphoreType.DMA((10,)),
                pltpu.SemaphoreType.DMA((3,)),
                pltpu.SemaphoreType.DMA((3,)),
                pltpu.SemaphoreType.DMA((3,)),
                pltpu.SemaphoreType.DMA((3,)),
                pltpu.SemaphoreType.DMA((3,)),
                pltpu.SemaphoreType.DMA((3,)),
            ],
            compiler_params=pltpu.CompilerParams(
                collective_id=0, has_side_effects=True, vmem_limit_bytes=55216 * 1024
            ),
        )(
            positions, features, send_list.reshape(1, GHOST), edge_src.reshape(8, 128), edge_dst.reshape(8, 128),
            edge_count, w_embed.T, w_env, jnp.swapaxes(w_update, 1, 2), w_out.reshape(1, C),
        )
        return forces, jnp.sum(energy)

    placed = (
        P(None, ("gx", "gy")), P(None, ("gx", "gy")), P(("gx", "gy")), P(("gx", "gy")), P(("gx", "gy")),
        P(("gx", "gy")), P(), P(), P(), P(),
    )
    return jax.shard_map(
        per_device, mesh=mesh, in_specs=placed, out_specs=(P(None, ("gx", "gy")), P()), check_vma=False
    )
```
